32 devices in a mesh: dp: 8 (over z, y), mp: 4 (over x, core).
Axes of the slice: x: 2, y: 2, z: 4, core: 2. Of those that a mesh axis runs over, the one named last changes fastest.
Arguments:
- tokens: bfloat16 [10240, 1024], P(('dp', 'mp')), may hold values from -6 to 6
- cond: bfloat16 [8, 1024], P('dp'), may hold values from -3 to 3
- pad_mask: int32 [8, 1280], P('dp'), may hold values from 0 to 1, as said below
- spatial_index: int32 [256, 256], replicated, may hold values from 0 to 960
- joint_index: int32 [320, 320], replicated, may hold values from 0 to 2024
- qkv_a: bfloat16 [1024, 3, 1024], P(None, None, 'mp'), may hold values from -0.1875 to 0.1875
- proj_a: bfloat16 [1024, 1024], P('mp'), may hold values from -0.75 to 0.75
- fc1_a: bfloat16 [1024, 4096], P(None, 'mp'), may hold values from -0.1875 to 0.1875
- fc2_a: bfloat16 [4096, 1024], P('mp'), may hold values from -0.09375 to 0.09375
- table_a: bfloat16 [961, 16], P(None, 'mp'), may hold values from -2.5 to 2.5
- ada_a: bfloat16 [1024, 6144], P(None, 'mp'), may hold values from -0.1875 to 0.1875
- qkv_b: bfloat16 [1024, 3, 1024], P(None, None, 'mp'), may hold values from -0.1875 to 0.1875
- proj_b: bfloat16 [1024, 1024], P('mp'), may hold values from -0.75 to 0.75
- fc1_b: bfloat16 [1024, 4096], P(None, 'mp'), may hold values from -0.1875 to 0.1875
- fc2_b: bfloat16 [4096, 1024], P('mp'), may hold values from -0.09375 to 0.09375
- table_b: bfloat16 [2025, 16], P(None, 'mp'), may hold values from -2.5 to 2.5
- ada_b: bfloat16 [1024, 6144], P(None, 'mp'), may hold values from -0.1875 to 0.1875
- cotangent: bfloat16 [10240, 1024], P(('dp', 'mp')), may hold values from -6 to 6
Outputs:
- output: float32 [10240, 1024], P(('dp', 'mp'))
- token_grad: float32 [10240, 1024], P(('dp', 'mp'))
- grad_qkv_a: float32 [1024, 3, 1024], P('dp', None, 'mp')
- grad_proj_a: float32 [1024, 1024], P('mp', 'dp')
- grad_fc1_a: float32 [1024, 4096], P('dp', 'mp')
- grad_fc2_a: float32 [4096, 1024], P('mp', 'dp')
- grad_table_a: float32 [961, 16], P(None, 'mp')
- grad_ada_a: float32 [1024, 6144], P('dp', 'mp')
- grad_qkv_b: float32 [1024, 3, 1024], P('dp', None, 'mp')
- grad_proj_b: float32 [1024, 1024], P('mp', 'dp')
- grad_fc1_b: float32 [1024, 4096], P('dp', 'mp')
- grad_fc2_b: float32 [4096, 1024], P('mp', 'dp')
- grad_table_b: float32 [2025, 16], P(None, 'mp')
- grad_ada_b: float32 [1024, 6144], P('dp', 'mp')
The draws below stay inside these ranges and needn't reach their ends.
Inputs may be any that keep to these rules, and one draw needn't show every extreme that they name: `pad_mask`: in each tile the positions marked 1 are those whose row is below the tile's own height and whose column is below its own width, both from 9 to 16, the same in all frames; the first tile is always narrower than 16.
All inputs are finite; a program needn't handle non-finite values.
Results may differ from the reference program's by a relative error of at most 0.035.
The reference program's roundings to bfloat16 on the way count: a program that leaves them out, or rounds other values in their place, can miss the bound.
Values may be sent and summed in bfloat16 or wider, within the bound.
A program may use at most 256 MiB of HBM per device.

```python
import jax
import jax.numpy as jnp
from jax import lax

D = 1024
FF = 4096
HEADS = 16
HEAD_DIM = 64
FRAMES = 5
SIDE = 16
TILE_TOK = 1280
WIN_A = 256
WIN_B = 320
NREL_A = 961
NREL_B = 2025
TILES = 8
TOKENS = 10240


def draw_pad_mask(key, part):
    key = jax.random.fold_in(key, 11)
    key_rows, key_cols = jax.random.split(key)
    lowest = SIDE // 2 + 1
    heights = jax.random.randint(key_rows, (TILES,), lowest, SIDE + 1)
    widths = jax.random.randint(key_cols, (TILES,), lowest, SIDE + 1)
    widths = jnp.where(jnp.arange(TILES) == 0, lowest, widths)
    places = jnp.arange(TILE_TOK) % (SIDE * SIDE)
    grid_rows = places // SIDE
    grid_cols = places % SIDE
    inside = (grid_rows[None, :] < heights[:, None]) & (grid_cols[None, :] < widths[:, None])
    return inside.astype(jnp.int32)


def with_ends(entries, stream_key, smallest, high):
    longest = entries.shape.index(max(entries.shape))
    spots = []
    for shift in (0, 1):
        where = [jax.random.randint(jax.random.fold_in(stream_key, axis), (), 0, length) for axis, length in enumerate(entries.shape)]
        where[longest] = (where[longest] + shift) % entries.shape[longest]
        spots.append(tuple(where))
    return entries.at[spots[0]].set(smallest).at[spots[1]].set(high)


def steps_of(rng, extent, cuts, least, high):
    factor_of, own = 1.0, jax.random.fold_in(rng, 6)
    for position, parts in cuts:
        steps = jnp.exp(jax.random.uniform(jax.random.fold_in(own, position), (parts,), jnp.float32, least / len(cuts), high / len(cuts)))
        factor_of = factor_of * jnp.repeat(steps, extent[position] // parts).reshape([-1 if axis == position else 1 for axis in range(len(extent))])
    return factor_of


def noise(stream_key, extent, spread, limit, cuts=(), held_as=jnp.bfloat16):
    loudness = steps_of(stream_key, extent, cuts, -0.22, 0.18) if cuts else 1.0
    result = jax.random.normal(stream_key, extent, jnp.float32) * spread * loudness
    return jnp.minimum(jnp.maximum(result, -limit), limit).astype(held_as)


def setup_inputs(seed: int = 0) -> dict:
    arg_keys = jax.random.split(jax.random.key(seed), 19)
    return {
        "tokens": noise(arg_keys[0], (TOKENS, D), 1.0, 6.0, ((0, 32),)),
        "cond": noise(arg_keys[1], (TILES, D), 1.0, 3.0, ((0, 8),)),
        "pad_mask": draw_pad_mask(jax.random.fold_in(arg_keys[18], 71), 0),
        "spatial_index": with_ends(jax.random.randint(arg_keys[3], (WIN_A, WIN_A), 0, NREL_A), jax.random.fold_in(arg_keys[3], 1), 0, NREL_A - 1).astype(jnp.int32),
        "joint_index": with_ends(jax.random.randint(arg_keys[4], (WIN_B, WIN_B), 0, NREL_B), jax.random.fold_in(arg_keys[4], 1), 0, NREL_B - 1).astype(jnp.int32),
        "qkv_a": noise(arg_keys[5], (D, 3, D), D ** -0.5, 0.1875, ((2, 4),)),
        "proj_a": noise(arg_keys[6], (D, D), (D // 16) ** -0.5, 0.75, ((0, 4),)),
        "fc1_a": noise(arg_keys[7], (D, FF), D ** -0.5, 0.1875, ((1, 4),)),
        "fc2_a": noise(arg_keys[8], (FF, D), FF ** -0.5, 0.09375, ((0, 4),)),
        "table_a": noise(arg_keys[9], (NREL_A, HEADS), 0.5, 2.5, ((1, 4),)),
        "ada_a": noise(arg_keys[10], (D, 6 * D), D ** -0.5, 0.1875, ((1, 4),)),
        "qkv_b": noise(arg_keys[11], (D, 3, D), D ** -0.5, 0.1875, ((2, 4),)),
        "proj_b": noise(arg_keys[12], (D, D), (D // 16) ** -0.5, 0.75, ((0, 4),)),
        "fc1_b": noise(arg_keys[13], (D, FF), D ** -0.5, 0.1875, ((1, 4),)),
        "fc2_b": noise(arg_keys[14], (FF, D), FF ** -0.5, 0.09375, ((0, 4),)),
        "table_b": noise(arg_keys[15], (NREL_B, HEADS), 0.5, 2.5, ((1, 4),)),
        "ada_b": noise(arg_keys[16], (D, 6 * D), D ** -0.5, 0.1875, ((1, 4),)),
        "cotangent": noise(arg_keys[17], (TOKENS, D), 1.0, 6.0, ((0, 32),)),
    }


EPSILON = 1e-06
HIGHEST = lax.Precision.HIGHEST

@jax.custom_vjp
def low(v):
    return lax.optimization_barrier(v.astype(jnp.bfloat16)).astype(jnp.float32)

@jax.custom_vjp
def low_back(v):
    return v

def low_keep(v):
    return (low(v), None)

def low_pass(kept, grad):
    return (grad,)

def back_keep(v):
    return (v, None)

def back_low(kept, grad):
    return (low(grad),)
low.defvjp(low_keep, low_pass)
low_back.defvjp(back_keep, back_low)

def layer_norm(values):
    average = lax.optimization_barrier(jnp.mean(values, axis=-1, keepdims=True))
    centred = values - average
    return centred * lax.rsqrt(lax.optimization_barrier(jnp.mean(centred * centred, axis=-1, keepdims=True)) + EPSILON)

def to_windows(tensor, layout):
    trailing = tensor.shape[1:]
    if layout == 0:
        return tensor.reshape((FRAMES, SIDE * SIDE) + trailing)
    half_side = SIDE // 2
    shaped = tensor.reshape((FRAMES, 2, half_side, 2, half_side) + trailing)
    ordering = (1, 3, 0, 2, 4) + tuple(range(5, 5 + len(trailing)))
    return jnp.transpose(shaped, ordering).reshape((4, FRAMES * half_side * half_side) + trailing)

def from_windows(tensor, layout):
    trailing = tensor.shape[2:]
    if layout == 0:
        return tensor.reshape((TILE_TOK,) + trailing)
    half_side = SIDE // 2
    shaped = tensor.reshape((2, 2, FRAMES, half_side, half_side) + trailing)
    ordering = (2, 0, 3, 1, 4) + tuple(range(5, 5 + len(trailing)))
    return jnp.transpose(shaped, ordering).reshape((TILE_TOK,) + trailing)

def attend(normed, qkv_w, bias_table, rel_index, validity, layout):
    projected = jnp.dot(normed, qkv_w.reshape(D, 3 * D), precision=HIGHEST)
    projected = projected.reshape(TILE_TOK, 3, HEADS, HEAD_DIM)
    queries = to_windows(low(low_back(projected[:, 0])), layout)
    keys_win = to_windows(low(low_back(projected[:, 1])), layout)
    values_win = to_windows(low(low_back(projected[:, 2])), layout)
    biases = jnp.transpose(jnp.take(bias_table, rel_index, axis=0), (2, 0, 1))
    scores = jnp.einsum('wqhe,wkhe->whqk', queries, keys_win, precision=HIGHEST) * HEAD_DIM ** (-0.5)
    scores = low_back(scores) + biases[None]
    visible = to_windows(validity, layout)[:, None, None, :] > 0
    scores = jnp.where(visible, scores, -1e+30)
    row_max = lax.optimization_barrier(jnp.max(scores, axis=-1, keepdims=True))
    weights = jnp.exp(scores - row_max)
    attn_prob = low(weights / lax.optimization_barrier(jnp.sum(weights, axis=-1, keepdims=True)))
    attended = jnp.einsum('whqk,wkhe->wqhe', attn_prob, values_win, precision=HIGHEST)
    return low(low_back(from_windows(attended, layout).reshape(TILE_TOK, D)))

def gelu_tanh(values):
    return jax.nn.gelu(values, approximate=True)

def block(stream, cond_act, validity, params, rel_index, layout):
    qkv_w, proj_w, fc1_w, fc2_w, bias_table, ada_w = params
    modulate = jnp.dot(cond_act[None], ada_w, precision=HIGHEST).reshape(6, D)
    normed_one = layer_norm(stream) * (1.0 + modulate[1]) + modulate[0]
    attended = attend(low(normed_one), qkv_w, bias_table, rel_index, validity, layout)
    attn_out = jnp.dot(attended, proj_w, precision=HIGHEST)
    stream_mid = stream + modulate[2] * low_back(attn_out)
    normed_two = layer_norm(stream_mid) * (1.0 + modulate[4]) + modulate[3]
    hidden = low_back(jnp.dot(low(normed_two), fc1_w, precision=HIGHEST))
    mlp_out = jnp.dot(low(gelu_tanh(hidden)), fc2_w, precision=HIGHEST)
    return stream_mid + modulate[5] * low_back(mlp_out)

def to_float(array):
    return array.astype(jnp.float32)

def reference(tokens, cond, pad_mask, spatial_index, joint_index, qkv_a, proj_a, fc1_a, fc2_a, table_a, ada_a, qkv_b, proj_b, fc1_b, fc2_b, table_b, ada_b, cotangent):
    params_a = tuple((to_float(weight_arr) for weight_arr in (qkv_a, proj_a, fc1_a, fc2_a, table_a, ada_a)))
    params_b = tuple((to_float(weight_arr) for weight_arr in (qkv_b, proj_b, fc1_b, fc2_b, table_b, ada_b)))
    inputs = to_float(tokens).reshape(TILES, TILE_TOK, D)
    cond_rows = to_float(cond)

    def forward(stream_all, first, second):

        def per_tile(pieces):
            stream, cond_row, validity = pieces
            cond_act = low(jax.nn.silu(cond_row))
            middle = block(stream, cond_act, validity, first, spatial_index, 0)
            return block(middle, cond_act, validity, second, joint_index, 1)
        return lax.map(jax.checkpoint(per_tile), (stream_all, cond_rows, pad_mask))
    output, pullback = jax.vjp(forward, inputs, params_a, params_b)
    token_grad, grads_a, grads_b = pullback(to_float(cotangent).reshape(TILES, TILE_TOK, D))
    return (output.reshape(TOKENS, D), token_grad.reshape(TOKENS, D), grads_a[0], grads_a[1], grads_a[2], grads_a[3], grads_a[4], grads_a[5], grads_b[0], grads_b[1], grads_b[2], grads_b[3], grads_b[4], grads_b[5])
```

```python
import functools

import jax
import jax.numpy as jnp
from jax import lax
from jax.experimental import pallas as pl
from jax.experimental.pallas import tpu as pltpu
from jax.sharding import PartitionSpec as P

FRAMES = 5
SIDE = 16
EPSILON = 1e-06
HIGHEST = lax.Precision.HIGHEST
MESH = pl.DeviceIdType.MESH
F32 = jnp.float32
BF16 = jnp.bfloat16
VMEM_LIMIT = 63 << 20
GELU_K = 0.7978845608028654
GELU_C = 0.044715
ANY = pl.BlockSpec(memory_space=pl.ANY)
VM = pl.BlockSpec(memory_space=pltpu.VMEM)


def dma(shape):
    return pltpu.SemaphoreType.DMA(shape)


def places():
    me = lax.axis_index("mp")
    x = lax.div(me, 2)
    core = lax.rem(me, 2)
    return x, core, x * 2 + 1 - core, (1 - x) * 2 + core


def greet(others):
    barrier = pltpu.get_barrier_semaphore()
    for other in others:
        pl.semaphore_signal(barrier, inc=1, device_id={"mp": other}, device_id_type=MESH)
    pl.semaphore_wait(barrier, len(others))


def remote(src, dst, send_sem, recv_sem, other):
    return pltpu.make_async_remote_copy(
        src_ref=src,
        dst_ref=dst,
        send_sem=send_sem,
        recv_sem=recv_sem,
        device_id={"mp": other},
        device_id_type=MESH,
    )


def loop(count, body):
    def step(i, _):
        body(i)
        return 0

    lax.fori_loop(0, count, step, 0)


def rows16(count, body):
    loop(count // 16, lambda i: body(pl.ds(pl.multiple_of(i * 16, 16), 16)))


def cols(count, width, body):
    loop(count // width, lambda j: body(pl.ds(pl.multiple_of(j * width, width), width)))


def norm(values):
    centred = values - jnp.mean(values, axis=-1, keepdims=True)
    inv = lax.rsqrt(jnp.mean(centred * centred, axis=-1, keepdims=True) + EPSILON)
    return centred * inv, inv


def norm_back(normed, inv, grad):
    mean_g = jnp.mean(grad, axis=-1, keepdims=True)
    mean_gn = jnp.mean(grad * normed, axis=-1, keepdims=True)
    return (grad - mean_g - normed * mean_gn) * inv


def dot(a, b):
    return jnp.dot(a, b, preferred_element_type=F32)


def dot_nt(a, b):
    return lax.dot_general(a, b, (((1,), (1,)), ((), ())), preferred_element_type=F32)


def dot_tn(a, b):
    return lax.dot_general(a, b, (((0,), (0,)), ((), ())), preferred_element_type=F32)


def store_a_to_b(dst, frame, value):
    shaped = value.reshape(2, 4, 2, 8, value.shape[-1])
    for qr in range(2):
        for qc in range(2):
            dst[qr * 2 + qc, pl.ds(pl.multiple_of(frame * 4, 4), 4)] = shaped[qr, :, qc]


def store_b_to_a(dst, window, value):
    shaped = value.reshape(FRAMES, 4, 8, value.shape[-1])
    qr, qc = lax.div(window, 2), lax.rem(window, 2)
    for frame in range(FRAMES):
        dst[frame * 2 + qr, :, qc] = shaped[frame]


def store_a_to_a(dst, frame, value):
    shaped = value.reshape(2, 4, 2, 8, value.shape[-1])
    for qr in range(2):
        dst[frame * 2 + qr] = shaped[qr]


def hand_out(groups, out, send_sem, recv_sem, x, core, sibling):
    copies = []
    for i in range(2):
        copies.append(
            remote(
                groups.at[5 * x + 3 - 3 * core + i],
                out.at[1 + 2 * i],
                send_sem.at[i],
                recv_sem.at[i],
                sibling,
            )
        )
        copies[-1].start()
    for i in range(3):
        out[2 * i] = groups[5 * x + 2 * core + i]
    for copy in copies:
        copy.wait()


def forward_kernel(
    windows,
    last,
    stream,
    mod,
    mask,
    bias,
    qkv_hbm,
    proj_hbm,
    fc1_hbm,
    fc2_hbm,
    h1_out,
    qkv_out,
    prob_out,
    att_out,
    ao_out,
    x1_out,
    h2_out,
    act_out,
    dg_out,
    mo_out,
    y_out,
    qkv_w,
    proj_w,
    fc1_w,
    fc2_w,
    h1,
    qkv,
    prob,
    att,
    ao,
    x1,
    h2,
    act,
    dg,
    mo,
    ps1s,
    ps1r,
    xs1s,
    xs1r,
    ps2s,
    ps2r,
    xs2s,
    xs2r,
    part1,
    part2,
    acc,
    groups,
    w_sem,
    out_sem,
    h1_sem,
    h2_sem,
    ps1_sem,
    ps2_sem,
    xs1_sem,
    xs2_sem,
    hand_sem,
):
    width = h1.shape[1]
    half = width // 2
    model = h1.shape[2]
    heads = bias.shape[0]
    inner = proj_w.shape[0]
    head_dim = inner // heads
    x, core, sibling, partner = places()
    own = pl.ds(pl.multiple_of(core * half, 16), half)
    theirs = pl.ds(pl.multiple_of((1 - core) * half, 16), half)

    weights = [
        pltpu.make_async_copy(src, dst, w_sem.at[i])
        for i, (src, dst) in enumerate(
            ((qkv_hbm, qkv_w), (proj_hbm, proj_w), (fc1_hbm, fc1_w), (fc2_hbm, fc2_w))
        )
    ]
    for copy in weights:
        copy.start()
    saves = [
        (h1, h1_out),
        (qkv, qkv_out),
        (prob, prob_out),
        (att, att_out),
        (ao, ao_out),
        (x1, x1_out),
        (h2, h2_out),
        (act, act_out),
        (dg, dg_out),
        (mo, mo_out),
    ]

    def save(which, f):
        src, dst = saves[which]
        return pltpu.make_async_copy(src.at[f], dst.at[f], out_sem.at[which, f])

    def share(buf, sem, f, rows):
        return remote(buf.at[f, own], buf.at[f, rows], sem.at[0, f], sem.at[1, f], sibling)

    def to_sibling(src, dst, sem, f):
        return remote(src.at[f], dst.at[f], sem.at[0, f], sem.at[1, f], sibling)

    def to_partner(src, dst, sem, f):
        return remote(src.at[f], dst.at[f], sem.at[0, f], sem.at[1, f], partner)

    greet((sibling, partner))

    def first_norm(f):
        def some(r):
            normed, _ = norm(stream[f, r].astype(F32))
            h1[f, pl.ds(pl.multiple_of(core * half + r.start, 16), 16)] = (
                normed * (1.0 + mod[1:2]) + mod[0:1]
            ).astype(BF16)

        rows16(half, some)
        share(h1, h1_sem, f, own).start()

    loop(windows, first_norm)
    weights[0].wait()
    weights[1].wait()

    lane_head = lax.div(lax.broadcasted_iota(jnp.int32, (width, inner), 1), head_dim)

    def attention(f):
        share(h1, h1_sem, f, theirs).wait_recv()
        save(0, f).start()
        rows = h1[f]

        def project(c):
            qkv[f, :, c] = dot(rows, qkv_w[:, c]).astype(BF16)

        cols(3 * inner, inner, project)
        save(1, f).start()
        queries = qkv[f, :, :inner] * BF16(head_dim ** (-0.5))
        keys = qkv[f, :, inner : 2 * inner]
        vals = qkv[f, :, 2 * inner :]
        zero = jnp.zeros((), BF16)
        out = jnp.zeros((width, inner), F32)
        for h in range(heads):
            scores = dot_nt(jnp.where(lane_head == h, queries, zero), keys)
            scores = scores + bias[h, :, :width].astype(F32) + mask[f]
            weight = jnp.exp(scores - jnp.max(scores, axis=-1, keepdims=True))
            p = (weight * (1.0 / jnp.sum(weight, axis=-1, keepdims=True))).astype(BF16)
            prob[f, h] = p
            out = out + dot(p, jnp.where(lane_head == h, vals, zero))
        att[f] = out.astype(BF16)
        save(2, f).start()
        save(3, f).start()

        def send_half(c):
            ps1s[f, :, c] = dot(att[f, theirs], proj_w[:, c]).astype(BF16)

        def keep_half(c):
            part1[:, c] = dot(att[f, own], proj_w[:, c])

        cols(model, 512, send_half)
        to_sibling(ps1s, ps1r, ps1_sem, f).start()
        cols(model, 512, keep_half)

    def pair_sum(part, recv, sem, sends, send_to, x_sem, f):
        recv.wait_recv()

        def some(r):
            sends[f, r] = (part[r] + recv_buf(sem)[f, r].astype(F32)).astype(BF16)

        rows16(half, some)
        send_to.start()

    def recv_buf(sem):
        return ps1r if sem is ps1_sem else ps2r

    def sum_first(f):
        pair_sum(
            part1,
            to_sibling(ps1s, ps1r, ps1_sem, f),
            ps1_sem,
            xs1s,
            to_partner(xs1s, xs1r, xs1_sem, f),
            xs1_sem,
            f,
        )

    def sum_second(f):
        pair_sum(
            part2,
            to_sibling(ps2s, ps2r, ps2_sem, f),
            ps2_sem,
            xs2s,
            to_partner(xs2s, xs2r, xs2_sem, f),
            xs2_sem,
            f,
        )

    def middle(f):
        to_partner(xs1s, xs1r, xs1_sem, f).wait_recv()

        def some(r):
            total = xs1s[f, r].astype(F32) + xs1r[f, r].astype(F32)
            mid = stream[f, r].astype(F32) + mod[2:3] * total
            ao[f, r] = total.astype(BF16)
            x1[f, r] = mid
            normed, _ = norm(mid)
            h2[f, pl.ds(pl.multiple_of(core * half + r.start, 16), 16)] = (
                normed * (1.0 + mod[4:5]) + mod[3:4]
            ).astype(BF16)

        rows16(half, some)
        share(h2, h2_sem, f, own).start()
        save(4, f).start()
        save(5, f).start()

    def mlp(f):
        share(h2, h2_sem, f, theirs).wait_recv()
        save(6, f).start()

        def up(c):
            u = dot(h2[f], fc1_w[:, c])
            sq = u * u
            t = jnp.tanh(GELU_K * (u + GELU_C * u * sq))
            one_t = 0.5 * (1.0 + t)
            act[f, :, c] = (u * one_t).astype(BF16)
            slope = one_t + (0.5 * GELU_K) * u * (1.0 - t * t) * (1.0 + (3.0 * GELU_C) * sq)
            dg[f, :, c] = slope.astype(BF16)

        cols(act.shape[2], 256, up)
        save(7, f).start()
        save(8, f).start()

        def send_half(c):
            ps2s[f, :, c] = dot(act[f, theirs], fc2_w[:, c]).astype(BF16)

        def keep_half(c):
            part2[:, c] = dot(act[f, own], fc2_w[:, c])

        cols(model, 256, send_half)
        to_sibling(ps2s, ps2r, ps2_sem, f).start()
        cols(model, 256, keep_half)

    def finish(f):
        to_partner(xs2s, xs2r, xs2_sem, f).wait_recv()

        def some(r):
            total = xs2s[f, r].astype(F32) + xs2r[f, r].astype(F32)
            mo[f, r] = total.astype(BF16)
            acc[r] = x1[f, r] + mod[5:6] * total

        rows16(half, some)
        save(9, f).start()
        if last:
            store_b_to_a(groups, f, acc[...])
        else:
            store_a_to_b(y_out, f, acc[...])

    def step(t):
        @pl.when((t >= 2) & (t < windows + 2))
        def _():
            @pl.when(t == 2)
            def _():
                weights[2].wait()
                weights[3].wait()

            mlp(t - 2)

        @pl.when(t < windows)
        def _():
            attention(t)

        @pl.when((t >= 2) & (t < windows + 2))
        def _():
            sum_second(t - 2)

        @pl.when(t < windows)
        def _():
            sum_first(t)

        @pl.when(t >= 3)
        def _():
            finish(t - 3)

        @pl.when((t >= 1) & (t < windows + 1))
        def _():
            middle(t - 1)

    loop(windows + 3, step)
    if last:
        hand_out(groups, y_out, hand_sem.at[0], hand_sem.at[1], x, core, sibling)

    def drain(f):
        for which in range(len(saves)):
            save(which, f).wait()
        share(h1, h1_sem, f, own).wait_send()
        share(h2, h2_sem, f, own).wait_send()
        to_sibling(ps1s, ps1r, ps1_sem, f).wait_send()
        to_sibling(ps2s, ps2r, ps2_sem, f).wait_send()
        to_partner(xs1s, xs1r, xs1_sem, f).wait_send()
        to_partner(xs2s, xs2r, xs2_sem, f).wait_send()

    loop(windows, drain)


def block_forward(stream, mod, params, bias, mask, last, collective_id):
    qkv_w, proj_w, fc1_w, fc2_w = params
    windows, half, model = stream.shape
    width = 2 * half
    heads = bias.shape[0]
    inner = proj_w.shape[0]
    hidden = fc1_w.shape[1]
    sds = jax.ShapeDtypeStruct
    saved = [
        sds((windows, width, model), BF16),
        sds((windows, width, 3 * inner), BF16),
        sds((windows, heads, width, width), BF16),
        sds((windows, width, inner), BF16),
        sds((windows, half, model), BF16),
        sds((windows, half, model), F32),
        sds((windows, width, model), BF16),
        sds((windows, width, hidden), BF16),
        sds((windows, width, hidden), BF16),
        sds((windows, half, model), BF16),
    ]
    if last:
        y_shape = sds((FRAMES, 4, 2, 8, model), F32)
        groups = (2 * FRAMES, 4, 2, 8, model)
    else:
        y_shape = sds((4, FRAMES * 4, 8, model), F32)
        groups = (1, 1, 1, 8, model)
    own_buf = pltpu.VMEM((windows, half, model), BF16)
    return pl.pallas_call(
        functools.partial(forward_kernel, windows, last),
        out_shape=saved + [y_shape],
        in_specs=[VM] * 4 + [ANY] * 4,
        out_specs=[ANY] * len(saved) + [VM],
        scratch_shapes=[pltpu.VMEM(w.shape, w.dtype) for w in params]
        + [pltpu.VMEM(s.shape, s.dtype) for s in saved]
        + [own_buf] * 8
        + [pltpu.VMEM((half, model), F32)] * 3
        + [
            pltpu.VMEM(groups, F32),
            dma((4,)),
            dma((len(saved), windows)),
        ]
        + [dma((2, windows))] * 6
        + [dma((2, 2))],
        compiler_params=pltpu.CompilerParams(
            collective_id=collective_id, has_side_effects=True, vmem_limit_bytes=VMEM_LIMIT
        ),
        name="forward_last" if last else "forward_first",
    )(stream, mod, mask, bias, qkv_w, proj_w, fc1_w, fc2_w)


def backward_kernel(
    windows,
    last,
    grad_y,
    mod,
    ao,
    mo,
    x1_hbm,
    x_hbm,
    h1_hbm,
    qkv_hbm,
    prob_hbm,
    att_hbm,
    h2_hbm,
    act_hbm,
    dg_hbm,
    qkv_whbm,
    proj_whbm,
    fc1_whbm,
    fc2_whbm,
    gx_out,
    weight_out,
    bias_out,
    mod_out,
    qkv_w,
    proj_w,
    fc1_w,
    fc2_w,
    x1,
    xin,
    h1,
    qkv,
    prob,
    att,
    h2,
    act,
    dg,
    gm,
    ga,
    gh,
    gqkv,
    gatt,
    turned,
    ps1s,
    ps1r,
    xs1s,
    xs1r,
    ps2s,
    ps2r,
    xs2s,
    xs2r,
    part1,
    part2,
    acc,
    groups,
    wgrad,
    wout,
    msum,
    mtot,
    mrecv,
    w_sem,
    in_sem,
    gm_sem,
    ga_sem,
    ps1_sem,
    ps2_sem,
    xs1_sem,
    xs2_sem,
    hand_sem,
    mod_sem,
    wout_sem,
):
    _, half, model = grad_y.shape
    width = 2 * half
    heads = prob.shape[1]
    inner = proj_w.shape[0]
    head_dim = inner // heads
    hidden = fc1_w.shape[1]
    scale = head_dim ** (-0.5)
    x, core, sibling, partner = places()
    own = pl.ds(pl.multiple_of(core * half, 16), half)
    theirs = pl.ds(pl.multiple_of((1 - core) * half, 16), half)

    weights = [
        pltpu.make_async_copy(src, dst, w_sem.at[i])
        for i, (src, dst) in enumerate(
            (
                (fc2_whbm, fc2_w),
                (fc1_whbm, fc1_w),
                (proj_whbm, proj_w),
                (qkv_whbm, qkv_w),
                (x1_hbm, x1),
            )
        )
    ]
    for copy in weights:
        copy.start()

    streams = [
        (act_hbm, act),
        (dg_hbm, dg),
        (h2_hbm, h2),
        (qkv_hbm, qkv),
        (prob_hbm, prob),
        (att_hbm, att),
        (h1_hbm, h1),
        (x_hbm, xin),
    ]

    def fetch(which, f):
        src, dst = streams[which]
        slot = lax.rem(f, 2)
        return pltpu.make_async_copy(src.at[f], dst.at[slot], in_sem.at[which, slot])

    def share(buf, sem, f, rows):
        return remote(buf.at[f, own], buf.at[f, rows], sem.at[0, f], sem.at[1, f], sibling)

    def to_sibling(src, dst, sem, f):
        return remote(src.at[f], dst.at[f], sem.at[0, f], sem.at[1, f], sibling)

    def to_partner(src, dst, sem, f):
        return remote(src.at[f], dst.at[f], sem.at[0, f], sem.at[1, f], partner)

    for which in range(3):
        fetch(which, 0).start()
    greet((sibling, partner))

    def top(f):
        def some(r):
            gm[f, pl.ds(pl.multiple_of(core * half + r.start, 16), 16)] = (
                mod[5:6] * grad_y[f, r]
            ).astype(BF16)

        rows16(half, some)
        share(gm, gm_sem, f, own).start()

    loop(windows, top)
    msum[...] = jnp.zeros_like(msum)
    bias_out[...] = jnp.zeros_like(bias_out)

    def zero_some(r):
        wgrad[r] = jnp.zeros((16, wgrad.shape[1]), F32)

    rows16(model, zero_some)

    lane_head = lax.div(lax.broadcasted_iota(jnp.int32, (width, inner), 1), head_dim)
    zero = jnp.zeros((), BF16)

    def mlp_back(f):
        slot = lax.rem(f, 2)
        for which in range(3):
            fetch(which, f).wait()
        share(gm, gm_sem, f, theirs).wait_recv()

        def up(c):
            back = dot_nt(gm[f], fc2_w[c, :])
            gh[:, c] = (back * dg[slot, :, c].astype(F32)).astype(BF16)

        cols(hidden, 256, up)

        def send_half(c):
            ps1s[f, :, c] = dot_nt(gh[theirs], fc1_w[c, :]).astype(BF16)

        def keep_half(c):
            part1[:, c] = dot_nt(gh[own], fc1_w[c, :])

        cols(model, 256, send_half)
        to_sibling(ps1s, ps1r, ps1_sem, f).start()
        cols(model, 256, keep_half)

    base_fc1 = 4 * inner
    base_fc2 = 4 * inner + hidden

    def add_weight(left, right, base, count):
        turned[...] = left.T

        def some(c):
            where = pl.ds(pl.multiple_of(base + c.start, 256), 256)

            def some_rows(r):
                wgrad[r, where] += dot(turned[r], right[:, c])

            cols(model, 256, some_rows)

        cols(count, 256, some)

    def mlp_weights(f):
        slot = lax.rem(f, 2)
        add_weight(h2[slot], gh, base_fc1, hidden)
        add_weight(gm[f], act.at[slot], base_fc2, hidden)

    def attention_back(f):
        slot = lax.rem(f, 2)
        for which in range(3, 7):
            fetch(which, f).wait()
        share(ga, ga_sem, f, theirs).wait_recv()
        grad_att = dot_nt(ga[f], proj_w[...]).astype(BF16)
        grad_att_t = grad_att.T
        queries_t = qkv[slot, :, :inner].T
        keys = qkv[slot, :, inner : 2 * inner] * BF16(scale)
        vals = qkv[slot, :, 2 * inner :]
        grad_q = jnp.zeros((width, inner), F32)
        grad_k, grad_v = [], []
        for h in range(heads):
            part = slice(h * head_dim, (h + 1) * head_dim)
            p = prob[slot, h]
            grad_p = dot_nt(jnp.where(lane_head == h, grad_att, zero), vals)
            pf = p.astype(F32)
            weighted = pf * grad_p
            grad_s = weighted - pf * jnp.sum(weighted, axis=-1, keepdims=True)
            bias_out[h, :, :width] += grad_s
            rounded = grad_s.astype(BF16)
            grad_q = grad_q + dot(rounded, jnp.where(lane_head == h, keys, zero))
            grad_v.append(dot(grad_att_t[part], p))
            grad_k.append(dot(queries_t[part], rounded) * scale)
        gqkv[:, :inner] = grad_q.astype(BF16)
        gqkv[:, inner : 2 * inner] = jnp.concatenate(grad_k, axis=0).astype(BF16).T
        gqkv[:, 2 * inner :] = jnp.concatenate(grad_v, axis=0).astype(BF16).T

        def send_half(c):
            ps2s[f, :, c] = dot_nt(gqkv[theirs], qkv_w[c, :]).astype(BF16)

        def keep_half(c):
            part2[:, c] = dot_nt(gqkv[own], qkv_w[c, :])

        cols(model, 256, send_half)
        to_sibling(ps2s, ps2r, ps2_sem, f).start()
        cols(model, 256, keep_half)

    def attention_weights(f):
        slot = lax.rem(f, 2)
        add_weight(h1[slot], gqkv, 0, 3 * inner)
        add_weight(ga[f], att.at[slot], 3 * inner, inner)

    def sum_first(f):
        to_sibling(ps1s, ps1r, ps1_sem, f).wait_recv()

        def some(r):
            xs1s[f, r] = (part1[r] + ps1r[f, r].astype(F32)).astype(BF16)

        rows16(half, some)
        to_partner(xs1s, xs1r, xs1_sem, f).start()

    def sum_second(f):
        to_sibling(ps2s, ps2r, ps2_sem, f).wait_recv()

        def some(r):
            xs2s[f, r] = (part2[r] + ps2r[f, r].astype(F32)).astype(BF16)

        rows16(half, some)
        to_partner(xs2s, xs2r, xs2_sem, f).start()

    def fold(values):
        return values.reshape(2, 8, model).sum(axis=0)

    def middle(f):
        to_partner(xs1s, xs1r, xs1_sem, f).wait_recv()

        def some(r):
            grad_h = xs1s[f, r].astype(F32) + xs1r[f, r].astype(F32)
            normed, inv = norm(x1[f, r])
            gy = grad_y[f, r]
            grad_mid = gy + norm_back(normed, inv, grad_h * (1.0 + mod[4:5]))
            msum[2] += fold(grad_mid * ao[f, r].astype(F32))
            msum[3] += fold(grad_h)
            msum[4] += fold(grad_h * normed)
            msum[5] += fold(gy * mo[f, r].astype(F32))
            x1[f, r] = grad_mid
            ga[f, pl.ds(pl.multiple_of(core * half + r.start, 16), 16)] = (
                mod[2:3] * grad_mid
            ).astype(BF16)

        rows16(half, some)
        share(ga, ga_sem, f, own).start()

    def finish(f):
        slot = lax.rem(f, 2)
        fetch(7, f).wait()
        to_partner(xs2s, xs2r, xs2_sem, f).wait_recv()

        def some(r):
            grad_h = xs2s[f, r].astype(F32) + xs2r[f, r].astype(F32)
            normed, inv = norm(xin[slot, r].astype(F32))
            msum[0] += fold(grad_h)
            msum[1] += fold(grad_h * normed)
            acc[r] = x1[f, r] + norm_back(normed, inv, grad_h * (1.0 + mod[1:2]))

        rows16(half, some)
        if last:
            store_b_to_a(gx_out, f, acc[...])
        else:
            store_a_to_a(groups, f, acc[...])

    def step(t):
        @pl.when(t + 1 < windows)
        def _():
            for which in range(3):
                fetch(which, t + 1).start()

        @pl.when((t >= 1) & (t < windows + 1))
        def _():
            for which in range(3, 7):
                fetch(which, t - 1).start()

        @pl.when((t >= 2) & (t < windows + 2))
        def _():
            fetch(7, t - 2).start()

        @pl.when((t >= 2) & (t < windows + 2))
        def _():
            @pl.when(t == 2)
            def _():
                weights[2].wait()
                weights[3].wait()

            attention_back(t - 2)

        @pl.when(t < windows)
        def _():
            @pl.when(t == 0)
            def _():
                weights[0].wait()
                weights[1].wait()

            mlp_back(t)

        @pl.when((t >= 2) & (t < windows + 2))
        def _():
            sum_second(t - 2)

        @pl.when(t < windows)
        def _():
            sum_first(t)

        @pl.when((t >= 2) & (t < windows + 2))
        def _():
            attention_weights(t - 2)

        @pl.when(t < windows)
        def _():
            mlp_weights(t)

        @pl.when(t >= 3)
        def _():
            finish(t - 3)

        @pl.when((t >= 1) & (t < windows + 1))
        def _():
            @pl.when(t == 1)
            def _():
                weights[4].wait()

            middle(t - 1)

    loop(windows + 3, step)

    for i in range(6):
        mtot[i : i + 1] = jnp.sum(msum[i], axis=0, keepdims=True)
    mod_copy = remote(mtot, mrecv, mod_sem.at[0], mod_sem.at[1], sibling)
    mod_copy.start()

    def round_some(i):
        slot = lax.rem(i, 2)
        r = pl.ds(pl.multiple_of(i * 128, 128), 128)
        out = pltpu.make_async_copy(wout.at[slot], weight_out.at[r], wout_sem.at[slot])

        @pl.when(i >= 2)
        def _():
            out.wait()

        wout[slot] = wgrad[r].astype(BF16)
        out.start()

    loop(model // 128, round_some)
    for i in range(model // 128 - 2, model // 128):
        pltpu.make_async_copy(
            wout.at[i % 2], weight_out.at[pl.ds(i * 128, 128)], wout_sem.at[i % 2]
        ).wait()
    mod_copy.wait()
    mod_out[...] = mtot[...] + mrecv[...]
    if not last:
        hand_out(groups, gx_out, hand_sem.at[0], hand_sem.at[1], x, core, sibling)

    def drain(f):
        share(gm, gm_sem, f, own).wait_send()
        share(ga, ga_sem, f, own).wait_send()
        to_sibling(ps1s, ps1r, ps1_sem, f).wait_send()
        to_sibling(ps2s, ps2r, ps2_sem, f).wait_send()
        to_partner(xs1s, xs1r, xs1_sem, f).wait_send()
        to_partner(xs2s, xs2r, xs2_sem, f).wait_send()

    loop(windows, drain)


def block_backward(stream, grad_y, mod, params, kept, padded, last, collective_id):
    qkv_w, proj_w, fc1_w, fc2_w = params
    h1, qkv, prob, att, ao, x1, h2, act, dg, mo = kept
    windows, half, model = stream.shape
    width = 2 * half
    heads = prob.shape[1]
    inner = proj_w.shape[0]
    hidden = fc1_w.shape[1]
    total = 4 * inner + 2 * hidden
    sds = jax.ShapeDtypeStruct
    if last:
        gx_shape = sds((2 * FRAMES, 4, 2, 8, model), F32)
        groups = (1, 1, 1, 8, model)
    else:
        gx_shape = sds((FRAMES, 4, 2, 8, model), F32)
        groups = (2 * FRAMES, 4, 2, 8, model)
    own_buf = pltpu.VMEM((windows, half, model), BF16)
    all_buf = pltpu.VMEM((windows, width, model), BF16)

    def two(array):
        return pltpu.VMEM((2,) + array.shape[1:], array.dtype)

    return pl.pallas_call(
        functools.partial(backward_kernel, windows, last),
        out_shape=[
            gx_shape,
            sds((model, total), BF16),
            sds((heads, width, padded), F32),
            sds((6, model), F32),
        ],
        in_specs=[VM] * 4 + [ANY] * 13,
        out_specs=[VM, ANY, VM, VM],
        scratch_shapes=[pltpu.VMEM(w.shape, w.dtype) for w in params]
        + [pltpu.VMEM(x1.shape, F32)]
        + [two(a) for a in (stream, h1, qkv, prob, att, h2, act, dg)]
        + [
            all_buf,
            all_buf,
            pltpu.VMEM((width, hidden), BF16),
            pltpu.VMEM((width, 3 * inner), BF16),
            pltpu.VMEM((16, 128), BF16),
            pltpu.VMEM((model, width), BF16),
        ]
        + [own_buf] * 8
        + [pltpu.VMEM((half, model), F32)] * 3
        + [
            pltpu.VMEM(groups, F32),
            pltpu.VMEM((model, total), F32),
            pltpu.VMEM((2, 128, total), BF16),
            pltpu.VMEM((6, 8, model), F32),
            pltpu.VMEM((6, model), F32),
            pltpu.VMEM((6, model), F32),
            dma((5,)),
            dma((8, 2)),
        ]
        + [dma((2, windows))] * 6
        + [dma((2, 2)), dma((2,)), dma((2,))],
        compiler_params=pltpu.CompilerParams(
            collective_id=collective_id, has_side_effects=True, vmem_limit_bytes=VMEM_LIMIT
        ),
        name="backward_last" if last else "backward_first",
    )(
        grad_y,
        mod,
        ao,
        mo,
        x1,
        stream,
        h1,
        qkv,
        prob,
        att,
        h2,
        act,
        dg,
        qkv_w,
        proj_w,
        fc1_w,
        fc2_w,
    )


def lookup_kernel(index, table, out):
    heads, groups = table.shape[0], table.shape[1]
    rows, width = index.shape

    def some(r):
        for block in range(width // 128):
            c = pl.ds(block * 128, 128)
            row = index[r, c]
            low = row & 127
            high = row >> 7
            found = [jnp.zeros((16, 128), F32) for _ in range(heads)]
            for g in range(groups):
                here = high == g
                for h in range(heads):
                    spread = jnp.broadcast_to(table[h, pl.ds(g, 1), :], (16, 128))
                    taken = jnp.take_along_axis(spread, low, axis=1, mode="promise_in_bounds")
                    found[h] = jnp.where(here, taken, found[h])
            for h in range(heads):
                out[h, r, c] = found[h].astype(BF16)

    rows16(rows, some)


def bias_lookup(index, table):
    rows, heads = table.shape
    groups = (rows + 127) // 128
    spread = jnp.pad(table.astype(F32), ((0, groups * 128 - rows), (0, 0))).T
    return pl.pallas_call(
        lookup_kernel,
        out_shape=jax.ShapeDtypeStruct((heads,) + index.shape, BF16),
        name="bias_lookup",
    )(index, spread.reshape(heads, groups, 128))


def scatter_kernel(index, grad, out):
    heads = grad.shape[0]
    groups = out.shape[1] // heads
    rows, width = index.shape
    out[...] = jnp.zeros_like(out)
    low_rows = lax.broadcasted_iota(jnp.int32, (128, width), 0)
    high_rows = lax.broadcasted_iota(jnp.int32, (groups, width), 0)

    def some(rb):
        r = pl.ds(pl.multiple_of(rb * 8, 8), 8)
        index_rows = index[r, :]
        low = index_rows & 127
        high = index_rows >> 7
        grads = [grad[h, r, :] for h in range(heads)]
        total = out[...]
        for i in range(8):
            onehot = jnp.where(low_rows == low[i : i + 1], 1.0, 0.0).astype(BF16)
            here = high_rows == high[i : i + 1]
            placed = jnp.concatenate(
                [jnp.where(here, g[i : i + 1], 0.0) for g in grads], axis=0
            ).astype(BF16)
            total = total + dot_nt(onehot, placed)
        out[...] = total

    loop(rows // 8, some)


def table_scatter(index, grad, table_len):
    heads = grad.shape[0]
    groups = (table_len + 127) // 128
    out = pl.pallas_call(
        scatter_kernel,
        out_shape=jax.ShapeDtypeStruct((128, heads * groups), F32),
        name="table_scatter",
    )(index, grad)
    return out.reshape(128, heads, groups)


def reduce_kernel(bits, parts, given, out, *scratch):
    bufs, own, sends, recvs, loads = scratch[:bits], *scratch[bits:]
    me = lax.axis_index("dp")
    mine = [lax.rem(lax.div(me, 1 << b), 2) for b in range(bits)]
    others = [me + (1 - 2 * mine[b]) * (1 << b) for b in range(bits)]
    rows, columns = own.shape[1], own.shape[2]
    share = columns // parts
    fetches = []
    for part in range(parts):
        c = pl.ds(part * share, share)
        fetches.append(pltpu.make_async_copy(given.at[:, :, c], own.at[:, :, c], loads.at[part]))
        fetches[-1].start()
    barrier = pltpu.get_barrier_semaphore()
    for other in others:
        pl.semaphore_signal(barrier, inc=1, device_id={"dp": other}, device_id_type=MESH)
    pl.semaphore_wait(barrier, bits)

    def slice_of(b, j, low):
        index = j * (1 << (b + 1)) + low * (1 << b)
        for lower in range(b):
            index = index + mine[lower] * (1 << lower)
        return index

    def copy(b, j, part):
        c = pl.ds(part * share, share)
        src = own.at[slice_of(b, j, 1 - mine[b]), :, c]
        sem = (b, part, j)
        return pltpu.make_async_remote_copy(
            src_ref=src,
            dst_ref=bufs[b].at[j, :, c],
            send_sem=sends.at[sem],
            recv_sem=recvs.at[sem],
            device_id={"dp": others[b]},
            device_id_type=MESH,
        )

    def add(b, j, part):
        copy(b, j, part).wait_recv()
        c = pl.ds(part * share, share)
        where = slice_of(b, j, mine[b])

        def some(r):
            total = own[where, r, c].astype(F32) + bufs[b][j, r, c].astype(F32)
            if b == bits - 1:
                out[r, c] = total
            else:
                own[where, r, c] = total.astype(BF16)

        rows16(rows, some)

    def first(b, j):
        return 2 * j + (1 - mine[b + 1])

    def second(b, j):
        return 2 * j + mine[b + 1]

    for part in range(parts):
        fetches[part].wait()
        for j in range(1 << (bits - 1)):
            copy(0, j, part).start()
    for part in range(parts):
        for b in range(bits):
            count = 1 << (bits - 1 - b)
            if b == bits - 1:
                add(b, 0, part)
                continue
            for j in range(count // 2):
                add(b, first(b, j), part)
                copy(b + 1, j, part).start()
            for j in range(count // 2):
                add(b, second(b, j), part)
    for part in range(parts):
        for b in range(bits):
            for j in range(1 << (bits - 1 - b)):
                copy(b, j, part).wait_send()


def reduce_weights(grads, size, collective_id):
    rows, columns = grads.shape
    bits = size.bit_length() - 1
    parts = 6
    shaped = grads.reshape(size, rows // size, columns)
    return pl.pallas_call(
        functools.partial(reduce_kernel, bits, parts),
        out_shape=jax.ShapeDtypeStruct((rows // size, columns), F32),
        in_specs=[ANY],
        out_specs=VM,
        scratch_shapes=[
            pltpu.VMEM((1 << (bits - 1 - b), rows // size, columns), BF16) for b in range(bits)
        ]
        + [pltpu.VMEM(shaped.shape, BF16)]
        + [dma((bits, parts, size // 2)), dma((bits, parts, size // 2)), dma((parts,))],
        compiler_params=pltpu.CompilerParams(
            collective_id=collective_id, has_side_effects=True, vmem_limit_bytes=VMEM_LIMIT
        ),
        name="reduce_weights",
    )(shaped)


def place_index(index, layout):
    if layout == 0:
        cut, order, pad = (2, 2, 64), (1, 0, 2), 0
    else:
        cut, order, pad = (FRAMES, 2, 32), (1, 0, 2), 64
    side = index.shape[0]
    both = index.reshape(cut + cut)
    both = both.transpose(order + tuple(3 + o for o in order)).reshape(side, side)
    return jnp.pad(both, ((0, 0), (0, pad)), constant_values=-1)


def local(
    tokens,
    cond,
    pad_mask,
    spatial_index,
    joint_index,
    qkv_a,
    proj_a,
    fc1_a,
    fc2_a,
    table_a,
    ada_a,
    qkv_b,
    proj_b,
    fc1_b,
    fc2_b,
    table_b,
    ada_b,
    cotangent,
    dp_size,
    mp_size,
):
    model = tokens.shape[1]
    inner = proj_a.shape[0]
    hidden = fc1_a.shape[1]
    core = lax.rem(lax.axis_index("mp"), 2)
    params_a = (qkv_a.reshape(model, -1), proj_a, fc1_a, fc2_a)
    params_b = (qkv_b.reshape(model, -1), proj_b, fc1_b, fc2_b)

    def own_rows(values):
        whole = lax.all_gather(values, "mp", axis=0, tiled=True)
        cut = whole.reshape(2 * FRAMES, 2, 4 * SIDE, model)
        return lax.dynamic_index_in_dim(cut, core, axis=1, keepdims=False)

    cond_act = jax.nn.silu(cond.astype(F32)).astype(BF16)
    parts = jnp.concatenate(
        [jnp.dot(cond_act, ada, preferred_element_type=F32) for ada in (ada_a, ada_b)], axis=0
    )
    mods = lax.all_gather(parts, "mp", axis=1, tiled=True).reshape(2, 6, model)

    x_a = own_rows(tokens).reshape(FRAMES, -1, model)
    grad_top = own_rows(cotangent).astype(F32).reshape(FRAMES, 2, 4, 2, 8, model)
    grad_top = grad_top.transpose(1, 3, 0, 2, 4, 5).reshape(4, -1, model)

    index_a = place_index(spatial_index, 0)
    index_b = place_index(joint_index, 1)
    bias_a = bias_lookup(index_a, table_a)
    bias_b = bias_lookup(index_b, table_b)
    hidden_keys = jnp.where(pad_mask.reshape(-1) > 0, 0.0, -1e30).astype(F32)
    mask_a = hidden_keys.reshape(FRAMES, 2, 2, 64).transpose(0, 2, 1, 3).reshape(FRAMES, 1, -1)
    mask_b = hidden_keys.reshape(FRAMES, 2, 2, 4, 2, 8).transpose(1, 4, 2, 0, 3, 5)
    mask_b = mask_b.reshape(4, 1, -1)

    *kept_a, y_a = block_forward(x_a, mods[0], params_a, bias_a, mask_a, False, 1)
    x_b = y_a.reshape(4, -1, model)
    *kept_b, output = block_forward(x_b, mods[1], params_b, bias_b, mask_b, True, 2)
    grad_mid, weights_b, grad_bias_b, mod_b = block_backward(
        x_b, grad_top, mods[1], params_b, kept_b, index_b.shape[1], True, 3
    )
    grad_x, weights_a, grad_bias_a, mod_a = block_backward(
        x_a,
        grad_mid.reshape(FRAMES, -1, model),
        mods[0],
        params_a,
        kept_a,
        index_a.shape[1],
        False,
        4,
    )
    table_grad_a = table_scatter(index_a, grad_bias_a, table_a.shape[0])
    table_grad_b = table_scatter(index_b, grad_bias_b, table_b.shape[0])

    summed = reduce_weights(jnp.concatenate([weights_a, weights_b], axis=1), dp_size, 5)

    wide = ada_a.shape[1]
    first = lax.axis_index("mp") * wide
    mod_columns = [
        lax.dynamic_slice_in_dim(m.reshape(-1), first, wide, axis=0) for m in (mod_a, mod_b)
    ]
    small = jnp.concatenate(
        [cond_act.astype(F32).reshape(-1)]
        + mod_columns
        + [table_grad_a.reshape(-1), table_grad_b.reshape(-1)]
    )
    everyone = lax.all_gather(small, "dp", axis=0, tiled=False)
    cut = [model, model + wide, model + 2 * wide, model + 2 * wide + table_grad_a.size]
    conds, cols_a, cols_b, tables_a, tables_b = jnp.split(everyone, cut, axis=1)
    rows_here = model // dp_size
    my_conds = lax.dynamic_slice_in_dim(conds, lax.axis_index("dp") * rows_here, rows_here, axis=1)

    def outer(columns):
        return jnp.einsum("td,tc->dc", my_conds, columns, precision=HIGHEST)

    def table(parts, like, length):
        summed_table = jnp.sum(parts, axis=0).reshape(like.shape)
        return summed_table.transpose(2, 0, 1).reshape(-1, like.shape[1])[:length]

    def split(piece):
        grad_qkv = piece[:, : 3 * inner].reshape(rows_here, 3, inner)
        grad_proj = piece[:, 3 * inner : 4 * inner].T
        grad_fc1 = piece[:, 4 * inner : 4 * inner + hidden]
        grad_fc2 = piece[:, 4 * inner + hidden :].T
        return grad_qkv, grad_proj, grad_fc1, grad_fc2

    total = 4 * inner + 2 * hidden
    return (
        output.reshape(tokens.shape),
        grad_x.reshape(tokens.shape),
        *split(summed[:, :total]),
        table(tables_a, table_grad_a, table_a.shape[0]),
        outer(cols_a),
        *split(summed[:, total:]),
        table(tables_b, table_grad_b, table_b.shape[0]),
        outer(cols_b),
    )


def solution(mesh):
    in_specs = (
        P(("dp", "mp"), None),
        P("dp", None),
        P("dp", None),
        P(),
        P(),
        P(None, None, "mp"),
        P("mp", None),
        P(None, "mp"),
        P("mp", None),
        P(None, "mp"),
        P(None, "mp"),
        P(None, None, "mp"),
        P("mp", None),
        P(None, "mp"),
        P("mp", None),
        P(None, "mp"),
        P(None, "mp"),
        P(("dp", "mp"), None),
    )
    out_specs = (
        P(("dp", "mp"), None),
        P(("dp", "mp"), None),
        P("dp", None, "mp"),
        P("mp", "dp"),
        P("dp", "mp"),
        P("mp", "dp"),
        P(None, "mp"),
        P("dp", "mp"),
        P("dp", None, "mp"),
        P("mp", "dp"),
        P("dp", "mp"),
        P("mp", "dp"),
        P(None, "mp"),
        P("dp", "mp"),
    )
    body = functools.partial(local, dp_size=mesh.shape["dp"], mp_size=mesh.shape["mp"])
    return jax.shard_map(body, mesh=mesh, in_specs=in_specs, out_specs=out_specs, check_vma=False)
```

```python
import functools

import jax
import jax.numpy as jnp
from jax import lax
from jax.experimental import pallas as pl
from jax.experimental.pallas import tpu as pltpu
from jax.sharding import PartitionSpec as P

FRAMES = 5
SIDE = 16
EPSILON = 1e-06
HIGHEST = lax.Precision.HIGHEST
MESH = pl.DeviceIdType.MESH
F32 = jnp.float32
BF16 = jnp.bfloat16
VMEM_LIMIT = 60 << 20
GELU_K = 0.7978845608028654
GELU_C = 0.044715
ANY = pl.BlockSpec(memory_space=pl.ANY)
VM = pl.BlockSpec(memory_space=pltpu.VMEM)


def dma(shape):
    return pltpu.SemaphoreType.DMA(shape)


def places():
    me = lax.axis_index("mp")
    x = lax.div(me, 2)
    core = lax.rem(me, 2)
    return x, core, x * 2 + 1 - core, (1 - x) * 2 + core


def greet(others):
    barrier = pltpu.get_barrier_semaphore()
    for other in others:
        pl.semaphore_signal(barrier, inc=1, device_id={"mp": other}, device_id_type=MESH)
    pl.semaphore_wait(barrier, len(others))


def remote(src, dst, send_sem, recv_sem, other):
    return pltpu.make_async_remote_copy(
        src_ref=src,
        dst_ref=dst,
        send_sem=send_sem,
        recv_sem=recv_sem,
        device_id={"mp": other},
        device_id_type=MESH,
    )


def loop(count, body):
    def step(i, _):
        body(i)
        return 0

    lax.fori_loop(0, count, step, 0)


def rows16(count, body, step=16):
    loop(count // step, lambda i: body(pl.ds(pl.multiple_of(i * step, step), step)))


def norm(values):
    centred = values - jnp.mean(values, axis=-1, keepdims=True)
    inv = lax.rsqrt(jnp.mean(centred * centred, axis=-1, keepdims=True) + EPSILON)
    return centred * inv, inv


def norm_back(normed, inv, grad):
    mean_g = jnp.mean(grad, axis=-1, keepdims=True)
    mean_gn = jnp.mean(grad * normed, axis=-1, keepdims=True)
    return (grad - mean_g - normed * mean_gn) * inv


def dot(a, b):
    return jnp.dot(a, b, preferred_element_type=F32)


def dot_nt(a, b):
    return lax.dot_general(a, b, (((1,), (1,)), ((), ())), preferred_element_type=F32)


def dot_tn(a, b):
    return lax.dot_general(a, b, (((0,), (0,)), ((), ())), preferred_element_type=F32)


def store_a_to_b(dst, frame, value):
    shaped = value.reshape(2, 4, 2, 8, value.shape[-1])
    for qr in range(2):
        for qc in range(2):
            dst[qr * 2 + qc, pl.ds(pl.multiple_of(frame * 4, 4), 4)] = shaped[qr, :, qc]


def store_b_to_a(dst, window, value):
    shaped = value.reshape(FRAMES, 4, 8, value.shape[-1])
    qr, qc = lax.div(window, 2), lax.rem(window, 2)
    for frame in range(FRAMES):
        dst[frame * 2 + qr, :, qc] = shaped[frame]


def store_a_to_a(dst, frame, value):
    shaped = value.reshape(2, 4, 2, 8, value.shape[-1])
    for qr in range(2):
        dst[frame * 2 + qr] = shaped[qr]


def hand_out(groups, out, send_sem, recv_sem, x, core, sibling):
    copies = []
    for i in range(2):
        copies.append(
            remote(
                groups.at[5 * x + 3 - 3 * core + i],
                out.at[1 + 2 * i],
                send_sem.at[i],
                recv_sem.at[i],
                sibling,
            )
        )
        copies[-1].start()
    for i in range(3):
        out[2 * i] = groups[5 * x + 2 * core + i]
    for copy in copies:
        copy.wait()


def forward_kernel(
    windows,
    last,
    stream,
    mod,
    mask,
    bias,
    qkv_hbm,
    proj_hbm,
    fc1_hbm,
    fc2_hbm,
    h1_out,
    qkv_out,
    prob_out,
    att_out,
    ao_out,
    x1_out,
    h2_out,
    act_out,
    dg_out,
    mo_out,
    y_out,
    qkv_w,
    proj_w,
    fc1_w,
    fc2_w,
    h1,
    qkv,
    prob,
    att,
    ao,
    x1,
    h2,
    act,
    dg,
    mo,
    ps1s,
    ps1r,
    xs1s,
    xs1r,
    ps2s,
    ps2r,
    xs2s,
    xs2r,
    part1,
    part2,
    groups,
    w_sem,
    out_sem,
    h1_sem,
    h2_sem,
    ps1_sem,
    ps2_sem,
    xs1_sem,
    xs2_sem,
    hand_sem,
):
    width = h1.shape[1]
    half = width // 2
    model = h1.shape[2]
    heads = bias.shape[0]
    inner = proj_w.shape[0]
    head_dim = inner // heads
    x, core, sibling, partner = places()
    own = pl.ds(pl.multiple_of(core * half, 16), half)
    theirs = pl.ds(pl.multiple_of((1 - core) * half, 16), half)

    weights = [
        pltpu.make_async_copy(src, dst, w_sem.at[i])
        for i, (src, dst) in enumerate(
            ((qkv_hbm, qkv_w), (proj_hbm, proj_w), (fc1_hbm, fc1_w), (fc2_hbm, fc2_w))
        )
    ]
    for copy in weights:
        copy.start()
    saves = [
        (h1, h1_out),
        (qkv, qkv_out),
        (prob, prob_out),
        (att, att_out),
        (ao, ao_out),
        (x1, x1_out),
        (h2, h2_out),
        (act, act_out),
        (dg, dg_out),
        (mo, mo_out),
    ]

    def save(which, f):
        src, dst = saves[which]
        return pltpu.make_async_copy(src.at[f], dst.at[f], out_sem.at[which, f])

    def share(buf, sem, f, rows):
        return remote(buf.at[f, own], buf.at[f, rows], sem.at[0, f], sem.at[1, f], sibling)

    def to_sibling(src, dst, sem, f):
        return remote(src.at[f], dst.at[f], sem.at[0, f], sem.at[1, f], sibling)

    def to_partner(src, dst, sem, f):
        return remote(src.at[f], dst.at[f], sem.at[0, f], sem.at[1, f], partner)

    greet((sibling, partner))

    def first_norm(f):
        normed, _ = norm(stream[f].astype(F32))
        h1[f, own] = (normed * (1.0 + mod[1:2]) + mod[0:1]).astype(BF16)
        share(h1, h1_sem, f, own).start()

    loop(windows, first_norm)
    weights[0].wait()
    weights[1].wait()

    lane_head = lax.div(lax.broadcasted_iota(jnp.int32, (width, inner), 1), head_dim)

    def attention(f):
        share(h1, h1_sem, f, theirs).wait_recv()
        save(0, f).start()
        qkv[f] = dot(h1[f], qkv_w[...]).astype(BF16)
        save(1, f).start()
        queries = qkv[f, :, :inner] * BF16(head_dim ** (-0.5))
        keys = qkv[f, :, inner : 2 * inner]
        vals = qkv[f, :, 2 * inner :]
        zero = jnp.zeros((), BF16)
        out = jnp.zeros((width, inner), F32)
        for h in range(heads):
            scores = dot_nt(jnp.where(lane_head == h, queries, zero), keys)
            scores = scores + bias[h, :, :width].astype(F32) + mask[f]
            weight = jnp.exp(scores - jnp.max(scores, axis=-1, keepdims=True))
            p = (weight * (1.0 / jnp.sum(weight, axis=-1, keepdims=True))).astype(BF16)
            prob[f, h] = p
            out = out + dot(p, jnp.where(lane_head == h, vals, zero))
        att[f] = out.astype(BF16)
        save(2, f).start()
        save(3, f).start()

        ps1s[f] = dot(att[f, theirs], proj_w[...]).astype(BF16)
        to_sibling(ps1s, ps1r, ps1_sem, f).start()
        part1[...] = dot(att[f, own], proj_w[...])

    def sum_first(f):
        to_sibling(ps1s, ps1r, ps1_sem, f).wait_recv()
        xs1s[f] = (part1[...] + ps1r[f].astype(F32)).astype(BF16)
        to_partner(xs1s, xs1r, xs1_sem, f).start()

    def sum_second(f):
        to_sibling(ps2s, ps2r, ps2_sem, f).wait_recv()
        xs2s[f] = (part2[...] + ps2r[f].astype(F32)).astype(BF16)
        to_partner(xs2s, xs2r, xs2_sem, f).start()

    def middle(f):
        to_partner(xs1s, xs1r, xs1_sem, f).wait_recv()

        total = xs1s[f].astype(F32) + xs1r[f].astype(F32)
        mid = stream[f].astype(F32) + mod[2:3] * total
        ao[f] = total.astype(BF16)
        x1[f] = mid
        normed, _ = norm(mid)
        h2[f, own] = (normed * (1.0 + mod[4:5]) + mod[3:4]).astype(BF16)
        share(h2, h2_sem, f, own).start()
        save(4, f).start()
        save(5, f).start()

    def mlp(f):
        share(h2, h2_sem, f, theirs).wait_recv()
        save(6, f).start()

        for start in range(0, act.shape[2], 256):
            c = pl.ds(start, 256)
            u = dot(h2[f], fc1_w[:, c])
            sq = u * u
            t = jnp.tanh(GELU_K * (u + GELU_C * u * sq))
            one_t = 0.5 * (1.0 + t)
            act[f, :, c] = (u * one_t).astype(BF16)
            slope = one_t + (0.5 * GELU_K) * u * (1.0 - t * t) * (1.0 + (3.0 * GELU_C) * sq)
            dg[f, :, c] = slope.astype(BF16)
        save(7, f).start()
        save(8, f).start()
        ps2s[f] = dot(act[f, theirs], fc2_w[...]).astype(BF16)
        to_sibling(ps2s, ps2r, ps2_sem, f).start()
        part2[...] = dot(act[f, own], fc2_w[...])

    def finish(f):
        to_partner(xs2s, xs2r, xs2_sem, f).wait_recv()

        total = xs2s[f].astype(F32) + xs2r[f].astype(F32)
        mo[f] = total.astype(BF16)
        save(9, f).start()
        result = x1[f] + mod[5:6] * total
        if last:
            store_b_to_a(groups, f, result)
        else:
            store_a_to_b(y_out, f, result)

    def step(t):
        @pl.when((t >= 2) & (t < windows + 2))
        def _():
            @pl.when(t == 2)
            def _():
                weights[2].wait()
                weights[3].wait()

            mlp(t - 2)

        @pl.when(t < windows)
        def _():
            attention(t)

        @pl.when((t >= 2) & (t < windows + 2))
        def _():
            sum_second(t - 2)

        @pl.when(t < windows)
        def _():
            sum_first(t)

        @pl.when(t >= 3)
        def _():
            finish(t - 3)

        @pl.when((t >= 1) & (t < windows + 1))
        def _():
            middle(t - 1)

    loop(windows + 3, step)
    if last:
        hand_out(groups, y_out, hand_sem.at[0], hand_sem.at[1], x, core, sibling)

    def drain(f):
        for which in range(len(saves)):
            save(which, f).wait()
        share(h1, h1_sem, f, own).wait_send()
        share(h2, h2_sem, f, own).wait_send()
        to_sibling(ps1s, ps1r, ps1_sem, f).wait_send()
        to_sibling(ps2s, ps2r, ps2_sem, f).wait_send()
        to_partner(xs1s, xs1r, xs1_sem, f).wait_send()
        to_partner(xs2s, xs2r, xs2_sem, f).wait_send()

    loop(windows, drain)


def block_forward(stream, mod, params, bias, mask, last, collective_id):
    qkv_w, proj_w, fc1_w, fc2_w = params
    windows, half, model = stream.shape
    width = 2 * half
    heads = bias.shape[0]
    inner = proj_w.shape[0]
    hidden = fc1_w.shape[1]
    sds = jax.ShapeDtypeStruct
    saved = [
        sds((windows, width, model), BF16),
        sds((windows, width, 3 * inner), BF16),
        sds((windows, heads, width, width), BF16),
        sds((windows, width, inner), BF16),
        sds((windows, half, model), BF16),
        sds((windows, half, model), F32),
        sds((windows, width, model), BF16),
        sds((windows, width, hidden), BF16),
        sds((windows, width, hidden), BF16),
        sds((windows, half, model), BF16),
    ]
    if last:
        y_shape = sds((FRAMES, 4, 2, 8, model), F32)
        groups = (2 * FRAMES, 4, 2, 8, model)
    else:
        y_shape = sds((4, FRAMES * 4, 8, model), F32)
        groups = (1, 1, 1, 8, model)
    own_buf = pltpu.VMEM((windows, half, model), BF16)
    return pl.pallas_call(
        functools.partial(forward_kernel, windows, last),
        out_shape=saved + [y_shape],
        in_specs=[VM] * 4 + [ANY] * 4,
        out_specs=[ANY] * len(saved) + [VM],
        scratch_shapes=[pltpu.VMEM(w.shape, w.dtype) for w in params]
        + [pltpu.VMEM(s.shape, s.dtype) for s in saved]
        + [own_buf] * 8
        + [pltpu.VMEM((half, model), F32)] * 2
        + [
            pltpu.VMEM(groups, F32),
            dma((4,)),
            dma((len(saved), windows)),
        ]
        + [dma((2, windows))] * 6
        + [dma((2, 2))],
        compiler_params=pltpu.CompilerParams(
            collective_id=collective_id, has_side_effects=True, vmem_limit_bytes=VMEM_LIMIT
        ),
        name="forward_last" if last else "forward_first",
    )(stream, mod, mask, bias, qkv_w, proj_w, fc1_w, fc2_w)


def backward_kernel(windows, last, size, names, *refs):
    r = dict(zip(names, refs, strict=True))
    mod, index = r["mod"], r["index"]
    grad, part1, part2, gh, gqkv = r["grad"], r["part1"], r["part2"], r["gh"], r["gqkv"]
    fc1_w, fc2_w, qkv_w, proj_w = r["fc1_w"], r["fc2_w"], r["qkv_w"], r["proj_w"]
    gm, ga, rest, wgrad, gbias = r["gm"], r["ga"], r["rest"], r["wgrad"], r["gbias"]
    ps1s, ps1r, ps2s, ps2r = r["ps1s"], r["ps1r"], r["ps2s"], r["ps2r"]
    xs1s, xs1r, xs2s, xs2r = r["xs1s"], r["xs1r"], r["xs2s"], r["xs2r"]
    buf1, buf2, msum, mtot, mrecv = r["buf1"], r["buf2"], r["msum"], r["mtot"], r["mrecv"]
    _, half, model = grad.shape
    width = 2 * half
    heads = gbias.shape[0]
    inner = proj_w.shape[0]
    head_dim = inner // heads
    hidden = wgrad.shape[1] // 2
    scale = head_dim ** (-0.5)
    chunk = buf1.shape[-1]
    fc_chunks = hidden // chunk
    rest_chunks = 4 * inner // chunk
    x, core, sibling, partner = places()
    own = pl.ds(pl.multiple_of(core * half, 16), half)
    theirs = pl.ds(pl.multiple_of((1 - core) * half, 16), half)
    lines = size // 2
    here = lax.axis_index("dp")
    line, side = lax.div(here, 2), lax.rem(here, 2)

    loads = [
        pltpu.make_async_copy(r[src], r[dst], r["w_sem"].at[i])
        for i, (src, dst) in enumerate(
            (("fc2", "fc2_w"), ("fc1", "fc1_w"), ("proj", "proj_w"), ("qkv", "qkv_w"))
            + (("grad_y", "grad"),)
            + (() if last else (("carry", "rest"),))
        )
    ]
    streams = [
        (r[name], r[name + "_v"])
        for name in ("act", "dg", "h2", "qkv_s", "prob", "att", "h1", "x1", "ao", "mo", "stream")
    ]

    def fetch(which, f):
        src, dst = streams[which]
        slot = lax.rem(f, 2)
        return pltpu.make_async_copy(src.at[f], dst.at[slot], r["in_sem"].at[which, slot])

    def share(buf, sem, f, rows):
        return remote(buf.at[f, own], buf.at[f, rows], sem.at[0, f], sem.at[1, f], sibling)

    def to_sibling(src, dst, sem, f):
        slot = lax.rem(f, 2)
        return remote(src.at[slot], dst.at[slot], sem.at[0, slot], sem.at[1, slot], sibling)

    def first_ps(f):
        return to_sibling(ps1s, ps1r, r["ps1_sem"], f)

    def second_ps(f):
        return to_sibling(ps2s, ps2r, r["ps2_sem"], f)

    def first_xs(f):
        sem = r["xs1_sem"]
        return remote(xs1s.at[f], xs1r.at[f], sem.at[0, f], sem.at[1, f], partner)

    def second_xs(f):
        sem, slot = r["xs2_sem"], lax.rem(f, 2)
        return remote(xs2s.at[slot], xs2r.at[f], sem.at[0, slot], sem.at[1, f], partner)

    def along_dp(src, dst, send_sem, recv_sem, other):
        return pltpu.make_async_remote_copy(
            src_ref=src,
            dst_ref=dst,
            send_sem=send_sem,
            recv_sem=recv_sem,
            device_id={"dp": other},
            device_id_type=MESH,
        )

    def chunk_cols(i):
        return pl.ds(pl.multiple_of(i * chunk, chunk), chunk)

    def across(g, k, i):
        return along_dp(
            g.at[:, 1 - side, :, chunk_cols(i)],
            buf1.at[k, i],
            r["across_sem"].at[0, k, i],
            r["across_sem"].at[1, k, i],
            line * 2 + 1 - side,
        )

    def along(k, i, j):
        to = lax.rem(line + 1 + j, lines)
        return along_dp(
            buf1.at[k, i, to],
            buf2.at[k, i, j],
            r["along_sem"].at[0, k, i, j],
            r["along_sem"].at[1, k, i, j],
            to * 2 + side,
        )

    def reduce_side(g, k, i):
        across(g, k, i).wait_recv()
        both = g[:, side, :, chunk_cols(i)].astype(F32) + buf1[k, i].astype(F32)
        buf1[k, i] = both.astype(BF16)
        loop(lines - 1, lambda j: along(k, i, j).start())

    def reduce_line(k, i):
        loop(lines - 1, lambda j: along(k, i, j).wait_recv())
        return buf1[k, i, line].astype(F32) + jnp.sum(buf2[k, i].astype(F32), axis=0)

    loads[4].start()
    for which in range(3):
        fetch(which, 0).start()
    for copy in loads[:4] + loads[5:]:
        copy.start()

    barrier = pltpu.get_barrier_semaphore()
    for other in (sibling, partner):
        pl.semaphore_signal(barrier, inc=1, device_id={"mp": other}, device_id_type=MESH)
    pl.semaphore_signal(
        barrier, inc=1, device_id={"dp": line * 2 + 1 - side}, device_id_type=MESH
    )
    for j in range(lines - 1):
        pl.semaphore_signal(
            barrier,
            inc=1,
            device_id={"dp": lax.rem(line + 1 + j, lines) * 2 + side},
            device_id_type=MESH,
        )
    pl.semaphore_wait(barrier, 2 + lines)

    loads[4].wait()

    def top(f):
        gm[f, own] = (mod[5:6] * grad[f]).astype(BF16)
        share(gm, r["gm_sem"], f, own).start()

    loop(windows, top)
    if not last:
        loads[5].wait()
        loop(rest_chunks, lambda i: across(rest, 2, i).start())
    msum[...] = jnp.zeros_like(msum)
    gbias[...] = jnp.zeros_like(gbias)
    wgrad[...] = jnp.zeros_like(wgrad)

    lane_head = lax.div(lax.broadcasted_iota(jnp.int32, (width, inner), 1), head_dim)
    zero = jnp.zeros((), BF16)

    def flat(weight):
        value = weight[...]
        return value.reshape(-1, value.shape[-1])

    def mlp_back(f):
        slot = lax.rem(f, 2)
        for which in range(3):
            fetch(which, f).wait()
        share(gm, r["gm_sem"], f, theirs).wait_recv()
        gh[...] = (dot_nt(gm[f], flat(fc2_w)) * r["dg_v"][slot].astype(F32)).astype(BF16)

        @pl.when(f >= 2)
        def _():
            first_ps(f - 2).wait_send()

        ps1s[slot] = dot_nt(gh[theirs], flat(fc1_w)).astype(BF16)
        first_ps(f).start()
        part1[...] = dot_nt(gh[own], flat(fc1_w))

    def sum_first(f):
        slot = lax.rem(f, 2)
        first_ps(f).wait_recv()
        xs1s[f] = (part1[...] + ps1r[slot].astype(F32)).astype(BF16)
        first_xs(f).start()

    def mlp_weights(f):
        slot = lax.rem(f, 2)
        for start in range(0, hidden, 512):
            c = pl.ds(start, 512)
            wgrad[:, c] += dot_tn(r["h2_v"][slot], gh[:, c])
        for start in range(0, hidden, 512):
            c, to = pl.ds(start, 512), pl.ds(hidden + start, 512)
            wgrad[:, to] += dot_tn(gm[f], r["act_v"][slot, :, c])

    def fold(values):
        return values.reshape(half // 8, 8, model).sum(axis=0)

    def middle(f):
        slot = lax.rem(f, 2)
        for which in range(7, 10):
            fetch(which, f).wait()
        first_xs(f).wait_recv()
        grad_h = xs1s[f].astype(F32) + xs1r[f].astype(F32)
        normed, inv = norm(r["x1_v"][slot])
        gy = grad[f]
        grad_mid = gy + norm_back(normed, inv, grad_h * (1.0 + mod[4:5]))
        msum[2] += fold(grad_mid * r["ao_v"][slot].astype(F32))
        msum[3] += fold(grad_h)
        msum[4] += fold(grad_h * normed)
        msum[5] += fold(gy * r["mo_v"][slot].astype(F32))
        grad[f] = grad_mid
        ga[f, own] = (mod[2:3] * grad_mid).astype(BF16)
        share(ga, r["ga_sem"], f, own).start()

    def attention_back(f):
        slot = lax.rem(f, 2)
        qkv = r["qkv_s_v"]
        for which in range(3, 7):
            fetch(which, f).wait()
        share(ga, r["ga_sem"], f, theirs).wait_recv()
        grad_att = dot_nt(ga[f], proj_w[...]).astype(BF16)
        grad_att_t = grad_att.T
        queries_t = qkv[slot, :, :inner].T
        keys = qkv[slot, :, inner : 2 * inner] * BF16(scale)
        vals = qkv[slot, :, 2 * inner :]
        grad_q = jnp.zeros((width, inner), F32)
        grad_k, grad_v = [], []
        for h in range(heads):
            part = slice(h * head_dim, (h + 1) * head_dim)
            p = r["prob_v"][slot, h]
            grad_p = dot_nt(jnp.where(lane_head == h, grad_att, zero), vals)
            pf = p.astype(F32)
            weighted = pf * grad_p
            grad_s = weighted - pf * jnp.sum(weighted, axis=-1, keepdims=True)
            gbias[h, :, :width] += grad_s
            rounded = grad_s.astype(BF16)
            grad_q = grad_q + dot(rounded, jnp.where(lane_head == h, keys, zero))
            grad_v.append(dot(grad_att_t[part], p))
            grad_k.append(dot(queries_t[part], rounded) * scale)
        gqkv[:, :inner] = grad_q.astype(BF16)
        gqkv[:, inner : 2 * inner] = jnp.concatenate(grad_k, axis=0).astype(BF16).T
        gqkv[:, 2 * inner :] = jnp.concatenate(grad_v, axis=0).astype(BF16).T

        @pl.when(f >= 2)
        def _():
            second_ps(f - 2).wait_send()

        ps2s[slot] = dot_nt(gqkv[theirs], qkv_w[...]).astype(BF16)
        second_ps(f).start()
        part2[...] = dot_nt(gqkv[own], qkv_w[...])

    def sum_second(f):
        slot = lax.rem(f, 2)
        second_ps(f).wait_recv()

        @pl.when(f >= 2)
        def _():
            second_xs(f - 2).wait_send()

        xs2s[slot] = (part2[...] + ps2r[slot].astype(F32)).astype(BF16)
        second_xs(f).start()

    def attention_weights(f):
        slot = lax.rem(f, 2)
        for start in range(0, 3 * inner, 384):
            c = pl.ds(start, 384)
            wgrad[:, c] += dot_tn(r["h1_v"][slot], gqkv[:, c])
        wgrad[:, 3 * inner : 4 * inner] += dot_tn(ga[f], r["att_v"][slot])

    def finish(f):
        slot = lax.rem(f, 2)
        fetch(10, f).wait()
        second_xs(f).wait_recv()
        grad_h = xs2s[slot].astype(F32) + xs2r[f].astype(F32)
        normed, inv = norm(r["stream_v"][slot].astype(F32))
        msum[0] += fold(grad_h)
        msum[1] += fold(grad_h * normed)
        grad_x = grad[f] + norm_back(normed, inv, grad_h * (1.0 + mod[1:2]))
        if last:
            store_b_to_a(r["gx"], f, grad_x)
        else:
            grad[f] = grad_x

    def first_step(f):
        @pl.when(f + 1 < windows)
        def _():
            for which in range(3):
                fetch(which, f + 1).start()

        @pl.when(f == 0)
        def _():
            loads[0].wait()
            loads[1].wait()

        mlp_back(f)
        sum_first(f)
        mlp_weights(f)
        if not last:

            @pl.when((f >= 1) & (f <= rest_chunks))
            def _():
                reduce_side(rest, 2, f - 1)

    loop(windows, first_step)

    for which in range(3, 11):
        fetch(which, 0).start()
    shape = fc1_w.shape
    fc1_w[...] = wgrad[:, :hidden].astype(BF16).reshape(shape)
    loop(fc_chunks, lambda i: across(fc1_w, 0, i).start())
    fc2_w[...] = wgrad[:, hidden:].astype(BF16).reshape(shape)
    loop(fc_chunks, lambda i: across(fc2_w, 1, i).start())
    wgrad[:, : 4 * inner] = jnp.zeros((model, 4 * inner), F32)
    for which in range(7, 10):
        fetch(which, 1).start()
    middle(0)
    loads[2].wait()
    loads[3].wait()
    offset = windows - fc_chunks

    def second_step(f):
        @pl.when(f + 1 < windows)
        def _():
            for which in range(3, 7):
                fetch(which, f + 1).start()
            middle(f + 1)

        @pl.when(f + 2 < windows)
        def _():
            for which in range(7, 10):
                fetch(which, f + 2).start()

        attention_back(f)
        sum_second(f)
        attention_weights(f)

        @pl.when(f >= 1)
        def _():
            finish(f - 1)

        @pl.when((f >= 1) & (f + 1 < windows))
        def _():
            fetch(10, f + 1).start()

        @pl.when(f == 0)
        def _():
            fetch(10, 1).start()

        @pl.when(f >= offset)
        def _():
            reduce_side(fc1_w, 0, f - offset)
            reduce_side(fc2_w, 1, f - offset)

    loop(windows, second_step)

    if not last:
        loop(rest_chunks, lambda i: across(rest, 2, i).wait_send())
    rest[...] = wgrad[:, : 4 * inner].astype(BF16).reshape(rest.shape)
    if last:
        carry = pltpu.make_async_copy(rest, r["carry"], r["w_sem"].at[5])
        carry.start()
    else:
        loop(rest_chunks, lambda i: across(rest, 3, i).start())
    finish(windows - 1)
    for i in range(6):
        mtot[i : i + 1] = jnp.sum(msum[i], axis=0, keepdims=True)
    mod_copy = remote(mtot, mrecv, r["mod_sem"].at[0], r["mod_sem"].at[1], sibling)
    mod_copy.start()
    hands = []
    if not last:
        gx = r["gx"]

        def group(j):
            which = 5 * x + j
            rows = pl.ds(pl.multiple_of(lax.rem(which, 2) * 64, 64), 64)
            return lax.div(which, 2), rows

        for i in range(2):
            f, rows = group(3 - 3 * core + i)
            hands.append(
                remote(
                    grad.at[f, rows],
                    gx.at[1 + 2 * i],
                    r["hand_sem"].at[0, i],
                    r["hand_sem"].at[1, i],
                    sibling,
                )
            )
            hands[-1].start()
        for i in range(3):
            f, rows = group(2 * core + i)
            gx[2 * i] = grad[f, rows]

    scatter(index, gbias, r["table"])
    fc_out = r["fc_out"]

    def finish_fc(i):
        for k in range(2):
            fc_out[k, :, chunk_cols(i)] = reduce_line(k, i)

    loop(fc_chunks, finish_fc)
    if not last:

        def finish_carry(i):
            r["carry_out"][:, chunk_cols(i)] = reduce_line(2, i)

        loop(rest_chunks, finish_carry)
        loop(rest_chunks, lambda i: reduce_side(rest, 3, i))

        def finish_rest(i):
            r["rest_out"][:, chunk_cols(i)] = reduce_line(3, i)

        loop(rest_chunks, finish_rest)
    else:
        carry.wait()
    mod_copy.wait()
    r["mod_out"][...] = mtot[...] + mrecv[...]
    for copy in hands:
        copy.wait()

    def drain(f):
        share(gm, r["gm_sem"], f, own).wait_send()
        share(ga, r["ga_sem"], f, own).wait_send()
        first_xs(f).wait_send()

    loop(windows, drain)
    for f in range(windows - 2, windows):
        for copy in (first_ps(f), second_ps(f), second_xs(f)):
            copy.wait_send()

    def drain_chunk(k, g, i):
        across(g, k, i).wait_send()
        loop(lines - 1, lambda j: along(k, i, j).wait_send())

    loop(fc_chunks, lambda i: drain_chunk(0, fc1_w, i))
    loop(fc_chunks, lambda i: drain_chunk(1, fc2_w, i))
    if not last:
        loop(rest_chunks, lambda i: loop(lines - 1, lambda j: along(2, i, j).wait_send()))
        loop(rest_chunks, lambda i: drain_chunk(3, rest, i))


def block_backward(stream, grad_y, mod, params, kept, index, table_len, carry, size, collective_id):
    last = carry is None
    qkv_w, proj_w, fc1_w, fc2_w = params
    h1, qkv, prob, att, ao, x1, h2, act, dg, mo = kept
    windows, half, model = stream.shape
    width = 2 * half
    heads = prob.shape[1]
    inner = proj_w.shape[0]
    hidden = fc1_w.shape[1]
    rows = model // size
    lines = size // 2
    chunk = 256
    chunks = max(hidden, 4 * inner) // chunk
    kinds = 2 if last else 4
    groups = (table_len + 127) // 128
    sds = jax.ShapeDtypeStruct
    sliced = (lines, 2, rows)
    cut = (*sliced, hidden)

    ins, outs, scratch = {}, {}, {}
    ins["grad_y"] = (grad_y, ANY)
    ins["mod"] = (mod, VM)
    ins["index"] = (index, VM)
    for name, value in (
        ("act", act),
        ("dg", dg),
        ("h2", h2),
        ("qkv_s", qkv),
        ("prob", prob),
        ("att", att),
        ("h1", h1),
        ("x1", x1),
        ("ao", ao),
        ("mo", mo),
        ("stream", stream),
    ):
        ins[name] = (value, ANY)
        scratch[name + "_v"] = pltpu.VMEM((2,) + value.shape[1:], value.dtype)
    ins["qkv"] = (qkv_w, ANY)
    ins["proj"] = (proj_w, ANY)
    ins["fc1"] = (fc1_w.reshape(cut), ANY)
    ins["fc2"] = (fc2_w.reshape(cut), ANY)
    if not last:
        ins["carry"] = (carry, ANY)
    if last:
        outs["gx"] = (sds((2 * FRAMES, 4, 2, 8, model), F32), VM)
        outs["carry"] = (sds((*sliced, 4 * inner), BF16), ANY)
    else:
        outs["gx"] = (sds((FRAMES, 4 * SIDE, model), F32), VM)
        outs["carry_out"] = (sds((rows, 4 * inner), F32), VM)
        outs["rest_out"] = (sds((rows, 4 * inner), F32), VM)
    outs["fc_out"] = (sds((2, rows, hidden), F32), VM)
    outs["table"] = (sds((128, heads * groups), F32), VM)
    outs["mod_out"] = (sds((6, model), F32), VM)

    own_all = pltpu.VMEM((windows, half, model), BF16)
    own_two = pltpu.VMEM((2, half, model), BF16)
    own_one = pltpu.VMEM((half, model), F32)
    every = pltpu.VMEM((windows, width, model), BF16)
    scratch.update(
        grad=pltpu.VMEM((windows, half, model), F32),
        part1=own_one,
        part2=own_one,
        gh=pltpu.VMEM((width, hidden), BF16),
        gqkv=pltpu.VMEM((width, 3 * inner), BF16),
        fc1_w=pltpu.VMEM(cut, BF16),
        fc2_w=pltpu.VMEM(cut, BF16),
        qkv_w=pltpu.VMEM(qkv_w.shape, BF16),
        proj_w=pltpu.VMEM(proj_w.shape, BF16),
        gm=every,
        ga=every,
        rest=pltpu.VMEM((*sliced, 4 * inner), BF16),
        wgrad=pltpu.VMEM((model, 2 * hidden), F32),
        gbias=pltpu.VMEM((heads, *index.shape), F32),
        ps1s=own_two,
        ps1r=own_two,
        ps2s=own_two,
        ps2r=own_two,
        xs1s=own_all,
        xs2s=own_two,
        xs1r=own_all,
        xs2r=own_all,
        buf1=pltpu.VMEM((kinds, chunks, lines, rows, chunk), BF16),
        buf2=pltpu.VMEM((kinds, chunks, lines - 1, rows, chunk), BF16),
        msum=pltpu.VMEM((6, 8, model), F32),
        mtot=pltpu.VMEM((6, model), F32),
        mrecv=pltpu.VMEM((6, model), F32),
        w_sem=dma((6,)),
        in_sem=dma((11, 2)),
        gm_sem=dma((2, windows)),
        ga_sem=dma((2, windows)),
        ps1_sem=dma((2, 2)),
        ps2_sem=dma((2, 2)),
        xs1_sem=dma((2, windows)),
        xs2_sem=dma((2, windows)),
        hand_sem=dma((2, 2)),
        mod_sem=dma((2,)),
        across_sem=dma((2, kinds, chunks)),
        along_sem=dma((2, kinds, chunks, lines - 1)),
    )
    names = (*ins, *outs, *scratch)
    return pl.pallas_call(
        functools.partial(backward_kernel, windows, last, size, names),
        out_shape=[shape for shape, _ in outs.values()],
        in_specs=[spec for _, spec in ins.values()],
        out_specs=[spec for _, spec in outs.values()],
        scratch_shapes=list(scratch.values()),
        compiler_params=pltpu.CompilerParams(
            collective_id=collective_id, has_side_effects=True, vmem_limit_bytes=VMEM_LIMIT
        ),
        name="backward_last" if last else "backward_first",
    )(*[value for value, _ in ins.values()])


def lookup_kernel(index, table, out):
    heads, groups = table.shape[0], table.shape[1]
    rows, width = index.shape

    def some(r):
        for block in range(width // 128):
            c = pl.ds(block * 128, 128)
            row = index[r, c]
            low = row & 127
            high = row >> 7
            found = [jnp.zeros((16, 128), F32) for _ in range(heads)]
            for g in range(groups):
                here = high == g
                for h in range(heads):
                    spread = jnp.broadcast_to(table[h, pl.ds(g, 1), :], (16, 128))
                    taken = jnp.take_along_axis(spread, low, axis=1, mode="promise_in_bounds")
                    found[h] = jnp.where(here, taken, found[h])
            for h in range(heads):
                out[h, r, c] = found[h].astype(BF16)

    rows16(rows, some)


def bias_lookup(index, table):
    rows, heads = table.shape
    groups = (rows + 127) // 128
    spread = jnp.pad(table.astype(F32), ((0, groups * 128 - rows), (0, 0))).T
    return pl.pallas_call(
        lookup_kernel,
        out_shape=jax.ShapeDtypeStruct((heads,) + index.shape, BF16),
        name="bias_lookup",
    )(index, spread.reshape(heads, groups, 128))


def scatter(index, grad, out):
    heads = grad.shape[0]
    groups = out.shape[1] // heads
    rows, width = index.shape
    out[...] = jnp.zeros_like(out)
    low_rows = lax.broadcasted_iota(jnp.int32, (128, width), 0)
    high_rows = lax.broadcasted_iota(jnp.int32, (groups, width), 0)

    def some(rb):
        r = pl.ds(pl.multiple_of(rb * 8, 8), 8)
        index_rows = index[r, :]
        low = index_rows & 127
        high = index_rows >> 7
        grads = [grad[h, r, :] for h in range(heads)]
        total = out[...]
        for i in range(8):
            onehot = jnp.where(low_rows == low[i : i + 1], 1.0, 0.0).astype(BF16)
            here = high_rows == high[i : i + 1]
            placed = jnp.concatenate(
                [jnp.where(here, g[i : i + 1], 0.0) for g in grads], axis=0
            ).astype(BF16)
            total = total + dot_nt(onehot, placed)
        out[...] = total

    loop(rows // 8, some)


def place_index(index, layout):
    if layout == 0:
        cut, order, pad = (2, 2, 64), (1, 0, 2), 0
    else:
        cut, order, pad = (FRAMES, 2, 32), (1, 0, 2), 64
    side = index.shape[0]
    both = index.reshape(cut + cut)
    both = both.transpose(order + tuple(3 + o for o in order)).reshape(side, side)
    return jnp.pad(both, ((0, 0), (0, pad)), constant_values=-1)


def local(
    tokens,
    cond,
    pad_mask,
    spatial_index,
    joint_index,
    qkv_a,
    proj_a,
    fc1_a,
    fc2_a,
    table_a,
    ada_a,
    qkv_b,
    proj_b,
    fc1_b,
    fc2_b,
    table_b,
    ada_b,
    cotangent,
    dp_size,
    mp_size,
):
    model = tokens.shape[1]
    inner = proj_a.shape[0]
    hidden = fc1_a.shape[1]
    core = lax.rem(lax.axis_index("mp"), 2)
    params_a = (qkv_a.reshape(model, -1), proj_a, fc1_a, fc2_a)
    params_b = (qkv_b.reshape(model, -1), proj_b, fc1_b, fc2_b)

    def own_rows(values):
        whole = lax.all_gather(values, "mp", axis=0, tiled=True)
        cut = whole.reshape(2 * FRAMES, 2, 4 * SIDE, model)
        return lax.dynamic_index_in_dim(cut, core, axis=1, keepdims=False)

    cond_act = jax.nn.silu(cond.astype(F32)).astype(BF16)
    parts = jnp.concatenate(
        [jnp.dot(cond_act, ada, preferred_element_type=F32) for ada in (ada_a, ada_b)], axis=0
    )
    mods = lax.all_gather(parts, "mp", axis=1, tiled=True).reshape(2, 6, model)

    x_a = own_rows(tokens).reshape(FRAMES, -1, model)
    grad_top = own_rows(cotangent).astype(F32).reshape(FRAMES, 2, 4, 2, 8, model)
    grad_top = grad_top.transpose(1, 3, 0, 2, 4, 5).reshape(4, -1, model)

    index_a = place_index(spatial_index, 0)
    index_b = place_index(joint_index, 1)
    bias_a = bias_lookup(index_a, table_a)
    bias_b = bias_lookup(index_b, table_b)
    hidden_keys = jnp.where(pad_mask.reshape(-1) > 0, 0.0, -1e30).astype(F32)
    mask_a = hidden_keys.reshape(FRAMES, 2, 2, 64).transpose(0, 2, 1, 3).reshape(FRAMES, 1, -1)
    mask_b = hidden_keys.reshape(FRAMES, 2, 2, 4, 2, 8).transpose(1, 4, 2, 0, 3, 5)
    mask_b = mask_b.reshape(4, 1, -1)

    *kept_a, y_a = block_forward(x_a, mods[0], params_a, bias_a, mask_a, False, 1)
    x_b = y_a.reshape(4, -1, model)
    *kept_b, output = block_forward(x_b, mods[1], params_b, bias_b, mask_b, True, 2)
    grad_mid, carry, fc_b, table_grad_b, mod_b = block_backward(
        x_b, grad_top, mods[1], params_b, kept_b, index_b, table_b.shape[0], None, dp_size, 3
    )
    grad_mid = grad_mid.reshape(FRAMES, -1, model)
    grad_x, rest_b, rest_a, fc_a, table_grad_a, mod_a = block_backward(
        x_a, grad_mid, mods[0], params_a, kept_a, index_a, table_a.shape[0], carry, dp_size, 4
    )

    wide = ada_a.shape[1]
    first = lax.axis_index("mp") * wide
    mod_columns = [
        lax.dynamic_slice_in_dim(m.reshape(-1), first, wide, axis=0) for m in (mod_a, mod_b)
    ]
    small = jnp.concatenate(
        [cond_act.astype(F32).reshape(-1)]
        + mod_columns
        + [table_grad_a.reshape(-1), table_grad_b.reshape(-1)]
    )
    everyone = lax.all_gather(small, "dp", axis=0, tiled=False)
    cut = [model, model + wide, model + 2 * wide, model + 2 * wide + table_grad_a.size]
    conds, cols_a, cols_b, tables_a, tables_b = jnp.split(everyone, cut, axis=1)
    rows_here = model // dp_size
    my_conds = lax.dynamic_slice_in_dim(conds, lax.axis_index("dp") * rows_here, rows_here, axis=1)

    def outer(columns):
        return jnp.einsum("td,tc->dc", my_conds, columns, precision=HIGHEST)

    def table(parts, like, length):
        heads = table_a.shape[1]
        summed_table = jnp.sum(parts, axis=0).reshape(128, heads, -1)
        return summed_table.transpose(2, 0, 1).reshape(-1, heads)[:length]

    def split(rest, fc):
        return (
            rest[:, : 3 * inner].reshape(rows_here, 3, inner),
            rest[:, 3 * inner :].T,
            fc[0],
            fc[1].T,
        )

    return (
        output.reshape(tokens.shape),
        grad_x.reshape(tokens.shape),
        *split(rest_a, fc_a),
        table(tables_a, table_grad_a, table_a.shape[0]),
        outer(cols_a),
        *split(rest_b, fc_b),
        table(tables_b, table_grad_b, table_b.shape[0]),
        outer(cols_b),
    )


def solution(mesh):
    in_specs = (
        P(("dp", "mp"), None),
        P("dp", None),
        P("dp", None),
        P(),
        P(),
        P(None, None, "mp"),
        P("mp", None),
        P(None, "mp"),
        P("mp", None),
        P(None, "mp"),
        P(None, "mp"),
        P(None, None, "mp"),
        P("mp", None),
        P(None, "mp"),
        P("mp", None),
        P(None, "mp"),
        P(None, "mp"),
        P(("dp", "mp"), None),
    )
    out_specs = (
        P(("dp", "mp"), None),
        P(("dp", "mp"), None),
        P("dp", None, "mp"),
        P("mp", "dp"),
        P("dp", "mp"),
        P("mp", "dp"),
        P(None, "mp"),
        P("dp", "mp"),
        P("dp", None, "mp"),
        P("mp", "dp"),
        P("dp", "mp"),
        P("mp", "dp"),
        P(None, "mp"),
        P("dp", "mp"),
    )
    body = functools.partial(local, dp_size=mesh.shape["dp"], mp_size=mesh.shape["mp"])
    return jax.shard_map(body, mesh=mesh, in_specs=in_specs, out_specs=out_specs, check_vma=False)
```

```python
import functools

import jax
import jax.numpy as jnp
from jax import lax
from jax.experimental import pallas as pl
from jax.experimental.pallas import tpu as pltpu
from jax.sharding import PartitionSpec as P

FRAMES = 5
SIDE = 16
EPSILON = 1e-06
HIGHEST = lax.Precision.HIGHEST
MESH = pl.DeviceIdType.MESH
F32 = jnp.float32
BF16 = jnp.bfloat16
VMEM_LIMIT = 60 << 20
GELU_K = 0.7978845608028654
GELU_C = 0.044715
ANY = pl.BlockSpec(memory_space=pl.ANY)
VM = pl.BlockSpec(memory_space=pltpu.VMEM)


def own_rows(src, dst, sems, x, core, sibling, partner, diagonal):
    sends, local, recvs = sems

    def place(j):
        return dst.at[lax.div(j, 2), lax.rem(j, 2)]

    def moves():
        found = []
        for k in range(5):
            j = 5 * x + lax.div(5 * core + k, 2)
            to = (partner,) if k % 2 == 0 else (diagonal, sibling)
            for i, other in enumerate(to):
                found.append(remote(src.at[k], place(j), sends.at[k, i], recvs.at[j], other))
            if k % 2 == 0:
                found.append(pltpu.make_async_copy(src.at[k], place(j), local.at[k // 2]))
        return found

    def start():
        for copy in moves():
            copy.start()

    def wait(j):
        row = 2 * j + core
        k = lax.rem(row, 5)
        here = (lax.div(row, 10) == x) & (lax.div(lax.rem(row, 10), 5) == core)

        @pl.when(here)
        def _():
            pltpu.make_async_copy(src.at[k], place(j), local.at[lax.div(k, 2)]).wait()

        @pl.when(jnp.logical_not(here))
        def _():
            remote(src.at[0], place(j), sends.at[0, 0], recvs.at[j], partner).wait_recv()

    def drain():
        for k in range(5):
            for i in range(1 if k % 2 == 0 else 2):
                remote(src.at[k], place(0), sends.at[k, i], recvs.at[0], partner).wait_send()

    return start, wait, drain


def dma(shape):
    return pltpu.SemaphoreType.DMA(shape)


def places():
    me = lax.axis_index("mp")
    x = lax.div(me, 2)
    core = lax.rem(me, 2)
    return x, core, x * 2 + 1 - core, (1 - x) * 2 + core, (1 - x) * 2 + 1 - core


def greet(others):
    barrier = pltpu.get_barrier_semaphore()
    for other in others:
        pl.semaphore_signal(barrier, inc=1, device_id={"mp": other}, device_id_type=MESH)
    pl.semaphore_wait(barrier, len(others))


def remote(src, dst, send_sem, recv_sem, other):
    return pltpu.make_async_remote_copy(
        src_ref=src,
        dst_ref=dst,
        send_sem=send_sem,
        recv_sem=recv_sem,
        device_id={"mp": other},
        device_id_type=MESH,
    )


def loop(count, body):
    def step(i, _):
        body(i)
        return 0

    lax.fori_loop(0, count, step, 0)


def rows16(count, body, step=16):
    loop(count // step, lambda i: body(pl.ds(pl.multiple_of(i * step, step), step)))


def norm(values):
    centred = values - jnp.mean(values, axis=-1, keepdims=True)
    inv = lax.rsqrt(jnp.mean(centred * centred, axis=-1, keepdims=True) + EPSILON)
    return centred * inv, inv


def norm_back(normed, inv, grad):
    mean_g = jnp.mean(grad, axis=-1, keepdims=True)
    mean_gn = jnp.mean(grad * normed, axis=-1, keepdims=True)
    return (grad - mean_g - normed * mean_gn) * inv


def dot(a, b):
    return jnp.dot(a, b, preferred_element_type=F32)


def dot_nt(a, b):
    return lax.dot_general(a, b, (((1,), (1,)), ((), ())), preferred_element_type=F32)


def dot_tn(a, b):
    return lax.dot_general(a, b, (((0,), (0,)), ((), ())), preferred_element_type=F32)


def store_a_to_b(dst, frame, value):
    shaped = value.reshape(2, 4, 2, 8, value.shape[-1])
    for qr in range(2):
        for qc in range(2):
            dst[qr * 2 + qc, pl.ds(pl.multiple_of(frame * 4, 4), 4)] = shaped[qr, :, qc]


def store_b_to_a(dst, window, value):
    shaped = value.reshape(FRAMES, 4, 8, value.shape[-1])
    qr, qc = lax.div(window, 2), lax.rem(window, 2)
    for frame in range(FRAMES):
        dst[frame * 2 + qr, :, qc] = shaped[frame]


def store_a_to_a(dst, frame, value):
    shaped = value.reshape(2, 4, 2, 8, value.shape[-1])
    for qr in range(2):
        dst[frame * 2 + qr] = shaped[qr]


def hand_out(groups, out, send_sem, recv_sem, x, core, sibling):
    copies = []
    for i in range(2):
        copies.append(
            remote(
                groups.at[5 * x + 3 - 3 * core + i],
                out.at[1 + 2 * i],
                send_sem.at[i],
                recv_sem.at[i],
                sibling,
            )
        )
        copies[-1].start()
    for i in range(3):
        out[2 * i] = groups[5 * x + 2 * core + i]
    for copy in copies:
        copy.wait()


def forward_kernel(windows, last, names, *refs):
    r = dict(zip(names, refs, strict=True))
    stream, mask, bias, y_out = r["stream"], r["mask"], r["bias"], r["y"]
    mod = r["mod"] if last else r["mods"].at[0]
    qkv_w, proj_w, fc1_w, fc2_w = r["qkv_w"], r["proj_w"], r["fc1_w"], r["fc2_w"]
    h1, qkv, prob, att, ao = r["h1_v"], r["qkv_s_v"], r["prob_v"], r["att_v"], r["ao_v"]
    x1, h2, act, dg, mo = r["x1_v"], r["h2_v"], r["act_v"], r["dg_v"], r["mo_v"]
    ps1s, ps1r, ps2s, ps2r = r["ps1s"], r["ps1r"], r["ps2s"], r["ps2r"]
    xs1s, xs1r, xs2s, xs2r = r["xs1s"], r["xs1r"], r["xs2s"], r["xs2r"]
    part1, part2, out_sem = r["part1"], r["part2"], r["out_sem"]
    h1_sem, h2_sem, ps1_sem, ps2_sem = r["h1_sem"], r["h2_sem"], r["ps1_sem"], r["ps2_sem"]
    xs1_sem, xs2_sem = r["xs1_sem"], r["xs2_sem"]
    width = h1.shape[1]
    half = width // 2
    model = h1.shape[2]
    heads = bias.shape[0]
    inner = proj_w.shape[0]
    head_dim = inner // heads
    x, core, sibling, partner, diagonal = places()
    own = pl.ds(pl.multiple_of(core * half, 16), half)
    theirs = pl.ds(pl.multiple_of((1 - core) * half, 16), half)

    weights = [
        pltpu.make_async_copy(r[name], r[name + "_w"], r["w_sem"].at[i])
        for i, name in enumerate(("qkv", "proj", "fc1", "fc2"))
    ]
    for copy in weights:
        copy.start()
    saves = [
        (r[name + "_v"], r[name])
        for name in ("h1", "qkv_s", "prob", "att", "ao", "x1", "h2", "act", "dg", "mo")
        + (("gm",) if last else ())
    ]

    def save(which, f):
        src, dst = saves[which]
        return pltpu.make_async_copy(src.at[f], dst.at[f], out_sem.at[which, f])

    def share(buf, sem, f, rows):
        return remote(buf.at[f, own], buf.at[f, rows], sem.at[0, f], sem.at[1, f], sibling)

    def to_sibling(src, dst, sem, f):
        return remote(src.at[f], dst.at[f], sem.at[0, f], sem.at[1, f], sibling)

    def to_partner(src, dst, sem, f):
        return remote(src.at[f], dst.at[f], sem.at[0, f], sem.at[1, f], partner)

    greet((sibling, partner, diagonal))
    rows_start, rows_wait, rows_drain = own_rows(
        r["rows"],
        r["top_rows"] if last else stream,
        (r["rows_send"], r["rows_local"], r["rows_recv"]),
        x,
        core,
        sibling,
        partner,
        diagonal,
    )
    if not last:
        me = lax.axis_index("mp")
        pieces, mods = r["pieces"], r["mods"]
        mod_copies = []
        for i in range(3):
            mod_copies.append(
                remote(
                    r["parts"],
                    pieces.at[me],
                    r["mod_sem"].at[0, i],
                    r["mod_sem"].at[1, i],
                    lax.rem(me + 1 + i, 4),
                )
            )
            mod_copies[-1].start()
        pieces[me] = r["parts"][...]
    rows_start()
    if not last:
        rows16(width, lambda rows: lookup(r["index"], r["table"], bias, rows))
        for copy in mod_copies:
            copy.wait()
        for i in range(12):
            half_row = pl.ds(i % 2 * 512, 512)
            for b in range(2):
                mods[b, pl.ds(i // 2, 1), half_row] = pieces[i // 3, b, pl.ds(i % 3, 1)]

    def own_stream(f):
        return stream[f].astype(F32).reshape(half, model)

    def first_norm(f):
        if not last:
            rows_wait(2 * f)
            rows_wait(2 * f + 1)
            keep_stream(f).start()
        normed, _ = norm(own_stream(f))
        h1[f, own] = (normed * (1.0 + mod[1:2]) + mod[0:1]).astype(BF16)
        share(h1, h1_sem, f, own).start()

    def keep_stream(f):
        return pltpu.make_async_copy(stream.at[f], r["stream_s"].at[f], r["top_sem"].at[f])

    loop(windows if last else 2, first_norm)
    weights[0].wait()
    weights[1].wait()

    def top():
        def place(f):
            rows_wait(2 * f)
            rows_wait(2 * f + 1)
            store_a_to_b(r["top_v"], f, r["top_rows"][f].astype(F32).reshape(-1, model))

        loop(FRAMES, place)

        def give(f):
            grad = r["top_v"][f].reshape(half, model)
            pltpu.make_async_copy(r["top_v"].at[f], r["top"].at[f], r["top_sem"].at[f]).start()
            r["gm_v"][f, own] = (mod[5:6] * grad).astype(BF16)
            share(r["gm_v"], r["gm_sem"], f, own).start()

        loop(windows, give)

    def top_weights():
        def some(f):
            share(r["gm_v"], r["gm_sem"], f, theirs).wait_recv()
            save(10, f).start()

        loop(windows, some)
        grads, acts = r["gm_v"][...].reshape(-1, model), act[...].reshape(-1, act.shape[2])
        fc2_grad = r["fc2_grad_v"]
        for start in range(0, acts.shape[1], 256):
            c = slice(start, start + 256)
            piece = dot_tn(grads, acts[:, c]).astype(BF16)
            fc2_grad[..., c] = piece.reshape(*fc2_grad.shape[:-1], 256)
        grad_copy().start()

    def grad_copy():
        return pltpu.make_async_copy(r["fc2_grad_v"], r["fc2_grad"], r["w_sem"].at[4])

    lane_head = lax.div(lax.broadcasted_iota(jnp.int32, (width, inner), 1), head_dim)

    def attention(f):
        share(h1, h1_sem, f, theirs).wait_recv()
        save(0, f).start()
        qkv[f] = dot(h1[f], qkv_w[...]).astype(BF16)
        save(1, f).start()
        queries = qkv[f, :, :inner] * BF16(head_dim ** (-0.5))
        keys = qkv[f, :, inner : 2 * inner]
        vals = qkv[f, :, 2 * inner :]
        zero = jnp.zeros((), BF16)
        out = jnp.zeros((width, inner), F32)
        for h in range(heads):
            scores = dot_nt(jnp.where(lane_head == h, queries, zero), keys)
            scores = scores + bias[h, :, :width].astype(F32) + mask[f]
            weight = jnp.exp(scores - jnp.max(scores, axis=-1, keepdims=True))
            p = (weight * (1.0 / jnp.sum(weight, axis=-1, keepdims=True))).astype(BF16)
            prob[f, h] = p
            out = out + dot(p, jnp.where(lane_head == h, vals, zero))
        att[f] = out.astype(BF16)
        save(2, f).start()
        save(3, f).start()

        ps1s[f] = dot(att[f, theirs], proj_w[...]).astype(BF16)
        to_sibling(ps1s, ps1r, ps1_sem, f).start()
        part1[...] = dot(att[f, own], proj_w[...])

    def sum_first(f):
        to_sibling(ps1s, ps1r, ps1_sem, f).wait_recv()
        xs1s[f] = (part1[...] + ps1r[f].astype(F32)).astype(BF16)
        to_partner(xs1s, xs1r, xs1_sem, f).start()

    def sum_second(f):
        to_sibling(ps2s, ps2r, ps2_sem, f).wait_recv()
        xs2s[f] = (part2[...] + ps2r[f].astype(F32)).astype(BF16)
        to_partner(xs2s, xs2r, xs2_sem, f).start()

    def middle(f):
        to_partner(xs1s, xs1r, xs1_sem, f).wait_recv()

        total = xs1s[f].astype(F32) + xs1r[f].astype(F32)
        mid = own_stream(f) + mod[2:3] * total
        ao[f] = total.astype(BF16)
        x1[f] = mid
        normed, _ = norm(mid)
        h2[f, own] = (normed * (1.0 + mod[4:5]) + mod[3:4]).astype(BF16)
        share(h2, h2_sem, f, own).start()
        save(4, f).start()
        save(5, f).start()

    def mlp(f):
        share(h2, h2_sem, f, theirs).wait_recv()
        save(6, f).start()

        for start in range(0, act.shape[2], 256):
            c = pl.ds(start, 256)
            u = dot(h2[f], fc1_w[:, c])
            sq = u * u
            t = jnp.tanh(GELU_K * (u + GELU_C * u * sq))
            one_t = 0.5 * (1.0 + t)
            act[f, :, c] = (u * one_t).astype(BF16)
            slope = one_t + (0.5 * GELU_K) * u * (1.0 - t * t) * (1.0 + (3.0 * GELU_C) * sq)
            dg[f, :, c] = slope.astype(BF16)
        save(7, f).start()
        save(8, f).start()
        ps2s[f] = dot(act[f, theirs], fc2_w[...]).astype(BF16)
        to_sibling(ps2s, ps2r, ps2_sem, f).start()
        part2[...] = dot(act[f, own], fc2_w[...])

    def finish(f):
        to_partner(xs2s, xs2r, xs2_sem, f).wait_recv()

        total = xs2s[f].astype(F32) + xs2r[f].astype(F32)
        mo[f] = total.astype(BF16)
        save(9, f).start()
        result = x1[f] + mod[5:6] * total
        if last:
            store_b_to_a(r["groups"], f, result)
        else:
            store_a_to_b(y_out, f, result)

    def step(t):
        @pl.when((t >= 2) & (t < windows + 2))
        def _():
            @pl.when(t == 2)
            def _():
                weights[2].wait()
                weights[3].wait()

            mlp(t - 2)

        @pl.when(t < windows)
        def _():
            attention(t)

        @pl.when((t >= 2) & (t < windows + 2))
        def _():
            sum_second(t - 2)

        @pl.when(t < windows)
        def _():
            sum_first(t)

        if last:

            @pl.when(t == 2)
            def _():
                top()

            @pl.when(t == windows + 1)
            def _():
                top_weights()

        @pl.when(t >= 3)
        def _():
            finish(t - 3)

        @pl.when((t >= 1) & (t < windows + 1))
        def _():
            middle(t - 1)

        if not last:

            @pl.when(t + 2 < windows)
            def _():
                first_norm(t + 2)

            blocks = r["next_index"].shape[0] // 16
            each = -(-blocks // (windows + 1))

            def next_bias(i):
                block = t * each + i

                @pl.when(block < blocks)
                def _():
                    rows = pl.ds(pl.multiple_of(block * 16, 16), 16)
                    lookup(r["next_index"], r["next_table"], r["next_bias"], rows)

            loop(each, next_bias)

    loop(windows + 3, step)
    if last:
        hand_out(r["groups"], y_out, r["hand_sem"].at[0], r["hand_sem"].at[1], x, core, sibling)

    def drain(f):
        for which in range(len(saves)):
            save(which, f).wait()
        share(h1, h1_sem, f, own).wait_send()
        share(h2, h2_sem, f, own).wait_send()
        to_sibling(ps1s, ps1r, ps1_sem, f).wait_send()
        to_sibling(ps2s, ps2r, ps2_sem, f).wait_send()
        to_partner(xs1s, xs1r, xs1_sem, f).wait_send()
        to_partner(xs2s, xs2r, xs2_sem, f).wait_send()
        if last:
            share(r["gm_v"], r["gm_sem"], f, own).wait_send()
            pltpu.make_async_copy(r["top_v"].at[f], r["top"].at[f], r["top_sem"].at[f]).wait()
        else:
            keep_stream(f).wait()

    loop(windows, drain)
    rows_drain()
    if last:
        grad_copy().wait()


def block_forward(rows, first, then, params, mask, size, collective_id):
    last = then is not None
    qkv_w, proj_w, fc1_w, fc2_w = params
    windows, _, width = mask.shape
    model = rows.shape[-1]
    half = width // 2
    heads = then[2].shape[0] if last else first[2].shape[0]
    inner = proj_w.shape[0]
    hidden = fc1_w.shape[1]
    sds = jax.ShapeDtypeStruct
    ins = {"rows": (rows, ANY), "mask": (mask, VM)}
    outs, scratch = {}, {}
    if last:
        ins.update({name: (v, VM) for name, v in zip(("stream", "mod", "bias"), then, strict=True)})
    else:
        given = ("parts", "index", "table", "next_index", "next_table")
        ins.update({name: (v, VM) for name, v in zip(given, first, strict=True)})
        outs["mods"] = (sds((2, 6, model), F32), VM)
        outs["next_bias"] = (sds((heads, *first[3].shape), BF16), VM)
        outs["stream_s"] = (sds((windows, 2, half // 2, model), BF16), ANY)
        scratch["stream"] = pltpu.VMEM((windows, 2, half // 2, model), BF16)
        scratch["bias"] = pltpu.VMEM((heads, *first[1].shape), BF16)
        scratch["pieces"] = pltpu.VMEM((4, 2, 3, 512), F32)
        scratch["mod_sem"] = dma((2, 3))
    scratch["rows_send"] = dma((5, 2))
    scratch["rows_local"] = dma((3,))
    scratch["rows_recv"] = dma((2 * FRAMES,))
    for name, value in (("qkv", qkv_w), ("proj", proj_w), ("fc1", fc1_w), ("fc2", fc2_w)):
        ins[name] = (value, ANY)
        scratch[name + "_w"] = pltpu.VMEM(value.shape, value.dtype)
    saved = {
        "h1": ((windows, width, model), BF16),
        "qkv_s": ((windows, width, 3 * inner), BF16),
        "prob": ((windows, heads, width, width), BF16),
        "att": ((windows, width, inner), BF16),
        "ao": ((windows, half, model), BF16),
        "x1": ((windows, half, model), F32),
        "h2": ((windows, width, model), BF16),
        "act": ((windows, width, hidden), BF16),
        "dg": ((windows, width, hidden), BF16),
        "mo": ((windows, half, model), BF16),
    }
    if last:
        outs["top"] = (sds((windows, half // 8, 8, model), F32), ANY)
        scratch["top_v"] = pltpu.VMEM((windows, half // 8, 8, model), F32)
        scratch["top_rows"] = pltpu.VMEM((FRAMES, 2, 4 * SIDE, model), BF16)
        saved["gm"] = ((windows, width, model), BF16)
        saved["fc2_grad"] = ((size // 2, 2, model // size, hidden), BF16)
    for name, (shape, dtype) in saved.items():
        outs[name] = (sds(shape, dtype), ANY)
        scratch[name + "_v"] = pltpu.VMEM(shape, dtype)
    if last:
        outs["y"] = (sds((FRAMES, 4, 2, 8, model), F32), VM)
        scratch["groups"] = pltpu.VMEM((2 * FRAMES, 4, 2, 8, model), F32)
    else:
        outs["y"] = (sds((4, FRAMES * 4, 8, model), F32), VM)
    own_all = pltpu.VMEM((windows, half, model), BF16)
    for name in ("ps1s", "ps1r", "xs1s", "xs1r", "ps2s", "ps2r", "xs2s", "xs2r"):
        scratch[name] = own_all
    for name in ("h1", "h2", "gm", "ps1", "ps2", "xs1", "xs2"):
        scratch[name + "_sem"] = dma((2, windows))
    scratch.update(
        part1=pltpu.VMEM((half, model), F32),
        part2=pltpu.VMEM((half, model), F32),
        w_sem=dma((5,)),
        out_sem=dma((11, windows)),
        top_sem=dma((windows,)),
        hand_sem=dma((2, 2)),
    )
    names = (*ins, *outs, *scratch)
    results = pl.pallas_call(
        functools.partial(forward_kernel, windows, last, names),
        out_shape=[shape for shape, _ in outs.values()],
        in_specs=[spec for _, spec in ins.values()],
        out_specs=[spec for _, spec in outs.values()],
        scratch_shapes=list(scratch.values()),
        compiler_params=pltpu.CompilerParams(
            collective_id=collective_id, has_side_effects=True, vmem_limit_bytes=VMEM_LIMIT
        ),
        name="forward_last" if last else "forward_first",
    )(*[value for value, _ in ins.values()])
    return dict(zip(outs, results, strict=True))


STREAMS = ("dg", "h2", "qkv_s", "prob", "att", "h1", "x1", "ao", "mo", "stream")


def backward_kernel(windows, last, size, names, *refs):
    r = dict(zip(names, refs, strict=True))
    mod, index = r["mod"], r.get("index")
    grad, part1, part2, gh, gqkv = r["grad"], r["part1"], r["part2"], r["gh"], r["gqkv"]
    fc1_w, fc2_w, qkv_w, proj_w = r["fc1_w"], r["fc2_w"], r["qkv_w"], r["proj_w"]
    gm, ga, rest, wgrad, gbias = r["gm"], r["ga"], r["rest"], r["wgrad"], r["gbias"]
    ps1s, ps1r, ps2s, ps2r = r["ps1s"], r["ps1r"], r["ps2s"], r["ps2r"]
    xs1s, xs1r, xs2s, xs2r = r["xs1s"], r["xs1r"], r["xs2s"], r["xs2r"]
    buf1, buf2, msum, mtot, mrecv = r["buf1"], r["buf2"], r["msum"], r["mtot"], r["mrecv"]
    _, half, model = grad.shape
    width = 2 * half
    heads = gbias.shape[0]
    inner = proj_w.shape[0]
    head_dim = inner // heads
    hidden = gh.shape[1]
    scale = head_dim ** (-0.5)
    chunk = buf1.shape[-1]
    fc_chunks = hidden // chunk
    rest_chunks = 4 * inner // chunk
    carry_chunks = r["carry"].shape[-1] // chunk
    early_chunks = rest_chunks // 2 if last else rest_chunks
    kinds = {"fc1": 0, "carry": 1, "rest": 2, "fc2": 3}
    sources = {"fc1": fc1_w, "carry": rest, "rest": rest, "fc2": r.get("fc2_grad")}
    if last:
        plan = {
            (0, 1): [("carry", 0)],
            (0, 2): [("carry", 1)],
            (0, 3): [("carry", 2)],
            (1, 0): [("carry", 3), ("fc1", 0)],
            (1, 1): [("fc1", 1)],
            (1, 2): [("fc1", 2)],
            (1, 3): [("fc1", 3)],
        }
    else:
        plan = {
            (0, 1): [("carry", 0)],
            (0, 2): [("carry", 1)],
            (0, 4): [("fc2", 0)],
            (1, 0): [("fc2", 1), ("fc2", 2)],
            (1, 1): [("fc2", 3)],
            (1, 2): [("fc1", 0)],
            (1, 3): [("fc1", 1)],
            (1, 4): [("fc1", 2)],
            (2, 0): [("fc1", 3)],
        }
    x, core, sibling, partner, diagonal = places()
    own = pl.ds(pl.multiple_of(core * half, 16), half)
    theirs = pl.ds(pl.multiple_of((1 - core) * half, 16), half)
    lines = size // 2
    here = lax.axis_index("dp")
    line, side = lax.div(here, 2), lax.rem(here, 2)

    loads = [
        pltpu.make_async_copy(
            r[src],
            r[dst] if dst else rest.at[..., pl.ds(0, r["carry"].shape[-1])],
            r["w_sem"].at[i],
        )
        for i, (src, dst) in enumerate(
            (("fc2", "fc2_w"), ("fc1", "fc1_w"), ("proj", "proj_w"), ("qkv", "qkv_w"))
            + (("grad_y", "grad"), ("carry", None))
            + ((("gm_s", "gm"),) if last else (("act", "act_v"),))
        )
    ]
    for_mlp = ("dg", "h2")
    for_attention = ("qkv_s", "prob", "att", "h1")
    for_middle = ("x1", "ao", "mo")

    def fetch(name, f):
        slot = lax.rem(f, 2)
        sem = r["in_sem"].at[STREAMS.index(name), slot]
        return pltpu.make_async_copy(r[name].at[f], r[name + "_v"].at[slot], sem)

    def share(buf, sem, f, rows):
        return remote(buf.at[f, own], buf.at[f, rows], sem.at[0, f], sem.at[1, f], sibling)

    def to_sibling(src, dst, sem, f):
        slot = lax.rem(f, 2)
        return remote(src.at[slot], dst.at[slot], sem.at[0, slot], sem.at[1, slot], sibling)

    def first_ps(f):
        return to_sibling(ps1s, ps1r, r["ps1_sem"], f)

    def second_ps(f):
        return to_sibling(ps2s, ps2r, r["ps2_sem"], f)

    def first_xs(f):
        sem = r["xs1_sem"]
        return remote(xs1s.at[f], xs1r.at[f], sem.at[0, f], sem.at[1, f], partner)

    def second_xs(f):
        sem, slot = r["xs2_sem"], lax.rem(f, 2)
        return remote(xs2s.at[slot], xs2r.at[f], sem.at[0, slot], sem.at[1, f], partner)

    def along_dp(src, dst, send_sem, recv_sem, other):
        return pltpu.make_async_remote_copy(
            src_ref=src,
            dst_ref=dst,
            send_sem=send_sem,
            recv_sem=recv_sem,
            device_id={"dp": other},
            device_id_type=MESH,
        )

    def chunk_cols(i):
        return pl.ds(pl.multiple_of(i * chunk, chunk), chunk)

    def across(kind, i):
        k = kinds[kind]
        return along_dp(
            sources[kind].at[:, 1 - side, :, chunk_cols(i)],
            buf1.at[k, i],
            r["across_sem"].at[0, k, i],
            r["across_sem"].at[1, k, i],
            line * 2 + 1 - side,
        )

    def along(kind, i, j):
        k = kinds[kind]
        to = lax.rem(line + 1 + j, lines)
        return along_dp(
            buf1.at[k, i, to],
            buf2.at[k, i, j],
            r["along_sem"].at[0, k, i, j],
            r["along_sem"].at[1, k, i, j],
            to * 2 + side,
        )

    def reduce_side(kind, i):
        k = kinds[kind]
        across(kind, i).wait_recv()
        mine = sources[kind][:, side, :, chunk_cols(i)]
        buf1[k, i] = (mine.astype(F32) + buf1[k, i].astype(F32)).astype(BF16)
        loop(lines - 1, lambda j: along(kind, i, j).start())

    def reduce_line(kind, i):
        k = kinds[kind]
        loop(lines - 1, lambda j: along(kind, i, j).wait_recv())
        return buf1[k, i, line].astype(F32) + jnp.sum(buf2[k, i].astype(F32), axis=0)

    def take_up(phase, f):
        for (when, step), sums in plan.items():
            if when != phase:
                continue

            @pl.when(f == step)
            def _(sums=sums):
                for kind, i in sums:
                    reduce_side(kind, i)

    def drain_sums(kind, count):
        def some(i):
            if kind != "carry":
                across(kind, i).wait_send()
            loop(lines - 1, lambda j: along(kind, i, j).wait_send())

        loop(count, some)

    for copy in loads[4:]:
        copy.start()
    for which in for_mlp:
        fetch(which, 0).start()
    for copy in loads[:4]:
        copy.start()

    barrier = pltpu.get_barrier_semaphore()
    for other in (sibling, partner):
        pl.semaphore_signal(barrier, inc=1, device_id={"mp": other}, device_id_type=MESH)

    def greet_dp(j):
        pl.semaphore_signal(
            barrier, inc=1, device_id={"dp": lax.rem(here + 1 + j, size)}, device_id_type=MESH
        )

    loop(size - 1, greet_dp)
    pl.semaphore_wait(barrier, 1 + size)

    def top(f):
        gm[f, own] = (mod[5:6] * grad[f]).astype(BF16)
        share(gm, r["gm_sem"], f, own).start()

    loads[4].wait()
    if last:
        loads[6].wait()
    else:
        loop(windows, top)
    loads[5].wait()
    loop(carry_chunks, lambda i: across("carry", i).start())
    msum[...] = jnp.zeros_like(msum)
    gbias[...] = jnp.zeros_like(gbias)
    wgrad[...] = jnp.zeros_like(wgrad)

    lane_head = lax.div(lax.broadcasted_iota(jnp.int32, (width, inner), 1), head_dim)
    zero = jnp.zeros((), BF16)

    def flat(weight):
        value = weight[...]
        return value.reshape(-1, value.shape[-1])

    def mlp_back(f):
        slot = lax.rem(f, 2)
        for which in for_mlp:
            fetch(which, f).wait()
        if not last:

            @pl.when(f == 0)
            def _():
                share(gm, r["gm_sem"], f, theirs).wait_recv()

        gh[...] = (dot_nt(gm[f], flat(fc2_w)) * r["dg_v"][slot].astype(F32)).astype(BF16)

        @pl.when(f >= 2)
        def _():
            first_ps(f - 2).wait_send()

        ps1s[slot] = dot_nt(gh[theirs], flat(fc1_w)).astype(BF16)
        first_ps(f).start()
        part1[...] = dot_nt(gh[own], flat(fc1_w))

    def sum_first(f):
        slot = lax.rem(f, 2)
        first_ps(f).wait_recv()
        xs1s[f] = (part1[...] + ps1r[slot].astype(F32)).astype(BF16)
        first_xs(f).start()

    def fc2_weights():
        loop(windows - 1, lambda f: share(gm, r["gm_sem"], f + 1, theirs).wait_recv())
        loads[6].wait()
        grads, acts = gm[...].reshape(-1, model), r["act_v"][...].reshape(-1, hidden)
        out = r["fc2_grad"]
        for i in range(fc_chunks):
            c = slice(i * chunk, (i + 1) * chunk)
            out[..., c] = dot_tn(grads, acts[:, c]).astype(BF16).reshape(*out.shape[:-1], chunk)
            across("fc2", i).start()

    def mlp_weights(f):
        slot = lax.rem(f, 2)
        for start in range(0, hidden, 512):
            c = pl.ds(start, 512)
            wgrad[:, c] += dot_tn(r["h2_v"][slot], gh[:, c])

    def fold(values):
        return values.reshape(half // 8, 8, model).sum(axis=0)

    def middle(f):
        slot = lax.rem(f, 2)
        for which in for_middle:
            fetch(which, f).wait()
        first_xs(f).wait_recv()
        grad_h = xs1s[f].astype(F32) + xs1r[f].astype(F32)
        normed, inv = norm(r["x1_v"][slot])
        gy = grad[f]
        grad_mid = gy + norm_back(normed, inv, grad_h * (1.0 + mod[4:5]))
        msum[2] += fold(grad_mid * r["ao_v"][slot].astype(F32))
        msum[3] += fold(grad_h)
        msum[4] += fold(grad_h * normed)
        msum[5] += fold(gy * r["mo_v"][slot].astype(F32))
        grad[f] = grad_mid
        ga[f, own] = (mod[2:3] * grad_mid).astype(BF16)
        share(ga, r["ga_sem"], f, own).start()

    def attention_back(f):
        slot = lax.rem(f, 2)
        qkv = r["qkv_s_v"]
        for which in for_attention:
            fetch(which, f).wait()
        share(ga, r["ga_sem"], f, theirs).wait_recv()
        grad_att = dot_nt(ga[f], proj_w[...]).astype(BF16)
        grad_att_t = grad_att.T
        queries_t = qkv[slot, :, :inner].T
        keys = qkv[slot, :, inner : 2 * inner] * BF16(scale)
        vals = qkv[slot, :, 2 * inner :]
        grad_q = jnp.zeros((width, inner), F32)
        grad_k, grad_v = [], []
        for h in range(heads):
            part = slice(h * head_dim, (h + 1) * head_dim)
            p = r["prob_v"][slot, h]
            grad_p = dot_nt(jnp.where(lane_head == h, grad_att, zero), vals)
            pf = p.astype(F32)
            weighted = pf * grad_p
            grad_s = weighted - pf * jnp.sum(weighted, axis=-1, keepdims=True)
            gbias[h, :, :width] += grad_s
            rounded = grad_s.astype(BF16)
            grad_q = grad_q + dot(rounded, jnp.where(lane_head == h, keys, zero))
            grad_v.append(dot(grad_att_t[part], p))
            grad_k.append(dot(queries_t[part], rounded) * scale)
        gqkv[:, :inner] = grad_q.astype(BF16)
        gqkv[:, inner : 2 * inner] = jnp.concatenate(grad_k, axis=0).astype(BF16).T
        gqkv[:, 2 * inner :] = jnp.concatenate(grad_v, axis=0).astype(BF16).T

        @pl.when(f >= 2)
        def _():
            second_ps(f - 2).wait_send()

        ps2s[slot] = dot_nt(gqkv[theirs], qkv_w[...]).astype(BF16)
        second_ps(f).start()
        part2[...] = dot_nt(gqkv[own], qkv_w[...])

    def sum_second(f):
        slot = lax.rem(f, 2)
        second_ps(f).wait_recv()

        @pl.when(f >= 2)
        def _():
            second_xs(f - 2).wait_send()

        xs2s[slot] = (part2[...] + ps2r[slot].astype(F32)).astype(BF16)
        second_xs(f).start()

    def attention_weights(f):
        slot = lax.rem(f, 2)
        for start in range(0, 3 * inner, 384):
            c = pl.ds(start, 384)
            wgrad[:, c] += dot_tn(r["h1_v"][slot], gqkv[:, c])
        wgrad[:, 3 * inner : 4 * inner] += dot_tn(ga[f], r["att_v"][slot])

    def finish(f):
        slot = lax.rem(f, 2)
        fetch("stream", f).wait()
        second_xs(f).wait_recv()
        grad_h = xs2s[slot].astype(F32) + xs2r[f].astype(F32)
        normed, inv = norm(r["stream_v"][slot].astype(F32).reshape(half, model))
        msum[0] += fold(grad_h)
        msum[1] += fold(grad_h * normed)
        grad_x = grad[f] + norm_back(normed, inv, grad_h * (1.0 + mod[1:2]))
        if last:
            store_b_to_a(r["gx"], f, grad_x)
        else:
            grad[f] = grad_x

    def first_step(f):
        @pl.when(f + 1 < windows)
        def _():
            for which in for_mlp:
                fetch(which, f + 1).start()

        @pl.when(f == 0)
        def _():
            loads[0].wait()
            loads[1].wait()

        mlp_back(f)
        sum_first(f)
        if not last:
            pl.when(f == 0)(fc2_weights)
        mlp_weights(f)
        take_up(0, f)

    loop(windows, first_step)

    for which in (*for_attention, *for_middle, "stream"):
        fetch(which, 0).start()
    shape = fc1_w.shape
    fc1_w[...] = wgrad[:, :hidden].astype(BF16).reshape(shape)
    loop(fc_chunks, lambda i: across("fc1", i).start())
    wgrad[:, : 4 * inner] = jnp.zeros((model, 4 * inner), F32)
    for which in for_middle:
        fetch(which, 1).start()
    middle(0)
    loads[2].wait()
    loads[3].wait()

    def second_step(f):
        @pl.when(f + 1 < windows)
        def _():
            for which in for_attention:
                fetch(which, f + 1).start()
            middle(f + 1)

        @pl.when(f + 2 < windows)
        def _():
            for which in for_middle:
                fetch(which, f + 2).start()

        attention_back(f)
        sum_second(f)
        attention_weights(f)

        @pl.when(f >= 1)
        def _():
            finish(f - 1)

        @pl.when((f >= 1) & (f + 1 < windows))
        def _():
            fetch("stream", f + 1).start()

        @pl.when(f == 0)
        def _():
            fetch("stream", 1).start()

        take_up(1, f)

    loop(windows, second_step)

    loop(carry_chunks, lambda i: across("carry", i).wait_send())
    rest[...] = wgrad[:, : 4 * inner].astype(BF16).reshape(rest.shape)
    loop(early_chunks, lambda i: across("rest", i).start())
    if last:
        later = pl.ds(early_chunks * chunk, (rest_chunks - early_chunks) * chunk)
        carry = pltpu.make_async_copy(rest.at[..., later], r["carry_next"], r["w_sem"].at[5])
        carry.start()
    else:
        wide = r["gbias_b"].shape[2]
        tall = r["gbias_b"].shape[1]

        def other_place(h):
            return pl.ds(h // 2 * tall, tall), pl.ds(h % 2 * wide, wide)

        other_loads = []
        for h in range(heads):
            other_loads.append(
                pltpu.make_async_copy(
                    r["gbias_b"].at[h], wgrad.at[other_place(h)], r["other_sem"].at[h]
                )
            )
            other_loads[-1].start()
    take_up(2, 0)
    finish(windows - 1)
    for i in range(12):
        c = slice(i % 2 * 512, i % 2 * 512 + 512)
        mtot[i // 3, pl.ds(i % 3, 1)] = jnp.sum(msum[i // 2, :, c], axis=0, keepdims=True)
    mod_copy = remote(mtot, mrecv, r["mod_sem"].at[0], r["mod_sem"].at[1], sibling)
    mod_copy.start()
    small, everyone, tabs = r.get("small"), r.get("everyone"), r.get("tabs")

    def give_small(j):
        return along_dp(
            small,
            everyone.at[here],
            r["small_sem"].at[0, j],
            r["small_sem"].at[1, j],
            lax.rem(here + 1 + j, size),
        )

    def give_table(j):
        to = lax.rem(here + 1 + j, size)
        sem = r["table_sem"]
        return along_dp(tabs.at[to], r["tab_parts"].at[j], sem.at[0, j], sem.at[1, j], to)

    def give_sum(j):
        to = lax.rem(here + 1 + j, size)
        sem = r["sum_sem"]
        return along_dp(r["tab_sum"], r["tables"].at[here], sem.at[0, j], sem.at[1, j], to)

    def start_mods():
        mod_copy.wait()
        me = lax.axis_index("mp")
        small[0:3] = mtot[me] + mrecv[me]
        small[3:6] = r["mod_b"][...]
        small[6:8] = r["cond"][...]
        everyone[here] = small[...]
        loop(size - 1, lambda j: give_small(j).start())

    def start_tables():
        each = tabs.shape[1]
        mine, other = r["table"], r["table_b"]
        for i in range(size):
            piece = slice(i * each, (i + 1) * each)
            tabs[i, :, : mine.shape[1]] = mine[piece]
            tabs[i, :, mine.shape[1] : mine.shape[1] + other.shape[1]] = other[piece]
        loop(size - 1, lambda j: give_table(j).start())

    def finish_tables():
        loop(size - 1, lambda j: give_table(j).wait_recv())
        total = tabs[here] + jnp.sum(r["tab_parts"][...], axis=0)
        r["tab_sum"][...] = total
        r["tables"][here] = total
        loop(size - 1, lambda j: give_sum(j).start())

    def finish_sums():
        for give in (give_small, give_sum):
            loop(size - 1, lambda j, give=give: give(j).wait_recv())
        for give in (give_small, give_table, give_sum):
            loop(size - 1, lambda j, give=give: give(j).wait_send())

    hands = []
    if not last:
        gx = r["gx"]

        def group(j):
            which = 5 * x + j
            rows = pl.ds(pl.multiple_of(lax.rem(which, 2) * 64, 64), 64)
            return lax.div(which, 2), rows

        for i in range(2):
            f, rows = group(3 - 3 * core + i)
            hands.append(
                remote(
                    grad.at[f, rows],
                    gx.at[1 + 2 * i],
                    r["hand_sem"].at[0, i],
                    r["hand_sem"].at[1, i],
                    sibling,
                )
            )
            hands[-1].start()
        for i in range(3):
            f, rows = group(2 * core + i)
            gx[2 * i] = grad[f, rows]

    if last:
        for i in range(early_chunks):
            reduce_side("rest", i)
    else:
        start_mods()
        mine = [gbias.at[h] for h in range(heads)]
        other = [wgrad.at[other_place(h)] for h in range(heads)]
        scatter(index, mine, r["table"])
        reduce_side("rest", 0)
        for copy in other_loads:
            copy.wait()
        for i in range(4):
            scatter(r["index_b"], other, r["table_b"], i, 4)
            if i < 3:
                reduce_side("rest", i + 1)
        start_tables()
    outputs = [("carry", carry_chunks), ("fc1", fc_chunks), ("rest", early_chunks)]
    if not last:
        outputs.insert(1, ("fc2", fc_chunks))
    for kind, count in outputs:
        out = r[kind + "_out"]

        def finish_chunk(i, kind=kind, out=out):
            out[:, chunk_cols(i)] = reduce_line(kind, i)

        if kind == "rest" and not last:
            finish_tables()
        loop(count, finish_chunk)
    if last:
        carry.wait()
        mod_copy.wait()
        me = lax.axis_index("mp")
        r["mod_out"][...] = mtot[me] + mrecv[me]
    else:
        finish_sums()
    for copy in hands:
        copy.wait()

    def drain(f):
        if not last:
            share(gm, r["gm_sem"], f, own).wait_send()
        share(ga, r["ga_sem"], f, own).wait_send()
        first_xs(f).wait_send()

    loop(windows, drain)
    for f in range(windows - 2, windows):
        for copy in (first_ps(f), second_ps(f), second_xs(f)):
            copy.wait_send()

    for kind, count in outputs:
        drain_sums(kind, count)


def block_backward(
    stream, grad_y, mod, params, kept, index, table_lens, carry, sums, size, collective_id
):
    last = "gm" in kept
    qkv_w, proj_w, fc1_w, fc2_w = params
    windows, half, model = kept["x1"].shape
    width = 2 * half
    heads = kept["prob"].shape[1]
    inner = proj_w.shape[0]
    hidden = fc1_w.shape[1]
    rows = model // size
    lines = size // 2
    chunk = 256
    chunks = max(hidden, 4 * inner) // chunk
    kinds = 3 if last else 4
    groups = [(count + 127) // 128 for count in table_lens]
    sds = jax.ShapeDtypeStruct
    sliced = (lines, 2, rows)
    cut = (*sliced, hidden)

    ins, outs, scratch = {}, {}, {}
    ins["grad_y"] = (grad_y, ANY)
    ins["mod"] = (mod, VM)
    if not last:
        ins["index"] = (index, VM)
    for name in STREAMS:
        value = stream if name == "stream" else kept[name]
        ins[name] = (value, ANY)
        scratch[name + "_v"] = pltpu.VMEM((2,) + value.shape[1:], value.dtype)
    ins["qkv"] = (qkv_w, ANY)
    ins["proj"] = (proj_w, ANY)
    ins["fc1"] = (fc1_w.reshape(cut), ANY)
    ins["fc2"] = (fc2_w.reshape(cut), ANY)
    ins["carry"] = (carry, ANY)
    if last:
        ins["gm_s"] = (kept["gm"], ANY)
        outs["gx"] = (sds((2 * FRAMES, 4, 2, 8, model), F32), VM)
        outs["carry_next"] = (sds((*sliced, 2 * inner), BF16), ANY)
        outs["rest_out"] = (sds((rows, 2 * inner), F32), VM)
        outs["gbias"] = (sds((heads, *index.shape), F32), VM)
    else:
        ins["act"] = (kept["act"], ANY)
        scratch["act_v"] = pltpu.VMEM(kept["act"].shape, BF16)
        scratch["fc2_grad"] = pltpu.VMEM(cut, BF16)
        scratch["gbias"] = pltpu.VMEM((heads, *index.shape), F32)
        outs["gx"] = (sds((FRAMES, 4 * SIDE, model), F32), VM)
        outs["rest_out"] = (sds((rows, 4 * inner), F32), VM)
        outs["fc2_out"] = (sds((rows, hidden), F32), VM)
    outs["carry_out"] = (sds((rows, carry.shape[-1]), F32), VM)
    outs["fc1_out"] = (sds((rows, hidden), F32), VM)
    if last:
        outs["mod_out"] = (sds((3, 512), F32), VM)
    else:
        each = 128 // size
        names = ("mod_b", "cond", "index_b")
        ins.update({name: (v, VM) for name, v in zip(names, sums[:3], strict=True)})
        ins["gbias_b"] = (sums[3], ANY)
        outs["everyone"] = (sds((size, 8, 512), F32), VM)
        outs["tables"] = (sds((size, each, 128), F32), VM)
        scratch.update(
            table=pltpu.VMEM((128, heads * groups[0]), F32),
            table_b=pltpu.VMEM((128, heads * groups[1]), F32),
            other_sem=dma((heads,)),
            small=pltpu.VMEM((8, 512), F32),
            tabs=pltpu.VMEM((size, each, 128), F32),
            tab_parts=pltpu.VMEM((size - 1, each, 128), F32),
            tab_sum=pltpu.VMEM((each, 128), F32),
            small_sem=dma((2, size - 1)),
            table_sem=dma((2, size - 1)),
            sum_sem=dma((2, size - 1)),
        )

    own_all = pltpu.VMEM((windows, half, model), BF16)
    own_two = pltpu.VMEM((2, half, model), BF16)
    own_one = pltpu.VMEM((half, model), F32)
    every = pltpu.VMEM((windows, width, model), BF16)
    scratch.update(
        grad=pltpu.VMEM((windows, half, model), F32),
        part1=own_one,
        part2=own_one,
        gh=pltpu.VMEM((width, hidden), BF16),
        gqkv=pltpu.VMEM((width, 3 * inner), BF16),
        fc1_w=pltpu.VMEM(cut, BF16),
        fc2_w=pltpu.VMEM(cut, BF16),
        qkv_w=pltpu.VMEM(qkv_w.shape, BF16),
        proj_w=pltpu.VMEM(proj_w.shape, BF16),
        gm=every,
        ga=every,
        rest=pltpu.VMEM((*sliced, 4 * inner), BF16),
        wgrad=pltpu.VMEM((model, max(4 * inner, hidden)), F32),
        ps1s=own_two,
        ps1r=own_two,
        ps2s=own_two,
        ps2r=own_two,
        xs1s=own_all,
        xs2s=own_two,
        xs1r=own_all,
        xs2r=own_all,
        buf1=pltpu.VMEM((kinds, chunks, lines, rows, chunk), BF16),
        buf2=pltpu.VMEM((kinds, chunks, lines - 1, rows, chunk), BF16),
        msum=pltpu.VMEM((6, 8, model), F32),
        mtot=pltpu.VMEM((4, 3, 512), F32),
        mrecv=pltpu.VMEM((4, 3, 512), F32),
        w_sem=dma((7,)),
        in_sem=dma((11, 2)),
        gm_sem=dma((2, windows)),
        ga_sem=dma((2, windows)),
        ps1_sem=dma((2, 2)),
        ps2_sem=dma((2, 2)),
        xs1_sem=dma((2, windows)),
        xs2_sem=dma((2, windows)),
        hand_sem=dma((2, 2)),
        mod_sem=dma((2,)),
        across_sem=dma((2, kinds, chunks)),
        along_sem=dma((2, kinds, chunks, lines - 1)),
    )
    names = (*ins, *outs, *scratch)
    results = pl.pallas_call(
        functools.partial(backward_kernel, windows, last, size, names),
        out_shape=[shape for shape, _ in outs.values()],
        in_specs=[spec for _, spec in ins.values()],
        out_specs=[spec for _, spec in outs.values()],
        scratch_shapes=list(scratch.values()),
        compiler_params=pltpu.CompilerParams(
            collective_id=collective_id, has_side_effects=True, vmem_limit_bytes=VMEM_LIMIT
        ),
        name="backward_last" if last else "backward_first",
    )(*[value for value, _ in ins.values()])
    return dict(zip(outs, results, strict=True))


def lookup(index, table, out, r):
    heads, groups = table.shape[0], table.shape[1]
    for block in range(index.shape[1] // 128):
        c = pl.ds(block * 128, 128)
        row = index[r, c]
        low = row & 127
        high = row >> 7
        found = [jnp.zeros((16, 128), F32) for _ in range(heads)]
        for g in range(groups):
            here = high == g
            for h in range(heads):
                spread = jnp.broadcast_to(table[h, pl.ds(g, 1), :], (16, 128))
                taken = jnp.take_along_axis(spread, low, axis=1, mode="promise_in_bounds")
                found[h] = jnp.where(here, taken, found[h])
        for h in range(heads):
            out[h, r, c] = found[h].astype(BF16)


def lane_table(table):
    rows, heads = table.shape
    groups = (rows + 127) // 128
    spread = jnp.pad(table.astype(F32), ((0, groups * 128 - rows), (0, 0))).T
    return spread.reshape(heads, groups, 128)


def scatter(index, grad, out, part=0, parts=1):
    heads = len(grad)
    groups = out.shape[1] // heads
    rows, width = index.shape
    if part == 0:
        out[...] = jnp.zeros_like(out)
    count = rows // 8 // parts
    low_rows = lax.broadcasted_iota(jnp.int32, (128, width), 0)
    high_rows = lax.broadcasted_iota(jnp.int32, (groups, width), 0)

    def some(i):
        r = pl.ds(pl.multiple_of((part * count + i) * 8, 8), 8)
        index_rows = index[r, :]
        low = index_rows & 127
        high = index_rows >> 7
        grads = [g[r, :] for g in grad]
        total = out[...]
        for i in range(8):
            onehot = jnp.where(low_rows == low[i : i + 1], 1.0, 0.0).astype(BF16)
            here = high_rows == high[i : i + 1]
            placed = jnp.concatenate(
                [jnp.where(here, g[i : i + 1], 0.0) for g in grads], axis=0
            ).astype(BF16)
            total = total + dot_nt(onehot, placed)
        out[...] = total

    loop(count, some)


def place_index(index, layout):
    if layout == 0:
        cut, order, pad = (2, 2, 64), (1, 0, 2), 0
    else:
        cut, order, pad = (FRAMES, 2, 32), (1, 0, 2), 64
    side = index.shape[0]
    both = index.reshape(cut + cut)
    both = both.transpose(order + tuple(3 + o for o in order)).reshape(side, side)
    return jnp.pad(both, ((0, 0), (0, pad)), constant_values=-1)


def local(
    tokens,
    cond,
    pad_mask,
    spatial_index,
    joint_index,
    qkv_a,
    proj_a,
    fc1_a,
    fc2_a,
    table_a,
    ada_a,
    qkv_b,
    proj_b,
    fc1_b,
    fc2_b,
    table_b,
    ada_b,
    cotangent,
    dp_size,
    mp_size,
):
    model = tokens.shape[1]
    inner = proj_a.shape[0]
    params_a = (qkv_a.reshape(model, -1), proj_a, fc1_a, fc2_a)
    params_b = (qkv_b.reshape(model, -1), proj_b, fc1_b, fc2_b)

    cond_act = lax.optimization_barrier(jax.nn.silu(cond.astype(F32)).astype(BF16))
    parts = jnp.concatenate(
        [jnp.dot(cond_act, ada, preferred_element_type=F32) for ada in (ada_a, ada_b)], axis=0
    ).reshape(2, 3, 512)

    index_a = place_index(spatial_index, 0)
    index_b = place_index(joint_index, 1)
    hidden_keys = jnp.where(pad_mask.reshape(-1) > 0, 0.0, -1e30).astype(F32)
    mask_a = hidden_keys.reshape(FRAMES, 2, 2, 64).transpose(0, 2, 1, 3).reshape(FRAMES, 1, -1)
    mask_b = hidden_keys.reshape(FRAMES, 2, 2, 4, 2, 8).transpose(1, 4, 2, 0, 3, 5)
    mask_b = mask_b.reshape(4, 1, -1)
    groups = (FRAMES, 4 * SIDE, model)

    first = (parts, index_a, lane_table(table_a), index_b, lane_table(table_b))
    kept_a = block_forward(tokens.reshape(groups), first, None, params_a, mask_a, dp_size, 1)
    mods = kept_a["mods"]
    x_b = kept_a["y"].reshape(4, -1, model)
    then = (x_b, mods[1], kept_a["next_bias"])
    kept_b = block_forward(cotangent.reshape(groups), None, then, params_b, mask_b, dp_size, 2)
    back_b = block_backward(
        x_b,
        kept_b["top"].reshape(x_b.shape),
        mods[1],
        params_b,
        kept_b,
        index_b,
        (),
        kept_b["fc2_grad"],
        None,
        dp_size,
        3,
    )
    back_a = block_backward(
        kept_a["stream_s"],
        back_b["gx"].reshape(FRAMES, -1, model),
        mods[0],
        params_a,
        kept_a,
        index_a,
        (table_a.shape[0], table_b.shape[0]),
        back_b["carry_next"],
        (back_b["mod_out"], cond_act.astype(F32).reshape(2, 512), index_b, back_b["gbias"]),
        dp_size,
        4,
    )
    everyone = back_a["everyone"]
    cols_a = everyone[:, 0:3].reshape(dp_size, -1)
    cols_b = everyone[:, 3:6].reshape(dp_size, -1)
    conds = everyone[:, 6:8].reshape(dp_size, model)
    rows_here = model // dp_size
    my_conds = lax.dynamic_slice_in_dim(conds, lax.axis_index("dp") * rows_here, rows_here, axis=1)
    tables = back_a["tables"].reshape(128, 128)

    rest_b = jnp.concatenate([back_b["rest_out"], back_a["carry_out"]], axis=1)

    def outer(columns):
        return jnp.einsum("td,tc->dc", my_conds, columns, precision=HIGHEST)

    def table(start, like):
        length, heads = like.shape
        count = (length + 127) // 128
        columns = tables[:, start : start + heads * count].reshape(128, heads, count)
        return columns.transpose(2, 0, 1).reshape(-1, heads)[:length]

    def split(rest, fc1, fc2):
        return (
            rest[:, : 3 * inner].reshape(rows_here, 3, inner),
            rest[:, 3 * inner :].T,
            fc1,
            fc2.T,
        )

    return (
        kept_b["y"].reshape(tokens.shape),
        back_a["gx"].reshape(tokens.shape),
        *split(back_a["rest_out"], back_a["fc1_out"], back_a["fc2_out"]),
        table(0, table_a),
        outer(cols_a),
        *split(rest_b, back_b["fc1_out"], back_b["carry_out"]),
        table(table_a.shape[1] * ((table_a.shape[0] + 127) // 128), table_b),
        outer(cols_b),
    )


def solution(mesh):
    in_specs = (
        P(("dp", "mp"), None),
        P("dp", None),
        P("dp", None),
        P(),
        P(),
        P(None, None, "mp"),
        P("mp", None),
        P(None, "mp"),
        P("mp", None),
        P(None, "mp"),
        P(None, "mp"),
        P(None, None, "mp"),
        P("mp", None),
        P(None, "mp"),
        P("mp", None),
        P(None, "mp"),
        P(None, "mp"),
        P(("dp", "mp"), None),
    )
    out_specs = (
        P(("dp", "mp"), None),
        P(("dp", "mp"), None),
        P("dp", None, "mp"),
        P("mp", "dp"),
        P("dp", "mp"),
        P("mp", "dp"),
        P(None, "mp"),
        P("dp", "mp"),
        P("dp", None, "mp"),
        P("mp", "dp"),
        P("dp", "mp"),
        P("mp", "dp"),
        P(None, "mp"),
        P("dp", "mp"),
    )
    body = functools.partial(local, dp_size=mesh.shape["dp"], mp_size=mesh.shape["mp"])
    return jax.shard_map(body, mesh=mesh, in_specs=in_specs, out_specs=out_specs, check_vma=False)
```

```python
import functools

import jax
import jax.numpy as jnp
from jax import lax
from jax.experimental import pallas as pl
from jax.experimental.pallas import tpu as pltpu
from jax.sharding import PartitionSpec as P

FRAMES = 5
SIDE = 16
EPSILON = 1e-06
HIGHEST = lax.Precision.HIGHEST
MESH = pl.DeviceIdType.MESH
F32 = jnp.float32
BF16 = jnp.bfloat16
VMEM_LIMIT = 60 << 20
GELU_K = 0.7978845608028654
GELU_C = 0.044715
ANY = pl.BlockSpec(memory_space=pl.ANY)
VM = pl.BlockSpec(memory_space=pltpu.VMEM)


def own_rows(src, dst, sems, x, core, sibling, partner, diagonal):
    sends, local, recvs = sems

    def place(j):
        return dst.at[lax.div(j, 2), lax.rem(j, 2)]

    def moves():
        found = []
        for k in range(5):
            j = 5 * x + lax.div(5 * core + k, 2)
            to = (partner,) if k % 2 == 0 else (diagonal, sibling)
            for i, other in enumerate(to):
                found.append(remote(src.at[k], place(j), sends.at[k, i], recvs.at[j], other))
            if k % 2 == 0:
                found.append(pltpu.make_async_copy(src.at[k], place(j), local.at[k // 2]))
        return found

    def start():
        for copy in moves():
            copy.start()

    def wait(j):
        row = 2 * j + core
        k = lax.rem(row, 5)
        here = (lax.div(row, 10) == x) & (lax.div(lax.rem(row, 10), 5) == core)

        @pl.when(here)
        def _():
            pltpu.make_async_copy(src.at[k], place(j), local.at[lax.div(k, 2)]).wait()

        @pl.when(jnp.logical_not(here))
        def _():
            remote(src.at[0], place(j), sends.at[0, 0], recvs.at[j], partner).wait_recv()

    def drain():
        for k in range(5):
            for i in range(1 if k % 2 == 0 else 2):
                remote(src.at[k], place(0), sends.at[k, i], recvs.at[0], partner).wait_send()

    return start, wait, drain


def qkv_copies(src, dst, sems):
    inner = src.shape[2]
    return [
        pltpu.make_async_copy(src.at[i], dst.at[:, pl.ds(i * inner, inner)], sems.at[i])
        for i in range(3)
    ]


def index_copies(r):
    copies = []
    for name, size, count in (("spatial", 64, 2), ("joint", 32, FRAMES)):
        dst = r["index_v" if name == "spatial" else "next_index_v"]
        for outer in range(count):
            for owner in range(2):
                copies.append(
                    pltpu.make_async_copy(
                        r[name].at[pl.ds((outer * 2 + owner) * size, size)],
                        dst.at[pl.ds((owner * count + outer) * size, size)],
                        r["index_sem"].at[len(copies)],
                    )
                )
    return copies


def place_index(src, dst, shift, count):
    width, wide = src.shape[1], dst.shape[1]
    lane = lax.broadcasted_iota(jnp.int32, (width, wide), 1)
    group = lane >> shift
    owner = (group >= count).astype(jnp.int32)
    origin = (((group - owner * count) * 2 + owner) << shift) + (lane & ((1 << shift) - 1))
    moved = lax.broadcasted_iota(jnp.int32, (width, wide), 0) == origin
    order = jnp.where(moved & (lane < width), 1.0, 0.0).astype(BF16)
    values = src[...]
    low = dot((values & 127).astype(F32).astype(BF16), order)
    high = dot((values >> 7).astype(F32).astype(BF16), order)
    placed = (low + 128.0 * high).astype(jnp.int32)
    dst[...] = jnp.where(lax.broadcasted_iota(jnp.int32, dst.shape, 1) < width, placed, -1)


def lane_table(src, dst):
    heads, rows = src.shape
    dst[...] = jnp.zeros_like(dst)
    values = src[...].astype(F32)
    for g in range(dst.shape[1]):
        count = min(128, rows - g * 128)
        for h in range(heads):
            dst[h, pl.ds(g, 1), pl.ds(0, count)] = values[h : h + 1, g * 128 : g * 128 + count]


def dma(shape):
    return pltpu.SemaphoreType.DMA(shape)


def places():
    me = lax.axis_index("mp")
    x = lax.div(me, 2)
    core = lax.rem(me, 2)
    return x, core, x * 2 + 1 - core, (1 - x) * 2 + core, (1 - x) * 2 + 1 - core


def greet(others):
    barrier = pltpu.get_barrier_semaphore()
    for other in others:
        pl.semaphore_signal(barrier, inc=1, device_id={"mp": other}, device_id_type=MESH)
    pl.semaphore_wait(barrier, len(others))


def remote(src, dst, send_sem, recv_sem, other):
    return pltpu.make_async_remote_copy(
        src_ref=src,
        dst_ref=dst,
        send_sem=send_sem,
        recv_sem=recv_sem,
        device_id={"mp": other},
        device_id_type=MESH,
    )


def loop(count, body):
    def step(i, _):
        body(i)
        return 0

    lax.fori_loop(0, count, step, 0)


def rows16(count, body, step=16):
    loop(count // step, lambda i: body(pl.ds(pl.multiple_of(i * step, step), step)))


def norm(values):
    centred = values - jnp.mean(values, axis=-1, keepdims=True)
    inv = lax.rsqrt(jnp.mean(centred * centred, axis=-1, keepdims=True) + EPSILON)
    return centred * inv, inv


def norm_back(normed, inv, grad):
    mean_g = jnp.mean(grad, axis=-1, keepdims=True)
    mean_gn = jnp.mean(grad * normed, axis=-1, keepdims=True)
    return (grad - mean_g - normed * mean_gn) * inv


def dot(a, b):
    return jnp.dot(a, b, preferred_element_type=F32)


def dot_nt(a, b):
    return lax.dot_general(a, b, (((1,), (1,)), ((), ())), preferred_element_type=F32)


def dot_tn(a, b):
    return lax.dot_general(a, b, (((0,), (0,)), ((), ())), preferred_element_type=F32)


def store_a_to_b(dst, frame, value):
    shaped = value.reshape(2, 4, 2, 8, value.shape[-1])
    for qr in range(2):
        for qc in range(2):
            dst[qr * 2 + qc, pl.ds(pl.multiple_of(frame * 4, 4), 4)] = shaped[qr, :, qc]


def store_b_to_a(dst, window, value):
    shaped = value.reshape(FRAMES, 4, 8, value.shape[-1])
    qr, qc = lax.div(window, 2), lax.rem(window, 2)
    for frame in range(FRAMES):
        dst[frame * 2 + qr, :, qc] = shaped[frame]


def store_a_to_a(dst, frame, value):
    shaped = value.reshape(2, 4, 2, 8, value.shape[-1])
    for qr in range(2):
        dst[frame * 2 + qr] = shaped[qr]


def hand_out(groups, out, send_sem, recv_sem, x, core, sibling):
    copies = []
    for i in range(2):
        copies.append(
            remote(
                groups.at[5 * x + 3 - 3 * core + i],
                out.at[1 + 2 * i],
                send_sem.at[i],
                recv_sem.at[i],
                sibling,
            )
        )
        copies[-1].start()
    for i in range(3):
        out[2 * i] = groups[5 * x + 2 * core + i]
    for copy in copies:
        copy.wait()


def forward_kernel(windows, last, names, *refs):
    r = dict(zip(names, refs, strict=True))
    stream, mask, bias, y_out = r["stream"], r["mask"], r["bias"], r["y"]
    mod = r["mod"].at[1] if last else r["mods"].at[0]
    qkv_w, proj_w, fc1_w, fc2_w = r["qkv_w"], r["proj_w"], r["fc1_w"], r["fc2_w"]
    h1, qkv, prob, att, ao = r["h1_v"], r["qkv_s_v"], r["prob_v"], r["att_v"], r["ao_v"]
    x1, h2, act, dg, mo = r["x1_v"], r["h2_v"], r["act_v"], r["dg_v"], r["mo_v"]
    ps1s, ps1r, ps2s, ps2r = r["ps1s"], r["ps1r"], r["ps2s"], r["ps2r"]
    xs1s, xs1r, xs2s, xs2r = r["xs1s"], r["xs1r"], r["xs2s"], r["xs2r"]
    part1, part2, out_sem = r["part1"], r["part2"], r["out_sem"]
    h1_sem, h2_sem, ps1_sem, ps2_sem = r["h1_sem"], r["h2_sem"], r["ps1_sem"], r["ps2_sem"]
    xs1_sem, xs2_sem = r["xs1_sem"], r["xs2_sem"]
    width = h1.shape[1]
    half = width // 2
    model = h1.shape[2]
    heads = bias.shape[0]
    inner = proj_w.shape[0]
    head_dim = inner // heads
    piece = half // FRAMES
    x, core, sibling, partner, diagonal = places()
    own = pl.ds(pl.multiple_of(core * half, 16), half)
    theirs = pl.ds(pl.multiple_of((1 - core) * half, 16), half)

    weights = qkv_copies(r["qkv"], qkv_w, r["qkv_sem"]) + [
        pltpu.make_async_copy(r[name], r[name + "_w"], r["w_sem"].at[i])
        for i, name in enumerate(("proj", "fc1", "fc2"))
    ]
    if not last:
        firsts = index_copies(r) + [
            pltpu.make_async_copy(r["ada_" + b], r["ada_v"].at[i], r["ada_sem"].at[i])
            for i, b in enumerate("ab")
        ]
        for copy in firsts:
            copy.start()
    for copy in weights:
        copy.start()
    saves = [
        (r[name + "_v"], r[name])
        for name in ("h1", "qkv_s", "prob", "att", "ao", "x1", "h2", "act", "dg", "mo")
        + (("gm",) if last else ())
    ]

    def save(which, f):
        src, dst = saves[which]
        return pltpu.make_async_copy(src.at[f], dst.at[f], out_sem.at[which, f])

    def share(buf, sem, f, rows):
        return remote(buf.at[f, own], buf.at[f, rows], sem.at[0, f], sem.at[1, f], sibling)

    def to_sibling(src, dst, sem, f):
        return remote(src.at[f], dst.at[f], sem.at[0, f], sem.at[1, f], sibling)

    def to_partner(src, dst, sem, f):
        return remote(src.at[f], dst.at[f], sem.at[0, f], sem.at[1, f], partner)

    greet((sibling, partner, diagonal))
    rows_start, rows_wait, rows_drain = own_rows(
        r["rows"],
        r["top_rows"] if last else stream,
        (r["rows_send"], r["rows_local"], r["rows_recv"]),
        x,
        core,
        sibling,
        partner,
        diagonal,
    )
    rows_start()
    if not last:
        me = lax.axis_index("mp")
        pieces, mods, parts = r["pieces"], r["mods"], r["parts"]
        cond = r["cond"][...].astype(F32)
        cond_act = (cond / (1.0 + jnp.exp(-cond))).astype(BF16)
        for i in range(2):
            r["cond_act"][pl.ds(i, 1)] = cond_act[:, i * 512 : i * 512 + 512].astype(F32)
        spread = jnp.broadcast_to(cond_act, (16, model))
        for i in range(2):
            firsts[-2 + i].wait()
            product = dot(spread, r["ada_v"][i])
            for j in range(3):
                parts[i, pl.ds(j, 1)] = product[0:1, j * 512 : j * 512 + 512]
        mod_copies = []
        for i in range(3):
            mod_copies.append(
                remote(
                    parts,
                    pieces.at[me],
                    r["mod_sem"].at[0, i],
                    r["mod_sem"].at[1, i],
                    lax.rem(me + 1 + i, 4),
                )
            )
            mod_copies[-1].start()
        pieces[me] = parts[...]
        for copy in firsts[:-2]:
            copy.wait()
        place_index(r["index_v"], r["index"], 6, 2)
        place_index(r["next_index_v"], r["next_index"], 5, FRAMES)
        lane_table(r["table"], r["table_v"])
        lane_table(r["next_table"], r["next_table_v"])
        rows16(width, lambda rows: lookup(r["index"], r["table_v"], bias, rows))
        for copy in mod_copies:
            copy.wait()
        for i in range(12):
            half_row = pl.ds(i % 2 * 512, 512)
            for b in range(2):
                mods[b, pl.ds(i // 2, 1), half_row] = pieces[i // 3, b, pl.ds(i % 3, 1)]

    def own_stream(f):
        return stream[f].astype(F32).reshape(half, model)

    def first_norm(f):
        if not last:
            rows_wait(2 * f)
            rows_wait(2 * f + 1)
            keep_stream(f).start()
        normed, _ = norm(own_stream(f))
        h1[f, own] = (normed * (1.0 + mod[1:2]) + mod[0:1]).astype(BF16)
        share(h1, h1_sem, f, own).start()

    def keep_stream(f):
        return pltpu.make_async_copy(stream.at[f], r["stream_s"].at[f], r["top_sem"].at[f])

    loop(windows if last else 2, first_norm)
    for copy in weights[:4]:
        copy.wait()

    def top():
        def place(f):
            rows_wait(2 * f)
            rows_wait(2 * f + 1)
            store_a_to_b(r["top_v"], f, r["top_rows"][f].astype(F32).reshape(-1, model))

        loop(FRAMES, place)

        def give(f):
            grad = r["top_v"][f].reshape(half, model)
            pltpu.make_async_copy(r["top_v"].at[f], r["top"].at[f], r["top_sem"].at[f]).start()
            r["gm_v"][f, own] = (mod[5:6] * grad).astype(BF16)
            share(r["gm_v"], r["gm_sem"], f, own).start()

        loop(windows, give)

    def top_weights():
        def some(f):
            share(r["gm_v"], r["gm_sem"], f, theirs).wait_recv()
            save(10, f).start()

        loop(windows, some)
        grads, acts = r["gm_v"][...].reshape(-1, model), act[...].reshape(-1, act.shape[2])
        fc2_grad = r["fc2_grad_v"]
        for start in range(0, acts.shape[1], 256):
            c = slice(start, start + 256)
            piece = dot_tn(grads, acts[:, c]).astype(BF16)
            fc2_grad[..., c] = piece.reshape(*fc2_grad.shape[:-1], 256)
        grad_copy().start()

    def grad_copy():
        return pltpu.make_async_copy(r["fc2_grad_v"], r["fc2_grad"], r["w_sem"].at[4])

    lane_head = lax.div(lax.broadcasted_iota(jnp.int32, (width, inner), 1), head_dim)

    def attention(f):
        share(h1, h1_sem, f, theirs).wait_recv()
        save(0, f).start()
        qkv[f] = dot(h1[f], qkv_w[...]).astype(BF16)
        save(1, f).start()
        queries = qkv[f, :, :inner] * BF16(head_dim ** (-0.5))
        keys = qkv[f, :, inner : 2 * inner]
        vals = qkv[f, :, 2 * inner :]
        zero = jnp.zeros((), BF16)
        out = jnp.zeros((width, inner), F32)
        for h in range(heads):
            scores = dot_nt(jnp.where(lane_head == h, queries, zero), keys)
            scores = scores + bias[h, :, :width].astype(F32) + mask[f]
            weight = jnp.exp(scores - jnp.max(scores, axis=-1, keepdims=True))
            p = (weight * (1.0 / jnp.sum(weight, axis=-1, keepdims=True))).astype(BF16)
            prob[f, h] = p
            out = out + dot(p, jnp.where(lane_head == h, vals, zero))
        att[f] = out.astype(BF16)
        save(2, f).start()
        save(3, f).start()

        ps1s[f] = dot(att[f, theirs], proj_w[...]).astype(BF16)
        to_sibling(ps1s, ps1r, ps1_sem, f).start()
        part1[...] = dot(att[f, own], proj_w[...])

    def sum_first(f):
        to_sibling(ps1s, ps1r, ps1_sem, f).wait_recv()
        xs1s[f] = (part1[...] + ps1r[f].astype(F32)).astype(BF16)
        to_partner(xs1s, xs1r, xs1_sem, f).start()

    def sum_second(f):
        to_sibling(ps2s, ps2r, ps2_sem, f).wait_recv()
        xs2s[f] = (part2[...] + ps2r[f].astype(F32)).astype(BF16)
        second_xs(f, 1 - x).start()

    def second_xs(f, holder):
        rows = pl.ds(0, half)
        if last:
            rows = pl.ds(pl.multiple_of(2 * piece * holder, piece), 3 * piece)
        return remote(
            xs2s.at[f, rows], xs2r.at[f, rows], xs2_sem.at[0, f], xs2_sem.at[1, f], partner
        )

    def middle(f):
        to_partner(xs1s, xs1r, xs1_sem, f).wait_recv()

        total = xs1s[f].astype(F32) + xs1r[f].astype(F32)
        mid = own_stream(f) + mod[2:3] * total
        ao[f] = total.astype(BF16)
        x1[f] = mid
        normed, _ = norm(mid)
        h2[f, own] = (normed * (1.0 + mod[4:5]) + mod[3:4]).astype(BF16)
        share(h2, h2_sem, f, own).start()
        save(4, f).start()
        save(5, f).start()

    def mlp(f):
        share(h2, h2_sem, f, theirs).wait_recv()
        save(6, f).start()

        for start in range(0, act.shape[2], 256):
            c = pl.ds(start, 256)
            u = dot(h2[f], fc1_w[:, c])
            sq = u * u
            t = jnp.tanh(GELU_K * (u + GELU_C * u * sq))
            one_t = 0.5 * (1.0 + t)
            act[f, :, c] = (u * one_t).astype(BF16)
            slope = one_t + (0.5 * GELU_K) * u * (1.0 - t * t) * (1.0 + (3.0 * GELU_C) * sq)
            dg[f, :, c] = slope.astype(BF16)
        save(7, f).start()
        save(8, f).start()
        ps2s[f] = dot(act[f, theirs], fc2_w[...]).astype(BF16)
        to_sibling(ps2s, ps2r, ps2_sem, f).start()
        part2[...] = dot(act[f, own], fc2_w[...])

    def finish(f):
        second_xs(f, x).wait_recv()
        if last:
            keep = pl.ds(pl.multiple_of(2 * piece * x, piece), 3 * piece)
            total = xs2s[f, keep].astype(F32) + xs2r[f, keep].astype(F32)
            result = x1[f, keep] + mod[5:6] * total
            mo[f] = jnp.zeros((half, model), BF16)
            qr, qc = lax.div(f, 2), lax.rem(f, 2)
            for i in range(3):
                frame = 2 * x + i
                counted = (frame != 2) | (qr == x)
                cut = slice(i * piece, (i + 1) * piece)
                rows = pl.ds(pl.multiple_of((2 * x + i) * piece, piece), piece)
                mo[f, rows] = jnp.where(counted, total[cut], 0.0).astype(BF16)
                r["groups"][frame * 2 + qr, :, qc] = result[cut].reshape(4, 8, model)
        else:
            total = xs2s[f].astype(F32) + xs2r[f].astype(F32)
            mo[f] = total.astype(BF16)
            store_a_to_b(y_out, f, x1[f] + mod[5:6] * total)
        save(9, f).start()

    def first_step(t):
        attention(t)
        sum_first(t)
        if not last:

            @pl.when(t + 2 < windows)
            def _():
                first_norm(t + 2)

    def second_step(t):
        @pl.when(t + 1 < windows)
        def _():
            middle(t + 1)

        mlp(t)
        sum_second(t)

    def last_step(t):
        if not last:
            blocks = r["next_index"].shape[0] // 16
            each = -(-blocks // windows)

            def next_bias(i):
                block = t * each + i

                @pl.when(block < blocks)
                def _():
                    rows = pl.ds(pl.multiple_of(block * 16, 16), 16)
                    lookup(r["next_index"], r["next_table_v"], r["next_bias"], rows)

            loop(each, next_bias)
        finish(t)

    loop(windows, first_step)
    if last:
        top()
    for copy in weights[4:]:
        copy.wait()
    middle(0)
    loop(windows, second_step)
    if last:
        top_weights()
    loop(windows, last_step)
    if last:
        hand_out(r["groups"], y_out, r["hand_sem"].at[0], r["hand_sem"].at[1], x, core, sibling)

    def drain(f):
        for which in range(len(saves)):
            save(which, f).wait()
        share(h1, h1_sem, f, own).wait_send()
        share(h2, h2_sem, f, own).wait_send()
        to_sibling(ps1s, ps1r, ps1_sem, f).wait_send()
        to_sibling(ps2s, ps2r, ps2_sem, f).wait_send()
        to_partner(xs1s, xs1r, xs1_sem, f).wait_send()
        second_xs(f, 1 - x).wait_send()
        if last:
            share(r["gm_v"], r["gm_sem"], f, own).wait_send()
            pltpu.make_async_copy(r["top_v"].at[f], r["top"].at[f], r["top_sem"].at[f]).wait()
        else:
            keep_stream(f).wait()

    loop(windows, drain)
    rows_drain()
    if last:
        grad_copy().wait()


def block_forward(rows, first, then, params, mask, size, collective_id):
    last = then is not None
    qkv_w, proj_w, fc1_w, fc2_w = params
    windows, _, width = mask.shape
    model = rows.shape[-1]
    half = width // 2
    heads = then[2].shape[0] if last else first["table"].shape[0]
    inner = proj_w.shape[0]
    hidden = fc1_w.shape[1]
    sds = jax.ShapeDtypeStruct
    ins = {"rows": (rows, ANY), "mask": (mask, VM)}
    outs, scratch = {}, {}
    if last:
        ins.update({name: (v, VM) for name, v in zip(("stream", "mod", "bias"), then, strict=True)})
    else:
        for name, value in first.items():
            whole = name in ("ada_a", "ada_b", "spatial", "joint")
            ins[name] = (value, ANY if whole else VM)
        spatial, joint = first["spatial"], first["joint"]
        next_shape = (joint.shape[0], -(-joint.shape[1] // 128) * 128)
        outs["mods"] = (sds((2, 6, model), F32), VM)
        outs["cond_act"] = (sds((2, 512), F32), VM)
        outs["index"] = (sds(spatial.shape, jnp.int32), VM)
        outs["next_index"] = (sds(next_shape, jnp.int32), VM)
        outs["next_bias"] = (sds((heads, *next_shape), BF16), VM)
        for name in ("table", "next_table"):
            count = -(-first[name].shape[1] // 128)
            scratch[name + "_v"] = pltpu.VMEM((heads, count, 128), F32)
        scratch["index_v"] = pltpu.VMEM(spatial.shape, jnp.int32)
        scratch["next_index_v"] = pltpu.VMEM(joint.shape, jnp.int32)
        scratch["ada_v"] = pltpu.VMEM((2, *first["ada_a"].shape), BF16)
        scratch["parts"] = pltpu.VMEM((2, 3, 512), F32)
        scratch["index_sem"] = dma((4 + 2 * FRAMES,))
        scratch["ada_sem"] = dma((2,))
        outs["stream_s"] = (sds((windows, 2, half // 2, model), BF16), ANY)
        scratch["stream"] = pltpu.VMEM((windows, 2, half // 2, model), BF16)
        scratch["bias"] = pltpu.VMEM((heads, *spatial.shape), BF16)
        scratch["pieces"] = pltpu.VMEM((4, 2, 3, 512), F32)
        scratch["mod_sem"] = dma((2, 3))
    scratch["rows_send"] = dma((5, 2))
    scratch["rows_local"] = dma((3,))
    scratch["rows_recv"] = dma((2 * FRAMES,))
    for name, value in (("qkv", qkv_w), ("proj", proj_w), ("fc1", fc1_w), ("fc2", fc2_w)):
        ins[name] = (value, ANY)
        shape = (model, 3 * inner) if name == "qkv" else value.shape
        scratch[name + "_w"] = pltpu.VMEM(shape, value.dtype)
    saved = {
        "h1": ((windows, width, model), BF16),
        "qkv_s": ((windows, width, 3 * inner), BF16),
        "prob": ((windows, heads, width, width), BF16),
        "att": ((windows, width, inner), BF16),
        "ao": ((windows, half, model), BF16),
        "x1": ((windows, half, model), F32),
        "h2": ((windows, width, model), BF16),
        "act": ((windows, width, hidden), BF16),
        "dg": ((windows, width, hidden), BF16),
        "mo": ((windows, half, model), BF16),
    }
    if last:
        outs["top"] = (sds((windows, half // 8, 8, model), F32), ANY)
        scratch["top_v"] = pltpu.VMEM((windows, half // 8, 8, model), F32)
        scratch["top_rows"] = pltpu.VMEM((FRAMES, 2, 4 * SIDE, model), BF16)
        saved["gm"] = ((windows, width, model), BF16)
        saved["fc2_grad"] = ((size // 2, 2, model // size, hidden), BF16)
    for name, (shape, dtype) in saved.items():
        outs[name] = (sds(shape, dtype), ANY)
        scratch[name + "_v"] = pltpu.VMEM(shape, dtype)
    if last:
        outs["y"] = (sds((FRAMES, 4, 2, 8, model), F32), VM)
        scratch["groups"] = pltpu.VMEM((2 * FRAMES, 4, 2, 8, model), F32)
    else:
        outs["y"] = (sds((4, FRAMES * 4, 8, model), F32), VM)
    own_all = pltpu.VMEM((windows, half, model), BF16)
    for name in ("ps1s", "ps1r", "xs1s", "xs1r", "ps2s", "ps2r", "xs2s", "xs2r"):
        scratch[name] = own_all
    for name in ("h1", "h2", "gm", "ps1", "ps2", "xs1", "xs2"):
        scratch[name + "_sem"] = dma((2, windows))
    scratch.update(
        part1=pltpu.VMEM((half, model), F32),
        part2=pltpu.VMEM((half, model), F32),
        w_sem=dma((5,)),
        qkv_sem=dma((3,)),
        out_sem=dma((11, windows)),
        top_sem=dma((windows,)),
        hand_sem=dma((2, 2)),
    )
    names = (*ins, *outs, *scratch)
    results = pl.pallas_call(
        functools.partial(forward_kernel, windows, last, names),
        out_shape=[shape for shape, _ in outs.values()],
        in_specs=[spec for _, spec in ins.values()],
        out_specs=[spec for _, spec in outs.values()],
        scratch_shapes=list(scratch.values()),
        compiler_params=pltpu.CompilerParams(
            collective_id=collective_id, has_side_effects=True, vmem_limit_bytes=VMEM_LIMIT
        ),
        name="forward_last" if last else "forward_first",
    )(*[value for value, _ in ins.values()])
    return dict(zip(outs, results, strict=True))


QKV_EARLY = 1
STREAMS = ("dg", "h2", "qkv_s", "prob", "h1", "x1", "ao", "mo", "stream")


def backward_kernel(windows, last, size, names, *refs):
    r = dict(zip(names, refs, strict=True))
    mod, index = r["mod"].at[1 if last else 0], r.get("index")
    grad, part1, part2, gh, gqkv = r["grad"], r["part1"], r["part2"], r["gh"], r["gqkv"]
    fc1_w, fc2_w, qkv_w, proj_w = r["fc1_w"], r["fc2_w"], r["qkv_w"], r["proj_w"]
    gm, rest, wgrad, gbias = r["gm"], r["rest"], r["wgrad"], r["gbias"]
    ga = gm
    ps1s, ps1r, ps2s, ps2r = r["ps1s"], r["ps1r"], r["ps2s"], r["ps2r"]
    xs1s, xs1r, xs2s, xs2r = r["xs1s"], r["xs1r"], r["xs2s"], r["xs2r"]
    buf1, buf2, msum, mtot, mrecv = r["buf1"], r["buf2"], r["msum"], r["mtot"], r["mrecv"]
    _, half, model = grad.shape
    width = 2 * half
    heads = gbias.shape[0]
    inner = proj_w.shape[0]
    head_dim = inner // heads
    hidden = gh.shape[1]
    scale = head_dim ** (-0.5)
    chunk = buf1.shape[-1]
    fc_chunks = hidden // chunk
    rest_chunks = 4 * inner // chunk
    carry_chunks = r["carry"].shape[-1] // chunk
    now = range(QKV_EARLY if last else rest_chunks - 1)
    kinds = {"fc1": 0, "carry": 1, "rest": 2, "fc2": 3}
    sources = {"fc1": fc1_w, "carry": rest, "rest": rest, "fc2": r.get("fc2_grad")}
    if last:
        plan = {
            (0, 1): [("carry", 0)],
            (0, 2): [("carry", 1)],
            (0, 3): [("carry", 2)],
            (1, 0): [("carry", 3), ("fc1", 0)],
            (1, 1): [("fc1", 1)],
            (1, 2): [("fc1", 2)],
            (1, 3): [("fc1", 3)],
        }
    else:
        plan = {
            (0, 1): [("carry", 0)],
            (0, 2): [("carry", 1)],
            (0, 4): [("fc2", 0)],
            (1, 0): [("fc2", 1), ("fc2", 2)],
            (1, 1): [("fc2", 3)],
            (1, 2): [("fc1", 0)],
            (1, 3): [("fc1", 1)],
            (1, 4): [("fc1", 2)],
            (2, 0): [("fc1", 3)],
        }
    if carry_chunks == 3:
        plan[0, 3] = [("carry", 2)]
    x, core, sibling, partner, diagonal = places()
    own = pl.ds(pl.multiple_of(core * half, 16), half)
    theirs = pl.ds(pl.multiple_of((1 - core) * half, 16), half)
    lines = size // 2
    here = lax.axis_index("dp")
    line, side = lax.div(here, 2), lax.rem(here, 2)

    targets = {
        "grad_y": grad,
        "gm_s": gm,
        "carry": rest.at[..., pl.ds(0, r["carry"].shape[-1])],
        "fc2": fc2_w,
        "fc1": fc1_w,
        "act": r.get("act_v"),
        "proj": proj_w,
        "att": r["att_v"],
    }
    loads = {
        name: pltpu.make_async_copy(r[name], target, r["w_sem"].at[i])
        for i, (name, target) in enumerate(targets.items())
        if name in r
    }
    qkv_loads = qkv_copies(r["qkv"], qkv_w, r["qkv_sem"])
    for_mlp = ("dg", "h2")
    for_attention = ("qkv_s", "prob", "h1")
    for_middle = ("x1", "ao", "mo")

    def fetch(name, f):
        slot = lax.rem(f, 2)
        sem = r["in_sem"].at[STREAMS.index(name), slot]
        return pltpu.make_async_copy(r[name].at[f], r[name + "_v"].at[slot], sem)

    def share(buf, sem, f, rows):
        return remote(buf.at[f, own], buf.at[f, rows], sem.at[0, f], sem.at[1, f], sibling)

    def to_sibling(src, dst, sem, f):
        slot = lax.rem(f, 2)
        return remote(src.at[slot], dst.at[slot], sem.at[0, slot], sem.at[1, slot], sibling)

    def first_ps(f):
        return to_sibling(ps1s, ps1r, r["ps1_sem"], f)

    def second_ps(f):
        return to_sibling(ps2s, ps2r, r["ps2_sem"], f)

    def first_xs(f):
        sem = r["xs1_sem"]
        return remote(xs1s.at[f], xs1r.at[f], sem.at[0, f], sem.at[1, f], partner)

    def second_xs(f):
        sem, slot = r["xs2_sem"], lax.rem(f, 2)
        return remote(xs2s.at[slot], xs2r.at[f], sem.at[0, slot], sem.at[1, f], partner)

    def along_dp(src, dst, send_sem, recv_sem, other):
        return pltpu.make_async_remote_copy(
            src_ref=src,
            dst_ref=dst,
            send_sem=send_sem,
            recv_sem=recv_sem,
            device_id={"dp": other},
            device_id_type=MESH,
        )

    def chunk_cols(i):
        return pl.ds(pl.multiple_of(i * chunk, chunk), chunk)

    def across(kind, i):
        k = kinds[kind]
        return along_dp(
            sources[kind].at[:, 1 - side, :, chunk_cols(i)],
            buf1.at[k, i],
            r["across_sem"].at[0, k, i],
            r["across_sem"].at[1, k, i],
            line * 2 + 1 - side,
        )

    def along(kind, i, j):
        k = kinds[kind]
        to = lax.rem(line + 1 + j, lines)
        return along_dp(
            buf1.at[k, i, to],
            buf2.at[k, i, j],
            r["along_sem"].at[0, k, i, j],
            r["along_sem"].at[1, k, i, j],
            to * 2 + side,
        )

    def reduce_side(kind, i):
        k = kinds[kind]
        across(kind, i).wait_recv()
        mine = sources[kind][:, side, :, chunk_cols(i)]
        buf1[k, i] = (mine.astype(F32) + buf1[k, i].astype(F32)).astype(BF16)
        loop(lines - 1, lambda j: along(kind, i, j).start())

    def reduce_line(kind, i):
        k = kinds[kind]
        loop(lines - 1, lambda j: along(kind, i, j).wait_recv())
        return buf1[k, i, line].astype(F32) + jnp.sum(buf2[k, i].astype(F32), axis=0)

    def take_up(phase, f):
        for (when, step), sums in plan.items():
            if when != phase:
                continue

            @pl.when(f == step)
            def _(sums=sums):
                for kind, i in sums:
                    reduce_side(kind, i)

    def drain_sum(kind, i):
        if kind != "carry":
            across(kind, i).wait_send()
        loop(lines - 1, lambda j: along(kind, i, j).wait_send())

    for copy in loads.values():
        copy.start()
    for which in for_mlp:
        fetch(which, 0).start()
    for copy in qkv_loads:
        copy.start()

    barrier = pltpu.get_barrier_semaphore()
    for other in (sibling, partner):
        pl.semaphore_signal(barrier, inc=1, device_id={"mp": other}, device_id_type=MESH)

    def greet_dp(j):
        pl.semaphore_signal(
            barrier, inc=1, device_id={"dp": lax.rem(here + 1 + j, size)}, device_id_type=MESH
        )

    loop(size - 1, greet_dp)
    pl.semaphore_wait(barrier, 1 + size)

    def top(f):
        gm[f, own] = (mod[5:6] * grad[f]).astype(BF16)
        share(gm, r["gm_sem"], f, own).start()

    loads["grad_y"].wait()
    if last:
        loads["gm_s"].wait()
    else:
        loop(windows, top)
    loads["carry"].wait()
    loop(carry_chunks, lambda i: across("carry", i).start())
    msum[...] = jnp.zeros_like(msum)
    gbias[...] = jnp.zeros_like(gbias)
    wgrad[...] = jnp.zeros_like(wgrad)

    lane_head = lax.div(lax.broadcasted_iota(jnp.int32, (width, inner), 1), head_dim)
    zero = jnp.zeros((), BF16)

    def flat(weight):
        value = weight[...]
        return value.reshape(-1, value.shape[-1])

    def mlp_back(f):
        slot = lax.rem(f, 2)
        for which in for_mlp:
            fetch(which, f).wait()
        if not last:

            @pl.when(f == 0)
            def _():
                share(gm, r["gm_sem"], f, theirs).wait_recv()

        gh[...] = (dot_nt(gm[f], flat(fc2_w)) * r["dg_v"][slot].astype(F32)).astype(BF16)

        @pl.when(f >= 2)
        def _():
            first_ps(f - 2).wait_send()

        ps1s[slot] = dot_nt(gh[theirs], flat(fc1_w)).astype(BF16)
        first_ps(f).start()
        part1[...] = dot_nt(gh[own], flat(fc1_w))

    def sum_first(f):
        slot = lax.rem(f, 2)
        first_ps(f).wait_recv()
        xs1s[f] = (part1[...] + ps1r[slot].astype(F32)).astype(BF16)
        first_xs(f).start()

    def fc2_weights():
        loop(windows - 1, lambda f: share(gm, r["gm_sem"], f + 1, theirs).wait_recv())
        loads["act"].wait()
        grads, acts = gm[...].reshape(-1, model), r["act_v"][...].reshape(-1, hidden)
        out = r["fc2_grad"]
        for i in range(fc_chunks):
            c = slice(i * chunk, (i + 1) * chunk)
            out[..., c] = dot_tn(grads, acts[:, c]).astype(BF16).reshape(*out.shape[:-1], chunk)
            across("fc2", i).start()

    def mlp_weights(f):
        slot = lax.rem(f, 2)
        for start in range(0, hidden, 512):
            c = pl.ds(start, 512)
            wgrad[:, c] += dot_tn(r["h2_v"][slot], gh[:, c])

    def fold(values):
        return values.reshape(half // 8, 8, model).sum(axis=0)

    def middle(f):
        slot = lax.rem(f, 2)
        for which in for_middle:
            fetch(which, f).wait()
        first_xs(f).wait_recv()
        grad_h = xs1s[f].astype(F32) + xs1r[f].astype(F32)
        normed, inv = norm(r["x1_v"][slot])
        gy = grad[f]
        grad_mid = gy + norm_back(normed, inv, grad_h * (1.0 + mod[4:5]))
        msum[2] += fold(grad_mid * r["ao_v"][slot].astype(F32))
        msum[3] += fold(grad_h)
        msum[4] += fold(grad_h * normed)
        msum[5] += fold(gy * r["mo_v"][slot].astype(F32))
        grad[f] = grad_mid
        ga[f, own] = (mod[2:3] * grad_mid).astype(BF16)
        share(ga, r["ga_sem"], f, own).start()

    def attention_back(f):
        slot = lax.rem(f, 2)
        qkv = r["qkv_s_v"]
        for which in for_attention:
            fetch(which, f).wait()

        @pl.when(f < windows - 1)
        def _():
            share(ga, r["ga_sem"], f, theirs).wait_recv()

        grad_att = dot_nt(ga[f], proj_w[...]).astype(BF16)
        grad_att_t = grad_att.T
        queries_t = qkv[slot, :, :inner].T
        keys = qkv[slot, :, inner : 2 * inner] * BF16(scale)
        vals = qkv[slot, :, 2 * inner :]
        grad_q = jnp.zeros((width, inner), F32)
        grad_k, grad_v = [], []
        for h in range(heads):
            part = slice(h * head_dim, (h + 1) * head_dim)
            p = r["prob_v"][slot, h]
            grad_p = dot_nt(jnp.where(lane_head == h, grad_att, zero), vals)
            pf = p.astype(F32)
            weighted = pf * grad_p
            grad_s = weighted - pf * jnp.sum(weighted, axis=-1, keepdims=True)
            gbias[h, :, :width] += grad_s
            rounded = grad_s.astype(BF16)
            grad_q = grad_q + dot(rounded, jnp.where(lane_head == h, keys, zero))
            grad_v.append(dot(grad_att_t[part], p))
            grad_k.append(dot(queries_t[part], rounded) * scale)
        gqkv[:, :inner] = grad_q.astype(BF16)
        gqkv[:, inner : 2 * inner] = jnp.concatenate(grad_k, axis=0).astype(BF16).T
        gqkv[:, 2 * inner :] = jnp.concatenate(grad_v, axis=0).astype(BF16).T

        @pl.when(f >= 2)
        def _():
            second_ps(f - 2).wait_send()

        ps2s[slot] = dot_nt(gqkv[theirs], qkv_w[...]).astype(BF16)
        second_ps(f).start()
        part2[...] = dot_nt(gqkv[own], qkv_w[...])

    def sum_second(f):
        slot = lax.rem(f, 2)
        second_ps(f).wait_recv()

        @pl.when(f >= 2)
        def _():
            second_xs(f - 2).wait_send()

        xs2s[slot] = (part2[...] + ps2r[slot].astype(F32)).astype(BF16)
        second_xs(f).start()

    def attention_weights(f):
        slot = lax.rem(f, 2)
        for start in range(0, 3 * inner, 384):
            c = pl.ds(start, 384)
            wgrad[:, c] += dot_tn(r["h1_v"][slot], gqkv[:, c])

    def proj_weights():
        share(ga, r["ga_sem"], windows - 1, theirs).wait_recv()
        loads["att"].wait()
        piece = dot_tn(ga[...].reshape(-1, model), r["att_v"][...].reshape(-1, inner))
        for i in range(carry_chunks):
            across("carry", i).wait_send()
        c = pl.ds(3 * inner, inner)
        rest[..., c] = piece.astype(BF16).reshape(*rest.shape[:-1], inner)
        across("rest", rest_chunks - 1).start()

    def finish(f):
        slot = lax.rem(f, 2)
        fetch("stream", f).wait()
        second_xs(f).wait_recv()
        grad_h = xs2s[slot].astype(F32) + xs2r[f].astype(F32)
        normed, inv = norm(r["stream_v"][slot].astype(F32).reshape(half, model))
        msum[0] += fold(grad_h)
        msum[1] += fold(grad_h * normed)
        grad_x = grad[f] + norm_back(normed, inv, grad_h * (1.0 + mod[1:2]))
        if last:
            store_b_to_a(r["gx"], f, grad_x)
        else:
            grad[f] = grad_x

    def first_step(f):
        @pl.when(f + 1 < windows)
        def _():
            for which in for_mlp:
                fetch(which, f + 1).start()

        @pl.when(f == 0)
        def _():
            loads["fc2"].wait()
            loads["fc1"].wait()

        mlp_back(f)
        mlp_weights(f)
        sum_first(f)
        if not last:
            pl.when(f == 0)(fc2_weights)
        take_up(0, f)

    loop(windows, first_step)
    if not last:
        loop(windows, lambda f: share(gm, r["gm_sem"], f, own).wait_send())

    for which in (*for_attention, *for_middle, "stream"):
        fetch(which, 0).start()
    shape = fc1_w.shape
    fc1_w[...] = wgrad[:, :hidden].astype(BF16).reshape(shape)
    loop(fc_chunks, lambda i: across("fc1", i).start())
    wgrad[:, : 3 * inner] = jnp.zeros((model, 3 * inner), F32)
    for which in for_middle:
        fetch(which, 1).start()
    middle(0)
    for copy in (loads["proj"], *qkv_loads):
        copy.wait()

    def second_step(f):
        @pl.when(f + 1 < windows)
        def _():
            for which in for_attention:
                fetch(which, f + 1).start()
            middle(f + 1)

        @pl.when(f + 2 < windows)
        def _():
            for which in for_middle:
                fetch(which, f + 2).start()

        attention_back(f)
        attention_weights(f)
        sum_second(f)
        pl.when(f == windows - 2)(proj_weights)

        @pl.when(f >= 1)
        def _():
            finish(f - 1)

        @pl.when((f >= 1) & (f + 1 < windows))
        def _():
            fetch("stream", f + 1).start()

        @pl.when(f == 0)
        def _():
            fetch("stream", 1).start()

        take_up(1, f)

    loop(windows, second_step)

    shape = (*rest.shape[:-1], 3 * inner)
    rest[..., pl.ds(0, 3 * inner)] = wgrad[:, : 3 * inner].astype(BF16).reshape(shape)
    for i in now:
        across("rest", i).start()
    if last:
        later = pl.ds(len(now) * chunk, (rest_chunks - 1 - len(now)) * chunk)
        carry = pltpu.make_async_copy(rest.at[..., later], r["carry_next"], r["w_sem"].at[8])
        carry.start()
    else:
        wide = r["gbias_b"].shape[2]
        tall = r["gbias_b"].shape[1]

        def other_place(h):
            return pl.ds(h // 2 * tall, tall), pl.ds(h % 2 * wide, wide)

        other_loads = []
        for h in range(heads):
            other_loads.append(
                pltpu.make_async_copy(
                    r["gbias_b"].at[h], wgrad.at[other_place(h)], r["other_sem"].at[h]
                )
            )
            other_loads[-1].start()
    take_up(2, 0)
    finish(windows - 1)
    for i in range(12):
        c = slice(i % 2 * 512, i % 2 * 512 + 512)
        mtot[i // 3, pl.ds(i % 3, 1)] = jnp.sum(msum[i // 2, :, c], axis=0, keepdims=True)
    if last:
        gate = r["gate"]
        gate[0] = mtot[3, 1:3]
        gate_copy = remote(
            gate.at[0], gate.at[1], r["mod_sem"].at[2], r["mod_sem"].at[3], partner
        )
        gate_copy.start()
        gate_copy.wait()
        mtot[3, 1:3] = gate[0] + gate[1]
    mod_copy = remote(mtot, mrecv, r["mod_sem"].at[0], r["mod_sem"].at[1], sibling)
    mod_copy.start()
    small, everyone, tabs = r.get("small"), r.get("everyone"), r.get("tabs")

    def give_small(j):
        return along_dp(
            small,
            everyone.at[here],
            r["small_sem"].at[0, j],
            r["small_sem"].at[1, j],
            lax.rem(here + 1 + j, size),
        )

    def give_table(j):
        to = lax.rem(here + 1 + j, size)
        sem = r["table_sem"]
        return along_dp(tabs.at[to], r["tab_parts"].at[j], sem.at[0, j], sem.at[1, j], to)

    def give_sum(j):
        to = lax.rem(here + 1 + j, size)
        sem = r["sum_sem"]
        return along_dp(r["tab_sum"], r["tables"].at[here], sem.at[0, j], sem.at[1, j], to)

    def start_mods():
        mod_copy.wait()
        me = lax.axis_index("mp")
        small[0:3] = mtot[me] + mrecv[me]
        small[3:6] = r["mod_b"][...]
        small[6:8] = r["cond"][...]
        everyone[here] = small[...]
        loop(size - 1, lambda j: give_small(j).start())

    def start_tables():
        each = tabs.shape[1]
        whole = r["whole_table"]
        whole[...] = jnp.zeros_like(whole)
        base = 0
        for table in (r["table"], r["table_b"]):
            rows, columns = table.shape
            whole[:rows, base : base + columns] = table[...]
            base += columns
        for i in range(size):
            tabs[i] = whole[i * each : (i + 1) * each]
        loop(size - 1, lambda j: give_table(j).start())

    def finish_tables():
        loop(size - 1, lambda j: give_table(j).wait_recv())
        total = tabs[here] + jnp.sum(r["tab_parts"][...], axis=0)
        r["tab_sum"][...] = total
        r["tables"][here] = total
        give_ada()
        loop(size - 1, lambda j: give_sum(j).start())

    def give_ada():
        loop(size - 1, lambda j: give_small(j).wait_recv())
        rows = r["ada_a_out"].shape[0]
        lane = lax.broadcasted_iota(jnp.int32, (rows, model), 1)
        row = lax.broadcasted_iota(jnp.int32, (rows, model), 0) + here * rows
        chosen = jnp.where(lane == row, 1.0, 0.0).astype(BF16)
        conds = [everyone[:, 6 + i, :].astype(BF16) for i in range(2)]
        mine = dot_nt(chosen[:, :512], conds[0]) + dot_nt(chosen[:, 512:], conds[1])
        for i in range(6):
            out = r["ada_a_out" if i < 3 else "ada_b_out"]
            out[:, pl.ds(i % 3 * 512, 512)] = jnp.dot(
                mine, everyone[:, i, :], precision=HIGHEST, preferred_element_type=F32
            )

    def finish_sums():
        loop(size - 1, lambda j: give_sum(j).wait_recv())
        whole, tables = r["whole_table"], r["tables"]
        each = tables.shape[1]
        for i in range(size):
            whole[i * each : (i + 1) * each] = tables[i]
        turned = whole[...].T
        base = 0
        for name, table in (("table_a_out", r["table"]), ("table_b_out", r["table_b"])):
            out, lows = r[name], table.shape[0]
            groups = table.shape[1] // heads
            for h in range(heads):
                for g in range(-(-out.shape[1] // lows)):
                    count = min(lows, out.shape[1] - g * lows)
                    row = base + h * groups + g
                    out[pl.ds(h, 1), pl.ds(g * lows, count)] = turned[row : row + 1, :count]
            base += heads * groups
        for give in (give_small, give_table, give_sum):
            loop(size - 1, lambda j, give=give: give(j).wait_send())

    hands = []
    if not last:
        gx = r["gx"]

        def group(j):
            which = 5 * x + j
            rows = pl.ds(pl.multiple_of(lax.rem(which, 2) * 64, 64), 64)
            return lax.div(which, 2), rows

        for i in range(2):
            f, rows = group(3 - 3 * core + i)
            hands.append(
                remote(
                    grad.at[f, rows],
                    gx.at[1 + 2 * i],
                    r["hand_sem"].at[0, i],
                    r["hand_sem"].at[1, i],
                    sibling,
                )
            )
            hands[-1].start()
        for i in range(3):
            f, rows = group(2 * core + i)
            gx[2 * i] = grad[f, rows]

    if last:
        for i in (rest_chunks - 1, *now):
            reduce_side("rest", i)
    else:
        start_mods()
        mine = [gbias.at[h] for h in range(heads)]
        other = [wgrad.at[other_place(h)] for h in range(heads)]
        scatter(index, mine, r["table"])
        reduce_side("rest", rest_chunks - 1)
        for copy in other_loads:
            copy.wait()
        for i in range(4):
            scatter(r["index_b"], other, r["table_b"], i, 4)
            if i < 2:
                reduce_side("rest", i)
        start_tables()
        reduce_side("rest", 2)
    outputs = [
        ("carry", range(carry_chunks)),
        ("fc1", range(fc_chunks)),
        ("rest", (rest_chunks - 1, *now)),
    ]
    if not last:
        outputs.insert(1, ("fc2", range(fc_chunks)))

    def finish_chunk(kind, i):
        value = reduce_line(kind, i)
        if kind == "fc1":
            r["fc1_out"][:, pl.ds(i * chunk, chunk)] = value
        elif kind == "fc2" or (last and kind == "carry"):
            r["fc2_out"][pl.ds(i * chunk, chunk)] = value.T
        else:
            piece = i if kind == "rest" else 3 - carry_chunks + i
            to = "_b_out" if kind == "carry" else "_out"
            if piece < 3:
                r["qkv" + to][piece] = value
            else:
                r["proj_out"][...] = value.T

    if not last:
        if QKV_EARLY:
            r["qkv_b_out"][pl.ds(0, QKV_EARLY)] = r["early"][...]
    for kind, chunks in outputs:
        if kind == "rest" and not last:
            finish_tables()
        for i in chunks:
            finish_chunk(kind, i)
    if last:
        carry.wait()
        mod_copy.wait()
        me = lax.axis_index("mp")
        r["mod_out"][...] = mtot[me] + mrecv[me]
    else:
        finish_sums()
    for copy in hands:
        copy.wait()

    def drain(f):
        share(ga, r["ga_sem"], f, own).wait_send()
        first_xs(f).wait_send()

    loop(windows, drain)
    for f in range(windows - 2, windows):
        for copy in (first_ps(f), second_ps(f), second_xs(f)):
            copy.wait_send()

    for kind, chunks in outputs:
        for i in chunks:
            drain_sum(kind, i)


def block_backward(
    stream, grad_y, mod, params, kept, index, table_lens, carry, sums, size, collective_id
):
    last = "gm" in kept
    qkv_w, proj_w, fc1_w, fc2_w = params
    windows, half, model = kept["x1"].shape
    width = 2 * half
    heads = kept["prob"].shape[1]
    inner = proj_w.shape[0]
    hidden = fc1_w.shape[1]
    rows = model // size
    lines = size // 2
    chunk = inner
    chunks = max(hidden, 4 * inner) // chunk
    kinds = 3 if last else 4
    groups = [-(-count // lows) for count, lows in zip(table_lens, (64, 128))]
    sds = jax.ShapeDtypeStruct
    sliced = (lines, 2, rows)
    cut = (*sliced, hidden)

    ins, outs, scratch = {}, {}, {}
    ins["grad_y"] = (grad_y, ANY)
    ins["mod"] = (mod, VM)
    if not last:
        ins["index"] = (index, VM)
    for name in STREAMS:
        value = stream if name == "stream" else kept[name]
        ins[name] = (value, ANY)
        scratch[name + "_v"] = pltpu.VMEM((2,) + value.shape[1:], value.dtype)
    ins["att"] = (kept["att"], ANY)
    scratch["att_v"] = pltpu.VMEM(kept["att"].shape, BF16)
    ins["qkv"] = (qkv_w, ANY)
    ins["proj"] = (proj_w, ANY)
    ins["fc1"] = (fc1_w.reshape(cut), ANY)
    ins["fc2"] = (fc2_w.reshape(cut), ANY)
    ins["carry"] = (carry, ANY)
    if last:
        ins["gm_s"] = (kept["gm"], ANY)
        outs["gx"] = (sds((2 * FRAMES, 4, 2, 8, model), F32), VM)
        outs["carry_next"] = (sds((*sliced, (3 - QKV_EARLY) * inner), BF16), ANY)
        if QKV_EARLY:
            outs["qkv_out"] = (sds((QKV_EARLY, rows, inner), F32), VM)
        outs["proj_out"] = (sds((inner, rows), F32), VM)
        outs["gbias"] = (sds((heads, *index.shape), F32), VM)
    else:
        ins["act"] = (kept["act"], ANY)
        scratch["act_v"] = pltpu.VMEM(kept["act"].shape, BF16)
        scratch["fc2_grad"] = pltpu.VMEM(cut, BF16)
        scratch["gbias"] = pltpu.VMEM((heads, *index.shape), F32)
        outs["gx"] = (sds((FRAMES, 4 * SIDE, model), F32), VM)
        for to in ("_out", "_b_out"):
            outs["qkv" + to] = (sds((3, rows, inner), F32), VM)
        outs["proj_out"] = (sds((inner, rows), F32), VM)
    outs["fc2_out"] = (sds((hidden, rows), F32), VM)
    outs["fc1_out"] = (sds((rows, hidden), F32), VM)
    if last:
        outs["mod_out"] = (sds((3, 512), F32), VM)
    else:
        each = 128 // size
        names = ("mod_b", "cond", "index_b", "early")
        ins.update(
            {name: (v, VM) for name, v in zip(names, sums[:4], strict=True) if v is not None}
        )
        ins["gbias_b"] = (sums[4], ANY)
        for b, count in zip("ab", table_lens, strict=True):
            outs[f"table_{b}_out"] = (sds((heads, count), F32), VM)
            outs[f"ada_{b}_out"] = (sds((rows, 3 * 512), F32), VM)
        scratch.update(
            everyone=pltpu.VMEM((size, 8, 512), F32),
            tables=pltpu.VMEM((size, each, 128), F32),
            whole_table=pltpu.VMEM((128, 128), F32),
            table=pltpu.VMEM((64, heads * groups[0]), F32),
            table_b=pltpu.VMEM((128, heads * groups[1]), F32),
            other_sem=dma((heads,)),
            small=pltpu.VMEM((8, 512), F32),
            tabs=pltpu.VMEM((size, each, 128), F32),
            tab_parts=pltpu.VMEM((size - 1, each, 128), F32),
            tab_sum=pltpu.VMEM((each, 128), F32),
            small_sem=dma((2, size - 1)),
            table_sem=dma((2, size - 1)),
            sum_sem=dma((2, size - 1)),
        )

    own_all = pltpu.VMEM((windows, half, model), BF16)
    own_two = pltpu.VMEM((2, half, model), BF16)
    own_one = pltpu.VMEM((half, model), F32)
    every = pltpu.VMEM((windows, width, model), BF16)
    scratch.update(
        grad=pltpu.VMEM((windows, half, model), F32),
        part1=own_one,
        part2=own_one,
        gh=pltpu.VMEM((width, hidden), BF16),
        gqkv=pltpu.VMEM((width, 3 * inner), BF16),
        fc1_w=pltpu.VMEM(cut, BF16),
        fc2_w=pltpu.VMEM(cut, BF16),
        qkv_w=pltpu.VMEM((model, 3 * inner), BF16),
        proj_w=pltpu.VMEM(proj_w.shape, BF16),
        gm=every,
        rest=pltpu.VMEM((*sliced, 4 * inner), BF16),
        wgrad=pltpu.VMEM((model, max(4 * inner, hidden)), F32),
        ps1s=own_two,
        ps1r=own_two,
        ps2s=own_two,
        ps2r=own_two,
        xs1s=own_all,
        xs2s=own_two,
        xs1r=own_all,
        xs2r=own_all,
        buf1=pltpu.VMEM((kinds, chunks, lines, rows, chunk), BF16),
        buf2=pltpu.VMEM((kinds, chunks, lines - 1, rows, chunk), BF16),
        msum=pltpu.VMEM((6, 8, model), F32),
        mtot=pltpu.VMEM((4, 3, 512), F32),
        mrecv=pltpu.VMEM((4, 3, 512), F32),
        w_sem=dma((9,)),
        qkv_sem=dma((3,)),
        in_sem=dma((11, 2)),
        gm_sem=dma((2, windows)),
        ga_sem=dma((2, windows)),
        ps1_sem=dma((2, 2)),
        ps2_sem=dma((2, 2)),
        xs1_sem=dma((2, windows)),
        xs2_sem=dma((2, windows)),
        hand_sem=dma((2, 2)),
        mod_sem=dma((4,)),
        gate=pltpu.VMEM((2, 2, 512), F32),
        across_sem=dma((2, kinds, chunks)),
        along_sem=dma((2, kinds, chunks, lines - 1)),
    )
    names = (*ins, *outs, *scratch)
    results = pl.pallas_call(
        functools.partial(backward_kernel, windows, last, size, names),
        out_shape=[shape for shape, _ in outs.values()],
        in_specs=[spec for _, spec in ins.values()],
        out_specs=[spec for _, spec in outs.values()],
        scratch_shapes=list(scratch.values()),
        compiler_params=pltpu.CompilerParams(
            collective_id=collective_id, has_side_effects=True, vmem_limit_bytes=VMEM_LIMIT
        ),
        name="backward_last" if last else "backward_first",
    )(*[value for value, _ in ins.values()])
    return dict(zip(outs, results, strict=True))


def lookup(index, table, out, r):
    heads, groups = table.shape[0], table.shape[1]
    for block in range(index.shape[1] // 128):
        c = pl.ds(block * 128, 128)
        row = index[r, c]
        low = row & 127
        high = row >> 7
        found = [jnp.zeros((16, 128), F32) for _ in range(heads)]
        for g in range(groups):
            here = high == g
            for h in range(heads):
                spread = jnp.broadcast_to(table[h, pl.ds(g, 1), :], (16, 128))
                taken = jnp.take_along_axis(spread, low, axis=1, mode="promise_in_bounds")
                found[h] = jnp.where(here, taken, found[h])
        for h in range(heads):
            out[h, r, c] = found[h].astype(BF16)


def scatter(index, grad, out, part=0, parts=1):
    heads = len(grad)
    groups = out.shape[1] // heads
    rows, width = index.shape
    if part == 0:
        out[...] = jnp.zeros_like(out)
    count = rows // 8 // parts
    lows = out.shape[0]
    shift = lows.bit_length() - 1
    low_rows = lax.broadcasted_iota(jnp.int32, (lows, width), 0)
    high_rows = lax.broadcasted_iota(jnp.int32, (groups, width), 0)

    def some(i):
        r = pl.ds(pl.multiple_of((part * count + i) * 8, 8), 8)
        index_rows = index[r, :]
        low = index_rows & (lows - 1)
        high = index_rows >> shift
        grads = [g[r, :] for g in grad]
        total = out[...]
        for i in range(8):
            onehot = jnp.where(low_rows == low[i : i + 1], 1.0, 0.0).astype(BF16)
            here = high_rows == high[i : i + 1]
            placed = jnp.concatenate(
                [jnp.where(here, g[i : i + 1], 0.0) for g in grads], axis=0
            ).astype(BF16)
            total = total + dot_nt(onehot, placed)
        out[...] = total

    loop(count, some)


def copy_kernel(count, *refs):
    given, out, held = refs[:count], refs[count : 2 * count], refs[2 * count : 3 * count]
    ins, outs = refs[3 * count :]
    reads = [pltpu.make_async_copy(given[i], held[i], ins.at[i]) for i in range(count)]
    writes = [pltpu.make_async_copy(held[i], out[i], outs.at[i]) for i in range(count)]
    for copy in reads:
        copy.start()
    for read, write in zip(reads, writes, strict=True):
        read.wait()
        write.start()
    for copy in writes:
        copy.wait()


def copy_out(arrays):
    return pl.pallas_call(
        functools.partial(copy_kernel, len(arrays)),
        out_shape=[jax.ShapeDtypeStruct(a.shape, a.dtype) for a in arrays],
        in_specs=[ANY] * len(arrays),
        out_specs=[ANY] * len(arrays),
        scratch_shapes=[pltpu.VMEM(a.shape, a.dtype) for a in arrays]
        + [dma((len(arrays),)), dma((len(arrays),))],
        compiler_params=pltpu.CompilerParams(vmem_limit_bytes=VMEM_LIMIT),
        name="copy_out",
    )(*arrays)


def local(
    tokens,
    cond,
    pad_mask,
    spatial_index,
    joint_index,
    qkv_a,
    proj_a,
    fc1_a,
    fc2_a,
    table_a,
    ada_a,
    qkv_b,
    proj_b,
    fc1_b,
    fc2_b,
    table_b,
    ada_b,
    cotangent,
    dp_size,
    mp_size,
):
    model = tokens.shape[1]
    inner = proj_a.shape[0]
    params_a = (qkv_a.transpose(1, 0, 2), proj_a, fc1_a, fc2_a)
    params_b = (qkv_b.transpose(1, 0, 2), proj_b, fc1_b, fc2_b)
    hidden_keys = jnp.where(pad_mask.reshape(-1) > 0, 0.0, -1e30).astype(F32)
    mask_a = hidden_keys.reshape(FRAMES, 2, 2, 64).transpose(0, 2, 1, 3).reshape(FRAMES, 1, -1)
    mask_b = hidden_keys.reshape(FRAMES, 2, 2, 4, 2, 8).transpose(1, 4, 2, 0, 3, 5)
    mask_b = mask_b.reshape(4, 1, -1)
    groups = (FRAMES, 4 * SIDE, model)

    first = {
        "cond": cond,
        "ada_a": ada_a,
        "ada_b": ada_b,
        "spatial": spatial_index,
        "joint": joint_index,
        "table": table_a.T,
        "next_table": table_b.T,
    }
    kept_a = block_forward(tokens.reshape(groups), first, None, params_a, mask_a, dp_size, 1)
    mods = kept_a["mods"]
    x_b = kept_a["y"].reshape(4, -1, model)
    then = (x_b, mods, kept_a["next_bias"])
    kept_b = block_forward(cotangent.reshape(groups), None, then, params_b, mask_b, dp_size, 2)
    back_b = block_backward(
        x_b,
        kept_b["top"].reshape(x_b.shape),
        mods,
        params_b,
        kept_b,
        kept_a["next_index"],
        (),
        kept_b["fc2_grad"],
        None,
        dp_size,
        3,
    )
    back_a = block_backward(
        kept_a["stream_s"],
        back_b["gx"].reshape(FRAMES, -1, model),
        mods,
        params_a,
        kept_a,
        kept_a["index"],
        (table_a.shape[0], table_b.shape[0]),
        back_b["carry_next"],
        (
            back_b["mod_out"],
            kept_a["cond_act"],
            kept_a["next_index"],
            back_b.get("qkv_out"),
            back_b["gbias"],
        ),
        dp_size,
        4,
    )

    def block_grads(b, fc):
        to = "_b_out" if b == "b" else "_out"
        return (
            back_a["qkv" + to],
            fc["proj_out"],
            fc["fc1_out"],
            fc["fc2_out"],
            back_a[f"table_{b}_out"],
            back_a[f"ada_{b}_out"],
        )

    results = list(
        copy_out((kept_b["y"], back_a["gx"], *block_grads("a", back_a), *block_grads("b", back_b)))
    )
    for i in (2, 8):
        results[i] = results[i].transpose(1, 0, 2)
        results[i + 4] = results[i + 4].T
    return (
        results[0].reshape(tokens.shape),
        results[1].reshape(tokens.shape),
        *results[2:],
    )


def solution(mesh):
    in_specs = (
        P(("dp", "mp"), None),
        P("dp", None),
        P("dp", None),
        P(),
        P(),
        P(None, None, "mp"),
        P("mp", None),
        P(None, "mp"),
        P("mp", None),
        P(None, "mp"),
        P(None, "mp"),
        P(None, None, "mp"),
        P("mp", None),
        P(None, "mp"),
        P("mp", None),
        P(None, "mp"),
        P(None, "mp"),
        P(("dp", "mp"), None),
    )
    out_specs = (
        P(("dp", "mp"), None),
        P(("dp", "mp"), None),
        P("dp", None, "mp"),
        P("mp", "dp"),
        P("dp", "mp"),
        P("mp", "dp"),
        P(None, "mp"),
        P("dp", "mp"),
        P("dp", None, "mp"),
        P("mp", "dp"),
        P("dp", "mp"),
        P("mp", "dp"),
        P(None, "mp"),
        P("dp", "mp"),
    )
    body = functools.partial(local, dp_size=mesh.shape["dp"], mp_size=mesh.shape["mp"])
    return jax.shard_map(body, mesh=mesh, in_specs=in_specs, out_specs=out_specs, check_vma=False)
```

```python
import functools

import jax
import jax.numpy as jnp
from jax import lax
from jax.experimental import pallas as pl
from jax.experimental.pallas import tpu as pltpu
from jax.sharding import PartitionSpec as P

FRAMES = 5
SIDE = 16
EPSILON = 1e-06
HIGHEST = lax.Precision.HIGHEST
MESH = pl.DeviceIdType.MESH
F32 = jnp.float32
BF16 = jnp.bfloat16
VMEM_LIMIT = 60 << 20
GELU_K = 0.7978845608028654
GELU_C = 0.044715
ANY = pl.BlockSpec(memory_space=pl.ANY)
VM = pl.BlockSpec(memory_space=pltpu.VMEM)


def own_rows(src, dst, sems, x, core, sibling, partner, diagonal):
    sends, local, recvs = sems

    def place(j):
        return dst.at[lax.div(j, 2), lax.rem(j, 2)]

    def moves():
        found = []
        for k in range(5):
            j = 5 * x + lax.div(5 * core + k, 2)
            to = (partner,) if k % 2 == 0 else (diagonal, sibling)
            for i, other in enumerate(to):
                found.append(remote(src.at[k], place(j), sends.at[k, i], recvs.at[j], other))
            if k % 2 == 0:
                found.append(pltpu.make_async_copy(src.at[k], place(j), local.at[k // 2]))
        return found

    def start():
        for copy in moves():
            copy.start()

    def wait(j):
        row = 2 * j + core
        k = lax.rem(row, 5)
        here = (lax.div(row, 10) == x) & (lax.div(lax.rem(row, 10), 5) == core)

        @pl.when(here)
        def _():
            pltpu.make_async_copy(src.at[k], place(j), local.at[lax.div(k, 2)]).wait()

        @pl.when(jnp.logical_not(here))
        def _():
            remote(src.at[0], place(j), sends.at[0, 0], recvs.at[j], partner).wait_recv()

    def drain():
        for k in range(5):
            for i in range(1 if k % 2 == 0 else 2):
                remote(src.at[k], place(0), sends.at[k, i], recvs.at[0], partner).wait_send()

    return start, wait, drain


def qkv_copies(src, dst, sems):
    inner = src.shape[2]
    return [
        pltpu.make_async_copy(src.at[i], dst.at[:, pl.ds(i * inner, inner)], sems.at[i])
        for i in range(3)
    ]


def index_copies(r):
    copies = []
    for name, size, count in (("spatial", 64, 2), ("joint", 32, FRAMES)):
        dst = r["index_v" if name == "spatial" else "next_index_v"]
        for outer in range(count):
            for owner in range(2):
                copies.append(
                    pltpu.make_async_copy(
                        r[name].at[pl.ds((outer * 2 + owner) * size, size)],
                        dst.at[pl.ds((owner * count + outer) * size, size)],
                        r["index_sem"].at[len(copies)],
                    )
                )
    return copies


def place_index(src, dst, shift, count):
    width, wide = src.shape[1], dst.shape[1]
    lane = lax.broadcasted_iota(jnp.int32, (width, wide), 1)
    group = lane >> shift
    owner = (group >= count).astype(jnp.int32)
    origin = (((group - owner * count) * 2 + owner) << shift) + (lane & ((1 << shift) - 1))
    moved = lax.broadcasted_iota(jnp.int32, (width, wide), 0) == origin
    order = jnp.where(moved & (lane < width), 1.0, 0.0).astype(BF16)
    values = src[...]
    low = dot((values & 127).astype(F32).astype(BF16), order)
    high = dot((values >> 7).astype(F32).astype(BF16), order)
    placed = (low + 128.0 * high).astype(jnp.int32)
    dst[...] = jnp.where(lax.broadcasted_iota(jnp.int32, dst.shape, 1) < width, placed, -1)


def lane_table(src, dst):
    heads, rows = src.shape
    dst[...] = jnp.zeros_like(dst)
    values = src[...].astype(F32)
    for g in range(dst.shape[1]):
        count = min(128, rows - g * 128)
        for h in range(heads):
            dst[h, pl.ds(g, 1), pl.ds(0, count)] = values[h : h + 1, g * 128 : g * 128 + count]


def dma(shape):
    return pltpu.SemaphoreType.DMA(shape)


def places():
    me = lax.axis_index("mp")
    x = lax.div(me, 2)
    core = lax.rem(me, 2)
    return x, core, x * 2 + 1 - core, (1 - x) * 2 + core, (1 - x) * 2 + 1 - core


def greet(others):
    barrier = pltpu.get_barrier_semaphore()
    for other in others:
        pl.semaphore_signal(barrier, inc=1, device_id={"mp": other}, device_id_type=MESH)
    pl.semaphore_wait(barrier, len(others))


def remote(src, dst, send_sem, recv_sem, other):
    return pltpu.make_async_remote_copy(
        src_ref=src,
        dst_ref=dst,
        send_sem=send_sem,
        recv_sem=recv_sem,
        device_id={"mp": other},
        device_id_type=MESH,
    )


def loop(count, body):
    def step(i, _):
        body(i)
        return 0

    lax.fori_loop(0, count, step, 0)


def rows16(count, body, step=16):
    loop(count // step, lambda i: body(pl.ds(pl.multiple_of(i * step, step), step)))


def norm(values):
    centred = values - jnp.mean(values, axis=-1, keepdims=True)
    inv = lax.rsqrt(jnp.mean(centred * centred, axis=-1, keepdims=True) + EPSILON)
    return centred * inv, inv


def norm_back(normed, inv, grad):
    mean_g = jnp.mean(grad, axis=-1, keepdims=True)
    mean_gn = jnp.mean(grad * normed, axis=-1, keepdims=True)
    return (grad - mean_g - normed * mean_gn) * inv


def dot(a, b):
    return jnp.dot(a, b, preferred_element_type=F32)


def dot_nt(a, b):
    return lax.dot_general(a, b, (((1,), (1,)), ((), ())), preferred_element_type=F32)


def dot_tn(a, b):
    return lax.dot_general(a, b, (((0,), (0,)), ((), ())), preferred_element_type=F32)


def store_a_to_b(dst, frame, value):
    shaped = value.reshape(2, 4, 2, 8, value.shape[-1])
    for qr in range(2):
        for qc in range(2):
            dst[qr * 2 + qc, pl.ds(pl.multiple_of(frame * 4, 4), 4)] = shaped[qr, :, qc]


def store_b_to_a(dst, window, value):
    shaped = value.reshape(FRAMES, 4, 8, value.shape[-1])
    qr, qc = lax.div(window, 2), lax.rem(window, 2)
    for frame in range(FRAMES):
        dst[frame * 2 + qr, :, qc] = shaped[frame]


def store_a_to_a(dst, frame, value):
    shaped = value.reshape(2, 4, 2, 8, value.shape[-1])
    for qr in range(2):
        dst[frame * 2 + qr] = shaped[qr]


def hand_out(groups, out, send_sem, recv_sem, x, core, sibling):
    copies = []
    for i in range(2):
        copies.append(
            remote(
                groups.at[5 * x + 3 - 3 * core + i],
                out.at[1 + 2 * i],
                send_sem.at[i],
                recv_sem.at[i],
                sibling,
            )
        )
        copies[-1].start()
    for i in range(3):
        out[2 * i] = groups[5 * x + 2 * core + i]
    for copy in copies:
        copy.wait()


def forward_kernel(windows, last, names, *refs):
    r = dict(zip(names, refs, strict=True))
    stream, mask, bias, y_out = r["stream"], r["mask"], r["bias"], r["y"]
    mod = r["mod"].at[1] if last else r["mods"].at[0]
    qkv_w, proj_w, fc1_w, fc2_w = r["qkv_w"], r["proj_w"], r["fc1_w"], r["fc2_w"]
    h1, qkv, prob, att, ao = r["h1_v"], r["qkv_s_v"], r["prob_v"], r["att_v"], r["ao_v"]
    x1, h2, act, dg, mo = r["x1_v"], r["h2_v"], r["act_v"], r["dg_v"], r["mo_v"]
    ps1s, ps1r, ps2s, ps2r = r["ps1s"], r["ps1r"], r["ps2s"], r["ps2r"]
    xs1s, xs1r, xs2s, xs2r = r["xs1s"], r["xs1r"], r["xs2s"], r["xs2r"]
    part1, part2, out_sem = r["part1"], r["part2"], r["out_sem"]
    h1_sem, h2_sem, ps1_sem, ps2_sem = r["h1_sem"], r["h2_sem"], r["ps1_sem"], r["ps2_sem"]
    xs1_sem, xs2_sem = r["xs1_sem"], r["xs2_sem"]
    width = h1.shape[1]
    half = width // 2
    model = h1.shape[2]
    heads = bias.shape[0]
    inner = proj_w.shape[0]
    head_dim = inner // heads
    piece = half // FRAMES
    x, core, sibling, partner, diagonal = places()
    own = pl.ds(pl.multiple_of(core * half, 16), half)
    theirs = pl.ds(pl.multiple_of((1 - core) * half, 16), half)

    weights = qkv_copies(r["qkv"], qkv_w, r["qkv_sem"]) + [
        pltpu.make_async_copy(r[name], r[name + "_w"], r["w_sem"].at[i])
        for i, name in enumerate(("proj", "fc1", "fc2"))
    ]
    if not last:
        firsts = index_copies(r) + [
            pltpu.make_async_copy(r["ada_" + b], r["ada_v"].at[i], r["ada_sem"].at[i])
            for i, b in enumerate("ab")
        ]
        for copy in firsts:
            copy.start()
    for copy in weights:
        copy.start()
    saves = [
        (r[name + "_v"], r[name])
        for name in ("h1", "qkv_s", "prob", "att", "ao", "x1", "h2", "act", "dg", "mo")
        + (("gm",) if last else ())
    ]

    def save(which, f):
        src, dst = saves[which]
        return pltpu.make_async_copy(src.at[f], dst.at[f], out_sem.at[which, f])

    def share(buf, sem, f, rows):
        return remote(buf.at[f, own], buf.at[f, rows], sem.at[0, f], sem.at[1, f], sibling)

    def to_sibling(src, dst, sem, f):
        return remote(src.at[f], dst.at[f], sem.at[0, f], sem.at[1, f], sibling)

    def to_partner(src, dst, sem, f):
        return remote(src.at[f], dst.at[f], sem.at[0, f], sem.at[1, f], partner)

    greet((sibling, partner, diagonal))
    rows_start, rows_wait, rows_drain = own_rows(
        r["rows"],
        r["top_rows"] if last else stream,
        (r["rows_send"], r["rows_local"], r["rows_recv"]),
        x,
        core,
        sibling,
        partner,
        diagonal,
    )
    later = (x == 0) & (core == 1)
    if last:
        rows_start()
    else:
        pl.when(jnp.logical_not(later))(rows_start)
        me = lax.axis_index("mp")
        pieces, mods, parts = r["pieces"], r["mods"], r["parts"]
        cond = r["cond"][...].astype(F32)
        cond_act = (cond / (1.0 + jnp.exp(-cond))).astype(BF16)
        for i in range(2):
            r["cond_act"][pl.ds(i, 1)] = cond_act[:, i * 512 : i * 512 + 512].astype(F32)
        spread = jnp.broadcast_to(cond_act, (16, model))
        for i in range(2):
            firsts[-2 + i].wait()
            product = dot(spread, r["ada_v"][i])
            for j in range(3):
                parts[i, pl.ds(j, 1)] = product[0:1, j * 512 : j * 512 + 512]
        mod_copies = []
        for i in range(3):
            mod_copies.append(
                remote(
                    parts,
                    pieces.at[me],
                    r["mod_sem"].at[0, i],
                    r["mod_sem"].at[1, i],
                    lax.rem(me + 1 + i, 4),
                )
            )
            mod_copies[-1].start()
        pieces[me] = parts[...]
        for copy in firsts[:-2]:
            copy.wait()
        place_index(r["index_v"], r["index"], 6, 2)
        place_index(r["next_index_v"], r["next_index"], 5, FRAMES)
        lane_table(r["table"], r["table_v"])
        lane_table(r["next_table"], r["next_table_v"])
        rows16(width, lambda rows: lookup(r["index"], r["table_v"], bias, rows))
        pl.when(later)(rows_start)
        for copy in mod_copies:
            copy.wait()
        for i in range(12):
            half_row = pl.ds(i % 2 * 512, 512)
            for b in range(2):
                mods[b, pl.ds(i // 2, 1), half_row] = pieces[i // 3, b, pl.ds(i % 3, 1)]

    def own_stream(f):
        return stream[f].astype(F32).reshape(half, model)

    def first_norm(f):
        if not last:
            rows_wait(2 * f)
            rows_wait(2 * f + 1)
            keep_stream(f).start()
        normed, _ = norm(own_stream(f))
        h1[f, own] = (normed * (1.0 + mod[1:2]) + mod[0:1]).astype(BF16)
        share(h1, h1_sem, f, own).start()

    def keep_stream(f):
        return pltpu.make_async_copy(stream.at[f], r["stream_s"].at[f], r["top_sem"].at[f])

    loop(windows if last else 2, first_norm)
    for copy in weights[:4]:
        copy.wait()

    def top():
        def place(f):
            rows_wait(2 * f)
            rows_wait(2 * f + 1)
            store_a_to_b(r["top_v"], f, r["top_rows"][f].astype(F32).reshape(-1, model))

        loop(FRAMES, place)

        def give(f):
            grad = r["top_v"][f].reshape(half, model)
            pltpu.make_async_copy(r["top_v"].at[f], r["top"].at[f], r["top_sem"].at[f]).start()
            r["gm_v"][f, own] = (mod[5:6] * grad).astype(BF16)
            share(r["gm_v"], r["gm_sem"], f, own).start()

        loop(windows, give)

    def top_weights():
        def some(f):
            share(r["gm_v"], r["gm_sem"], f, theirs).wait_recv()
            save(10, f).start()

        loop(windows, some)
        grads, acts = r["gm_v"][...].reshape(-1, model), act[...].reshape(-1, act.shape[2])
        fc2_grad = r["fc2_grad_v"]
        for start in range(0, acts.shape[1], 256):
            c = slice(start, start + 256)
            piece = dot_tn(grads, acts[:, c]).astype(BF16)
            fc2_grad[..., c] = piece.reshape(*fc2_grad.shape[:-1], 256)
        grad_copy().start()

    def grad_copy():
        return pltpu.make_async_copy(r["fc2_grad_v"], r["fc2_grad"], r["w_sem"].at[4])

    lane_head = lax.div(lax.broadcasted_iota(jnp.int32, (width, inner), 1), head_dim)

    def attention(f):
        share(h1, h1_sem, f, theirs).wait_recv()
        save(0, f).start()
        qkv[f] = dot(h1[f], qkv_w[...]).astype(BF16)
        save(1, f).start()
        queries = qkv[f, :, :inner] * BF16(head_dim ** (-0.5))
        keys = qkv[f, :, inner : 2 * inner]
        vals = qkv[f, :, 2 * inner :]
        zero = jnp.zeros((), BF16)
        out = jnp.zeros((width, inner), F32)
        for h in range(heads):
            scores = dot_nt(jnp.where(lane_head == h, queries, zero), keys)
            scores = scores + bias[h, :, :width].astype(F32) + mask[f]
            weight = jnp.exp(scores - jnp.max(scores, axis=-1, keepdims=True))
            p = (weight * (1.0 / jnp.sum(weight, axis=-1, keepdims=True))).astype(BF16)
            prob[f, h] = p
            out = out + dot(p, jnp.where(lane_head == h, vals, zero))
        att[f] = out.astype(BF16)
        save(2, f).start()
        save(3, f).start()

        ps1s[f] = dot(att[f, theirs], proj_w[...]).astype(BF16)
        to_sibling(ps1s, ps1r, ps1_sem, f).start()
        part1[...] = dot(att[f, own], proj_w[...])

    def sum_first(f):
        to_sibling(ps1s, ps1r, ps1_sem, f).wait_recv()
        xs1s[f] = (part1[...] + ps1r[f].astype(F32)).astype(BF16)
        to_partner(xs1s, xs1r, xs1_sem, f).start()

    def sum_second(f):
        to_sibling(ps2s, ps2r, ps2_sem, f).wait_recv()
        xs2s[f] = (part2[...] + ps2r[f].astype(F32)).astype(BF16)
        second_xs(f, 1 - x).start()

    def second_xs(f, holder):
        rows = pl.ds(0, half)
        if last:
            rows = pl.ds(pl.multiple_of(2 * piece * holder, piece), 3 * piece)
        return remote(
            xs2s.at[f, rows], xs2r.at[f, rows], xs2_sem.at[0, f], xs2_sem.at[1, f], partner
        )

    def middle(f):
        to_partner(xs1s, xs1r, xs1_sem, f).wait_recv()

        total = xs1s[f].astype(F32) + xs1r[f].astype(F32)
        mid = own_stream(f) + mod[2:3] * total
        ao[f] = total.astype(BF16)
        x1[f] = mid
        normed, _ = norm(mid)
        h2[f, own] = (normed * (1.0 + mod[4:5]) + mod[3:4]).astype(BF16)
        share(h2, h2_sem, f, own).start()
        save(4, f).start()
        save(5, f).start()

    def mlp(f):
        share(h2, h2_sem, f, theirs).wait_recv()
        save(6, f).start()

        for start in range(0, act.shape[2], 256):
            c = pl.ds(start, 256)
            u = dot(h2[f], fc1_w[:, c])
            sq = u * u
            t = jnp.tanh(GELU_K * (u + GELU_C * u * sq))
            one_t = 0.5 * (1.0 + t)
            act[f, :, c] = (u * one_t).astype(BF16)
            slope = one_t + (0.5 * GELU_K) * u * (1.0 - t * t) * (1.0 + (3.0 * GELU_C) * sq)
            dg[f, :, c] = slope.astype(BF16)
        save(7, f).start()
        save(8, f).start()
        ps2s[f] = dot(act[f, theirs], fc2_w[...]).astype(BF16)
        to_sibling(ps2s, ps2r, ps2_sem, f).start()
        part2[...] = dot(act[f, own], fc2_w[...])

    def finish(f):
        second_xs(f, x).wait_recv()
        if last:
            keep = pl.ds(pl.multiple_of(2 * piece * x, piece), 3 * piece)
            total = xs2s[f, keep].astype(F32) + xs2r[f, keep].astype(F32)
            result = x1[f, keep] + mod[5:6] * total
            mo[f] = jnp.zeros((half, model), BF16)
            qr, qc = lax.div(f, 2), lax.rem(f, 2)
            for i in range(3):
                frame = 2 * x + i
                counted = (frame != 2) | (qr == x)
                cut = slice(i * piece, (i + 1) * piece)
                rows = pl.ds(pl.multiple_of((2 * x + i) * piece, piece), piece)
                mo[f, rows] = jnp.where(counted, total[cut], 0.0).astype(BF16)
                r["groups"][frame * 2 + qr, :, qc] = result[cut].reshape(4, 8, model)
        else:
            total = xs2s[f].astype(F32) + xs2r[f].astype(F32)
            mo[f] = total.astype(BF16)
            store_a_to_b(y_out, f, x1[f] + mod[5:6] * total)
        save(9, f).start()

    def first_step(t):
        attention(t)
        sum_first(t)
        if not last:

            @pl.when(t + 2 < windows)
            def _():
                first_norm(t + 2)

    def second_step(t):
        @pl.when(t + 1 < windows)
        def _():
            middle(t + 1)

        mlp(t)
        sum_second(t)

    def last_step(t):
        if not last:
            blocks = r["next_index"].shape[0] // 16
            each = -(-blocks // windows)

            def next_bias(i):
                block = t * each + i

                @pl.when(block < blocks)
                def _():
                    rows = pl.ds(pl.multiple_of(block * 16, 16), 16)
                    lookup(r["next_index"], r["next_table_v"], r["next_bias"], rows)

            loop(each, next_bias)
        finish(t)

    loop(windows, first_step)
    if last:
        top()
    for copy in weights[4:]:
        copy.wait()
    middle(0)
    loop(windows, second_step)
    if last:
        top_weights()
    loop(windows, last_step)
    if last:
        hand_out(r["groups"], y_out, r["hand_sem"].at[0], r["hand_sem"].at[1], x, core, sibling)

    def drain(f):
        for which in range(len(saves)):
            save(which, f).wait()
        share(h1, h1_sem, f, own).wait_send()
        share(h2, h2_sem, f, own).wait_send()
        to_sibling(ps1s, ps1r, ps1_sem, f).wait_send()
        to_sibling(ps2s, ps2r, ps2_sem, f).wait_send()
        to_partner(xs1s, xs1r, xs1_sem, f).wait_send()
        second_xs(f, 1 - x).wait_send()
        if last:
            share(r["gm_v"], r["gm_sem"], f, own).wait_send()
            pltpu.make_async_copy(r["top_v"].at[f], r["top"].at[f], r["top_sem"].at[f]).wait()
        else:
            keep_stream(f).wait()

    loop(windows, drain)
    rows_drain()
    if last:
        grad_copy().wait()


def block_forward(rows, first, then, params, mask, size, collective_id):
    last = then is not None
    qkv_w, proj_w, fc1_w, fc2_w = params
    windows, _, width = mask.shape
    model = rows.shape[-1]
    half = width // 2
    heads = then[2].shape[0] if last else first["table"].shape[0]
    inner = proj_w.shape[0]
    hidden = fc1_w.shape[1]
    sds = jax.ShapeDtypeStruct
    ins = {"rows": (rows, ANY), "mask": (mask, VM)}
    outs, scratch = {}, {}
    if last:
        ins.update({name: (v, VM) for name, v in zip(("stream", "mod", "bias"), then, strict=True)})
    else:
        for name, value in first.items():
            whole = name in ("ada_a", "ada_b", "spatial", "joint")
            ins[name] = (value, ANY if whole else VM)
        spatial, joint = first["spatial"], first["joint"]
        next_shape = (joint.shape[0], -(-joint.shape[1] // 128) * 128)
        outs["mods"] = (sds((2, 6, model), F32), VM)
        outs["cond_act"] = (sds((2, 512), F32), VM)
        outs["index"] = (sds(spatial.shape, jnp.int32), VM)
        outs["next_index"] = (sds(next_shape, jnp.int32), VM)
        outs["next_bias"] = (sds((heads, *next_shape), BF16), VM)
        for name in ("table", "next_table"):
            count = -(-first[name].shape[1] // 128)
            scratch[name + "_v"] = pltpu.VMEM((heads, count, 128), F32)
        scratch["index_v"] = pltpu.VMEM(spatial.shape, jnp.int32)
        scratch["next_index_v"] = pltpu.VMEM(joint.shape, jnp.int32)
        scratch["ada_v"] = pltpu.VMEM((2, *first["ada_a"].shape), BF16)
        scratch["parts"] = pltpu.VMEM((2, 3, 512), F32)
        scratch["index_sem"] = dma((4 + 2 * FRAMES,))
        scratch["ada_sem"] = dma((2,))
        outs["stream_s"] = (sds((windows, 2, half // 2, model), BF16), ANY)
        scratch["stream"] = pltpu.VMEM((windows, 2, half // 2, model), BF16)
        scratch["bias"] = pltpu.VMEM((heads, *spatial.shape), BF16)
        scratch["pieces"] = pltpu.VMEM((4, 2, 3, 512), F32)
        scratch["mod_sem"] = dma((2, 3))
    scratch["rows_send"] = dma((5, 2))
    scratch["rows_local"] = dma((3,))
    scratch["rows_recv"] = dma((2 * FRAMES,))
    for name, value in (("qkv", qkv_w), ("proj", proj_w), ("fc1", fc1_w), ("fc2", fc2_w)):
        ins[name] = (value, ANY)
        shape = (model, 3 * inner) if name == "qkv" else value.shape
        scratch[name + "_w"] = pltpu.VMEM(shape, value.dtype)
    saved = {
        "h1": ((windows, width, model), BF16),
        "qkv_s": ((windows, width, 3 * inner), BF16),
        "prob": ((windows, heads, width, width), BF16),
        "att": ((windows, width, inner), BF16),
        "ao": ((windows, half, model), BF16),
        "x1": ((windows, half, model), F32),
        "h2": ((windows, width, model), BF16),
        "act": ((windows, width, hidden), BF16),
        "dg": ((windows, width, hidden), BF16),
        "mo": ((windows, half, model), BF16),
    }
    if last:
        outs["top"] = (sds((windows, half // 8, 8, model), F32), ANY)
        scratch["top_v"] = pltpu.VMEM((windows, half // 8, 8, model), F32)
        scratch["top_rows"] = pltpu.VMEM((FRAMES, 2, 4 * SIDE, model), BF16)
        saved["gm"] = ((windows, width, model), BF16)
        saved["fc2_grad"] = ((size // 2, 2, model // size, hidden), BF16)
    for name, (shape, dtype) in saved.items():
        outs[name] = (sds(shape, dtype), ANY)
        scratch[name + "_v"] = pltpu.VMEM(shape, dtype)
    if last:
        outs["y"] = (sds((FRAMES, 4, 2, 8, model), F32), VM)
        scratch["groups"] = pltpu.VMEM((2 * FRAMES, 4, 2, 8, model), F32)
    else:
        outs["y"] = (sds((4, FRAMES * 4, 8, model), F32), VM)
    own_all = pltpu.VMEM((windows, half, model), BF16)
    for name in ("ps1s", "ps1r", "xs1s", "xs1r", "ps2s", "ps2r", "xs2s", "xs2r"):
        scratch[name] = own_all
    for name in ("h1", "h2", "gm", "ps1", "ps2", "xs1", "xs2"):
        scratch[name + "_sem"] = dma((2, windows))
    scratch.update(
        part1=pltpu.VMEM((half, model), F32),
        part2=pltpu.VMEM((half, model), F32),
        w_sem=dma((5,)),
        qkv_sem=dma((3,)),
        out_sem=dma((11, windows)),
        top_sem=dma((windows,)),
        hand_sem=dma((2, 2)),
    )
    names = (*ins, *outs, *scratch)
    results = pl.pallas_call(
        functools.partial(forward_kernel, windows, last, names),
        out_shape=[shape for shape, _ in outs.values()],
        in_specs=[spec for _, spec in ins.values()],
        out_specs=[spec for _, spec in outs.values()],
        scratch_shapes=list(scratch.values()),
        compiler_params=pltpu.CompilerParams(
            collective_id=collective_id, has_side_effects=True, vmem_limit_bytes=VMEM_LIMIT
        ),
        name="forward_last" if last else "forward_first",
    )(*[value for value, _ in ins.values()])
    return dict(zip(outs, results, strict=True))


QKV_EARLY = 0
STREAMS = ("dg", "h2", "qkv_s", "prob", "h1", "x1", "ao", "mo", "stream")


def backward_kernel(windows, last, size, names, *refs):
    r = dict(zip(names, refs, strict=True))
    mod, index = r["mod"].at[1 if last else 0], r.get("index")
    grad, part1, part2, gh, gqkv = r["grad"], r["part1"], r["part2"], r["gh"], r["gqkv"]
    fc1_w, fc2_w, qkv_w, proj_w = r["fc1_w"], r["fc2_w"], r["qkv_w"], r["proj_w"]
    gm, rest, wgrad, gbias = r["gm"], r["rest"], r["wgrad"], r["gbias"]
    ga = gm
    ps1s, ps1r, ps2s, ps2r = r["ps1s"], r["ps1r"], r["ps2s"], r["ps2r"]
    xs1s, xs1r, xs2s, xs2r = r["xs1s"], r["xs1r"], r["xs2s"], r["xs2r"]
    buf1, buf2, msum, mtot, mrecv = r["buf1"], r["buf2"], r["msum"], r["mtot"], r["mrecv"]
    _, half, model = grad.shape
    width = 2 * half
    heads = gbias.shape[0]
    inner = proj_w.shape[0]
    head_dim = inner // heads
    hidden = gh.shape[1]
    scale = head_dim ** (-0.5)
    chunk = buf1.shape[-1]
    fc_chunks = hidden // chunk
    rest_chunks = 4 * inner // chunk
    carry_chunks = r["carry"].shape[-1] // chunk
    now = range(QKV_EARLY if last else rest_chunks - 1)
    kinds = {"fc1": 0, "carry": 1, "rest": 2, "fc2": 3}
    sources = {"fc1": fc1_w, "carry": rest, "rest": rest, "fc2": r.get("fc2_grad")}
    if last:
        plan = {
            (0, 1): [("carry", 0)],
            (0, 2): [("carry", 1)],
            (0, 3): [("carry", 2)],
            (1, 0): [("carry", 3), ("fc1", 0)],
            (1, 1): [("fc1", 1)],
            (1, 2): [("fc1", 2)],
            (1, 3): [("fc1", 3), ("rest", 3)],
        }
    else:
        plan = {
            (0, 1): [("carry", 0)],
            (0, 2): [("carry", 1)],
            (0, 4): [("fc2", 0)],
            (1, 0): [("fc2", 1), ("fc2", 2)],
            (1, 1): [("fc2", 3), ("fc1", 0)],
            (1, 2): [("fc1", 1)],
            (1, 3): [("fc1", 2)],
            (1, 4): [("fc1", 3)],
        }
    if carry_chunks == 3:
        plan[0, 3] = [("carry", 2)]
    x, core, sibling, partner, diagonal = places()
    own = pl.ds(pl.multiple_of(core * half, 16), half)
    theirs = pl.ds(pl.multiple_of((1 - core) * half, 16), half)
    lines = size // 2
    here = lax.axis_index("dp")
    line, side = lax.div(here, 2), lax.rem(here, 2)

    targets = {
        "grad_y": grad,
        "gm_s": gm,
        "carry": rest.at[..., pl.ds(0, r["carry"].shape[-1])],
        "fc2": fc2_w,
        "fc1": fc1_w,
        "act": r.get("act_v"),
        "proj": proj_w,
        "att": r["att_v"],
    }
    loads = {
        name: pltpu.make_async_copy(r[name], target, r["w_sem"].at[i])
        for i, (name, target) in enumerate(targets.items())
        if name in r
    }
    qkv_loads = qkv_copies(r["qkv"], qkv_w, r["qkv_sem"])
    for_mlp = ("dg", "h2")
    for_attention = ("qkv_s", "prob", "h1")
    for_middle = ("x1", "ao", "mo")

    def fetch(name, f):
        slot = lax.rem(f, 2)
        sem = r["in_sem"].at[STREAMS.index(name), slot]
        return pltpu.make_async_copy(r[name].at[f], r[name + "_v"].at[slot], sem)

    def share(buf, sem, f, rows):
        return remote(buf.at[f, own], buf.at[f, rows], sem.at[0, f], sem.at[1, f], sibling)

    def to_sibling(src, dst, sem, f):
        slot = lax.rem(f, 2)
        return remote(src.at[slot], dst.at[slot], sem.at[0, slot], sem.at[1, slot], sibling)

    def first_ps(f):
        return to_sibling(ps1s, ps1r, r["ps1_sem"], f)

    def second_ps(f):
        return to_sibling(ps2s, ps2r, r["ps2_sem"], f)

    def first_xs(f):
        sem = r["xs1_sem"]
        return remote(xs1s.at[f], xs1r.at[f], sem.at[0, f], sem.at[1, f], partner)

    def second_xs(f):
        sem, slot = r["xs2_sem"], lax.rem(f, 2)
        return remote(xs2s.at[slot], xs2r.at[f], sem.at[0, slot], sem.at[1, f], partner)

    def along_dp(src, dst, send_sem, recv_sem, other):
        return pltpu.make_async_remote_copy(
            src_ref=src,
            dst_ref=dst,
            send_sem=send_sem,
            recv_sem=recv_sem,
            device_id={"dp": other},
            device_id_type=MESH,
        )

    def chunk_cols(i):
        return pl.ds(pl.multiple_of(i * chunk, chunk), chunk)

    def across(kind, i):
        k = kinds[kind]
        return along_dp(
            sources[kind].at[:, 1 - side, :, chunk_cols(i)],
            buf1.at[k, i],
            r["across_sem"].at[0, k, i],
            r["across_sem"].at[1, k, i],
            line * 2 + 1 - side,
        )

    def along(kind, i, j):
        k = kinds[kind]
        to = lax.rem(line + 1 + j, lines)
        return along_dp(
            buf1.at[k, i, to],
            buf2.at[k, i, j],
            r["along_sem"].at[0, k, i, j],
            r["along_sem"].at[1, k, i, j],
            to * 2 + side,
        )

    def reduce_side(kind, i):
        k = kinds[kind]
        across(kind, i).wait_recv()
        mine = sources[kind][:, side, :, chunk_cols(i)]
        buf1[k, i] = (mine.astype(F32) + buf1[k, i].astype(F32)).astype(BF16)
        loop(lines - 1, lambda j: along(kind, i, j).start())

    def reduce_line(kind, i):
        k = kinds[kind]
        loop(lines - 1, lambda j: along(kind, i, j).wait_recv())
        return buf1[k, i, line].astype(F32) + jnp.sum(buf2[k, i].astype(F32), axis=0)

    def take_up(phase, f):
        for (when, step), sums in plan.items():
            if when != phase:
                continue

            @pl.when(f == step)
            def _(sums=sums):
                for kind, i in sums:
                    reduce_side(kind, i)

    def drain_sum(kind, i):
        if kind != "carry":
            across(kind, i).wait_send()
        loop(lines - 1, lambda j: along(kind, i, j).wait_send())

    for copy in loads.values():
        copy.start()
    for which in for_mlp:
        fetch(which, 0).start()
    for copy in qkv_loads:
        copy.start()

    barrier = pltpu.get_barrier_semaphore()
    for other in (sibling, partner):
        pl.semaphore_signal(barrier, inc=1, device_id={"mp": other}, device_id_type=MESH)

    def greet_dp(j):
        pl.semaphore_signal(
            barrier, inc=1, device_id={"dp": lax.rem(here + 1 + j, size)}, device_id_type=MESH
        )

    loop(size - 1, greet_dp)
    pl.semaphore_wait(barrier, 1 + size)

    def top(f):
        gm[f, own] = (mod[5:6] * grad[f]).astype(BF16)
        share(gm, r["gm_sem"], f, own).start()

    loads["grad_y"].wait()
    if last:
        loads["gm_s"].wait()
    else:
        loop(windows, top)
    loads["carry"].wait()
    loop(carry_chunks, lambda i: across("carry", i).start())
    msum[...] = jnp.zeros_like(msum)
    gbias[...] = jnp.zeros_like(gbias)
    wgrad[...] = jnp.zeros_like(wgrad)

    lane_head = lax.div(lax.broadcasted_iota(jnp.int32, (width, inner), 1), head_dim)
    zero = jnp.zeros((), BF16)

    def flat(weight):
        value = weight[...]
        return value.reshape(-1, value.shape[-1])

    def mlp_back(f):
        slot = lax.rem(f, 2)
        for which in for_mlp:
            fetch(which, f).wait()
        if not last:

            @pl.when(f == 0)
            def _():
                share(gm, r["gm_sem"], f, theirs).wait_recv()

        gh[...] = (dot_nt(gm[f], flat(fc2_w)) * r["dg_v"][slot].astype(F32)).astype(BF16)

        @pl.when(f >= 2)
        def _():
            first_ps(f - 2).wait_send()

        ps1s[slot] = dot_nt(gh[theirs], flat(fc1_w)).astype(BF16)
        first_ps(f).start()
        part1[...] = dot_nt(gh[own], flat(fc1_w))

    def sum_first(f):
        slot = lax.rem(f, 2)
        first_ps(f).wait_recv()
        xs1s[f] = (part1[...] + ps1r[slot].astype(F32)).astype(BF16)
        first_xs(f).start()

    def fc2_weights():
        loop(windows - 1, lambda f: share(gm, r["gm_sem"], f + 1, theirs).wait_recv())
        loads["act"].wait()
        grads, acts = gm[...].reshape(-1, model), r["act_v"][...].reshape(-1, hidden)
        out = r["fc2_grad"]
        for i in range(fc_chunks):
            c = slice(i * chunk, (i + 1) * chunk)
            out[..., c] = dot_tn(grads, acts[:, c]).astype(BF16).reshape(*out.shape[:-1], chunk)
            across("fc2", i).start()

    def mlp_weights(f):
        slot = lax.rem(f, 2)
        for start in range(0, hidden, 512):
            c = pl.ds(start, 512)
            wgrad[:, c] += dot_tn(r["h2_v"][slot], gh[:, c])

    def fold(values):
        return values.reshape(half // 8, 8, model).sum(axis=0)

    def middle(f):
        slot = lax.rem(f, 2)
        for which in for_middle:
            fetch(which, f).wait()
        first_xs(f).wait_recv()
        grad_h = xs1s[f].astype(F32) + xs1r[f].astype(F32)
        normed, inv = norm(r["x1_v"][slot])
        gy = grad[f]
        grad_mid = gy + norm_back(normed, inv, grad_h * (1.0 + mod[4:5]))
        msum[2] += fold(grad_mid * r["ao_v"][slot].astype(F32))
        msum[3] += fold(grad_h)
        msum[4] += fold(grad_h * normed)
        msum[5] += fold(gy * r["mo_v"][slot].astype(F32))
        grad[f] = grad_mid
        ga[f, own] = (mod[2:3] * grad_mid).astype(BF16)
        share(ga, r["ga_sem"], f, own).start()

    def attention_back(f):
        slot = lax.rem(f, 2)
        qkv = r["qkv_s_v"]
        for which in for_attention:
            fetch(which, f).wait()

        @pl.when(f < windows - 1)
        def _():
            share(ga, r["ga_sem"], f, theirs).wait_recv()

        grad_att = dot_nt(ga[f], proj_w[...]).astype(BF16)
        grad_att_t = grad_att.T
        queries_t = qkv[slot, :, :inner].T
        keys = qkv[slot, :, inner : 2 * inner] * BF16(scale)
        vals = qkv[slot, :, 2 * inner :]
        grad_q = jnp.zeros((width, inner), F32)
        grad_k, grad_v = [], []
        for h in range(heads):
            part = slice(h * head_dim, (h + 1) * head_dim)
            p = r["prob_v"][slot, h]
            grad_p = dot_nt(jnp.where(lane_head == h, grad_att, zero), vals)
            pf = p.astype(F32)
            weighted = pf * grad_p
            grad_s = weighted - pf * jnp.sum(weighted, axis=-1, keepdims=True)
            gbias[h, :, :width] += grad_s
            rounded = grad_s.astype(BF16)
            grad_q = grad_q + dot(rounded, jnp.where(lane_head == h, keys, zero))
            grad_v.append(dot(grad_att_t[part], p))
            grad_k.append(dot(queries_t[part], rounded) * scale)
        gqkv[:, :inner] = grad_q.astype(BF16)
        gqkv[:, inner : 2 * inner] = jnp.concatenate(grad_k, axis=0).astype(BF16).T
        gqkv[:, 2 * inner :] = jnp.concatenate(grad_v, axis=0).astype(BF16).T

        @pl.when(f >= 2)
        def _():
            second_ps(f - 2).wait_send()

        ps2s[slot] = dot_nt(gqkv[theirs], qkv_w[...]).astype(BF16)
        second_ps(f).start()
        part2[...] = dot_nt(gqkv[own], qkv_w[...])

    def sum_second(f):
        slot = lax.rem(f, 2)
        second_ps(f).wait_recv()

        @pl.when(f >= 2)
        def _():
            second_xs(f - 2).wait_send()

        xs2s[slot] = (part2[...] + ps2r[slot].astype(F32)).astype(BF16)
        second_xs(f).start()

    def attention_weights(f):
        slot = lax.rem(f, 2)
        for start in range(0, 3 * inner, 384):
            c = pl.ds(start, 384)
            wgrad[:, c] += dot_tn(r["h1_v"][slot], gqkv[:, c])

    def proj_weights():
        share(ga, r["ga_sem"], windows - 1, theirs).wait_recv()
        loads["att"].wait()
        piece = dot_tn(ga[...].reshape(-1, model), r["att_v"][...].reshape(-1, inner))
        for i in range(carry_chunks):
            across("carry", i).wait_send()
        c = pl.ds(3 * inner, inner)
        rest[..., c] = piece.astype(BF16).reshape(*rest.shape[:-1], inner)
        across("rest", rest_chunks - 1).start()

    def finish(f):
        slot = lax.rem(f, 2)
        fetch("stream", f).wait()
        second_xs(f).wait_recv()
        grad_h = xs2s[slot].astype(F32) + xs2r[f].astype(F32)
        normed, inv = norm(r["stream_v"][slot].astype(F32).reshape(half, model))
        msum[0] += fold(grad_h)
        msum[1] += fold(grad_h * normed)
        grad_x = grad[f] + norm_back(normed, inv, grad_h * (1.0 + mod[1:2]))
        if last:
            store_b_to_a(r["gx"], f, grad_x)
        else:
            grad[f] = grad_x

    def first_step(f):
        @pl.when(f + 1 < windows)
        def _():
            for which in for_mlp:
                fetch(which, f + 1).start()

        @pl.when(f == 0)
        def _():
            loads["fc2"].wait()
            loads["fc1"].wait()

        mlp_back(f)
        mlp_weights(f)
        sum_first(f)
        if not last:
            pl.when(f == 0)(fc2_weights)
        take_up(0, f)

    loop(windows, first_step)
    if not last:
        loop(windows, lambda f: share(gm, r["gm_sem"], f, own).wait_send())

    for which in (*for_attention, *for_middle, "stream"):
        fetch(which, 0).start()
    shape = fc1_w.shape
    fc1_w[...] = wgrad[:, :hidden].astype(BF16).reshape(shape)
    loop(fc_chunks, lambda i: across("fc1", i).start())
    wgrad[:, : 3 * inner] = jnp.zeros((model, 3 * inner), F32)
    for which in for_middle:
        fetch(which, 1).start()
    middle(0)
    for copy in (loads["proj"], *qkv_loads):
        copy.wait()

    gate = r["gate"]
    if last:
        sems = r["mod_sem"]
        gate_copy = remote(gate.at[0], gate.at[1], sems.at[2], sems.at[3], partner)

    def give_gate():
        for i in range(2):
            c = slice(i * 512, i * 512 + 512)
            gate[0, pl.ds(i, 1)] = jnp.sum(msum[5, :, c], axis=0, keepdims=True)
        gate_copy.start()

    def second_step(f):
        @pl.when(f + 1 < windows)
        def _():
            for which in for_attention:
                fetch(which, f + 1).start()
            middle(f + 1)

        @pl.when(f + 2 < windows)
        def _():
            for which in for_middle:
                fetch(which, f + 2).start()

        attention_back(f)
        attention_weights(f)
        sum_second(f)
        pl.when(f == windows - 2)(proj_weights)
        if last:
            pl.when(f == windows - 2)(give_gate)

        @pl.when(f >= 1)
        def _():
            finish(f - 1)

        @pl.when((f >= 1) & (f + 1 < windows))
        def _():
            fetch("stream", f + 1).start()

        @pl.when(f == 0)
        def _():
            fetch("stream", 1).start()

        take_up(1, f)

    loop(windows, second_step)

    shape = (*rest.shape[:-1], 3 * inner)
    rest[..., pl.ds(0, 3 * inner)] = wgrad[:, : 3 * inner].astype(BF16).reshape(shape)
    for i in now:
        across("rest", i).start()
    if last:
        later = pl.ds(len(now) * chunk, (rest_chunks - 1 - len(now)) * chunk)
        carry = pltpu.make_async_copy(rest.at[..., later], r["carry_next"], r["w_sem"].at[8])
        carry.start()
    if not last:
        wide = r["gbias_b"].shape[2]
        tall = r["gbias_b"].shape[1]

        def other_place(h):
            return pl.ds(h // 2 * tall, tall), pl.ds(h % 2 * wide, wide)

        other_loads = []
        for h in range(heads):
            other_loads.append(
                pltpu.make_async_copy(
                    r["gbias_b"].at[h], wgrad.at[other_place(h)], r["other_sem"].at[h]
                )
            )
            other_loads[-1].start()
        mine = [gbias.at[h] for h in range(heads)]
        other = [wgrad.at[other_place(h)] for h in range(heads)]
        scatter(index, mine, r["table"])
    else:
        for i in range(2):
            scatter(index, [gbias.at[h] for h in range(heads)], r["table_part"], i, 4)
    take_up(2, 0)
    finish(windows - 1)
    for i in range(12):
        c = slice(i % 2 * 512, i % 2 * 512 + 512)
        mtot[i // 3, pl.ds(i % 3, 1)] = jnp.sum(msum[i // 2, :, c], axis=0, keepdims=True)
    if last:
        gate_copy.wait()
        mtot[3, 1:3] = gate[0] + gate[1]
    mod_copy = remote(mtot, mrecv, r["mod_sem"].at[0], r["mod_sem"].at[1], sibling)
    mod_copy.start()
    small, everyone, tabs = r.get("small"), r.get("everyone"), r.get("tabs")

    def give_small(j):
        return along_dp(
            small,
            everyone.at[here],
            r["small_sem"].at[0, j],
            r["small_sem"].at[1, j],
            lax.rem(here + 1 + j, size),
        )

    def give_table(j):
        to = lax.rem(here + 1 + j, size)
        sem = r["table_sem"]
        return along_dp(tabs.at[to], r["tab_parts"].at[j], sem.at[0, j], sem.at[1, j], to)

    def give_sum(j):
        to = lax.rem(here + 1 + j, size)
        sem = r["sum_sem"]
        return along_dp(r["tab_sum"], r["tables"].at[here], sem.at[0, j], sem.at[1, j], to)

    def start_mods():
        mod_copy.wait()
        me = lax.axis_index("mp")
        small[0:3] = mtot[me] + mrecv[me]
        small[3:6] = r["mod_b"][...]
        small[6:8] = r["cond"][...]
        everyone[here] = small[...]
        loop(size - 1, lambda j: give_small(j).start())

    def start_tables():
        each = tabs.shape[1]
        whole = r["whole_table"]
        whole[...] = jnp.zeros_like(whole)
        base = 0
        for table in (r["table"], r["table_b"]):
            rows, columns = table.shape
            whole[:rows, base : base + columns] = table[...]
            base += columns
        for i in range(size):
            tabs[i] = whole[i * each : (i + 1) * each]
        loop(size - 1, lambda j: give_table(j).start())

    def finish_tables():
        loop(size - 1, lambda j: give_table(j).wait_recv())
        total = tabs[here] + jnp.sum(r["tab_parts"][...], axis=0)
        r["tab_sum"][...] = total
        r["tables"][here] = total
        give_ada()
        loop(size - 1, lambda j: give_sum(j).start())

    def give_ada():
        loop(size - 1, lambda j: give_small(j).wait_recv())
        rows = r["ada_a_out"].shape[0]
        lane = lax.broadcasted_iota(jnp.int32, (rows, model), 1)
        row = lax.broadcasted_iota(jnp.int32, (rows, model), 0) + here * rows
        chosen = jnp.where(lane == row, 1.0, 0.0).astype(BF16)
        conds = [everyone[:, 6 + i, :].astype(BF16) for i in range(2)]
        mine = dot_nt(chosen[:, :512], conds[0]) + dot_nt(chosen[:, 512:], conds[1])
        for i in range(6):
            out = r["ada_a_out" if i < 3 else "ada_b_out"]
            out[:, pl.ds(i % 3 * 512, 512)] = jnp.dot(
                mine, everyone[:, i, :], precision=HIGHEST, preferred_element_type=F32
            )

    def finish_sums():
        loop(size - 1, lambda j: give_sum(j).wait_recv())
        whole, tables = r["whole_table"], r["tables"]
        each = tables.shape[1]
        for i in range(size):
            whole[i * each : (i + 1) * each] = tables[i]
        turned = whole[...].T
        base = 0
        for name, table in (("table_a_out", r["table"]), ("table_b_out", r["table_b"])):
            out, lows = r[name], table.shape[0]
            groups = table.shape[1] // heads
            for h in range(heads):
                for g in range(-(-out.shape[1] // lows)):
                    count = min(lows, out.shape[1] - g * lows)
                    row = base + h * groups + g
                    out[pl.ds(h, 1), pl.ds(g * lows, count)] = turned[row : row + 1, :count]
            base += heads * groups
        for give in (give_small, give_table, give_sum):
            loop(size - 1, lambda j, give=give: give(j).wait_send())

    hands = []
    if not last:
        gx = r["gx"]

        def group(j):
            which = 5 * x + j
            rows = pl.ds(pl.multiple_of(lax.rem(which, 2) * 64, 64), 64)
            return lax.div(which, 2), rows

        for i in range(2):
            f, rows = group(3 - 3 * core + i)
            hands.append(
                remote(
                    grad.at[f, rows],
                    gx.at[1 + 2 * i],
                    r["hand_sem"].at[0, i],
                    r["hand_sem"].at[1, i],
                    sibling,
                )
            )
            hands[-1].start()
        for i in range(3):
            f, rows = group(2 * core + i)
            gx[2 * i] = grad[f, rows]

    if last:
        for i in now:
            reduce_side("rest", i)
    else:
        for copy in other_loads:
            copy.wait()
        reduce_side("rest", rest_chunks - 1)
        r["table_b"][...] = r["table_part"][...]
        for i in range(2, 4):
            scatter(r["index_b"], other, r["table_b"], i, 4)
            if i == 2:
                start_mods()
            else:
                start_tables()
            reduce_side("rest", i - 2)
        reduce_side("rest", 2)
    outputs = [
        ("carry", range(carry_chunks)),
        ("fc1", range(fc_chunks)),
        ("rest", (rest_chunks - 1, *now)),
    ]
    if not last:
        outputs.insert(1, ("fc2", range(fc_chunks)))

    def finish_chunk(kind, i):
        value = reduce_line(kind, i)
        if kind == "fc1":
            r["fc1_out"][:, pl.ds(i * chunk, chunk)] = value
        elif kind == "fc2" or (last and kind == "carry"):
            r["fc2_out"][pl.ds(i * chunk, chunk)] = value.T
        else:
            piece = i if kind == "rest" else 3 - carry_chunks + i
            to = "_b_out" if kind == "carry" else "_out"
            if piece < 3:
                r["qkv" + to][piece] = value
            else:
                r["proj_out"][...] = value.T

    if not last:
        if QKV_EARLY:
            r["qkv_b_out"][pl.ds(0, QKV_EARLY)] = r["early"][...]
    for kind, chunks in outputs:
        if kind == "rest" and not last:
            finish_tables()
        for i in chunks:
            finish_chunk(kind, i)
    if last:
        carry.wait()
        mod_copy.wait()
        me = lax.axis_index("mp")
        r["mod_out"][...] = mtot[me] + mrecv[me]
    else:
        finish_sums()
    for copy in hands:
        copy.wait()

    def drain(f):
        share(ga, r["ga_sem"], f, own).wait_send()
        first_xs(f).wait_send()

    loop(windows, drain)
    for f in range(windows - 2, windows):
        for copy in (first_ps(f), second_ps(f), second_xs(f)):
            copy.wait_send()

    for kind, chunks in outputs:
        for i in chunks:
            drain_sum(kind, i)


def block_backward(
    stream, grad_y, mod, params, kept, index, table_lens, carry, sums, size, collective_id
):
    last = "gm" in kept
    qkv_w, proj_w, fc1_w, fc2_w = params
    windows, half, model = kept["x1"].shape
    width = 2 * half
    heads = kept["prob"].shape[1]
    inner = proj_w.shape[0]
    hidden = fc1_w.shape[1]
    rows = model // size
    lines = size // 2
    chunk = inner
    chunks = max(hidden, 4 * inner) // chunk
    kinds = 3 if last else 4
    groups = [-(-count // lows) for count, lows in zip(table_lens, (64, 128))]
    sds = jax.ShapeDtypeStruct
    sliced = (lines, 2, rows)
    cut = (*sliced, hidden)

    ins, outs, scratch = {}, {}, {}
    ins["grad_y"] = (grad_y, ANY)
    ins["mod"] = (mod, VM)
    ins["index"] = (index, VM)
    for name in STREAMS:
        value = stream if name == "stream" else kept[name]
        ins[name] = (value, ANY)
        scratch[name + "_v"] = pltpu.VMEM((2,) + value.shape[1:], value.dtype)
    ins["att"] = (kept["att"], ANY)
    scratch["att_v"] = pltpu.VMEM(kept["att"].shape, BF16)
    ins["qkv"] = (qkv_w, ANY)
    ins["proj"] = (proj_w, ANY)
    ins["fc1"] = (fc1_w.reshape(cut), ANY)
    ins["fc2"] = (fc2_w.reshape(cut), ANY)
    ins["carry"] = (carry, ANY)
    if last:
        ins["gm_s"] = (kept["gm"], ANY)
        outs["gx"] = (sds((2 * FRAMES, 4, 2, 8, model), F32), VM)
        outs["carry_next"] = (sds((*sliced, (3 - QKV_EARLY) * inner), BF16), ANY)
        if QKV_EARLY:
            outs["qkv_out"] = (sds((QKV_EARLY, rows, inner), F32), VM)
        outs["proj_out"] = (sds((inner, rows), F32), VM)
        outs["gbias"] = (sds((heads, *index.shape), F32), VM)
        outs["table_part"] = (sds((128, heads * groups[1]), F32), VM)
    else:
        ins["act"] = (kept["act"], ANY)
        scratch["act_v"] = pltpu.VMEM(kept["act"].shape, BF16)
        scratch["fc2_grad"] = pltpu.VMEM(cut, BF16)
        scratch["gbias"] = pltpu.VMEM((heads, *index.shape), F32)
        outs["gx"] = (sds((FRAMES, 4 * SIDE, model), F32), VM)
        for to in ("_out", "_b_out"):
            outs["qkv" + to] = (sds((3, rows, inner), F32), VM)
        outs["proj_out"] = (sds((inner, rows), F32), VM)
    outs["fc2_out"] = (sds((hidden, rows), F32), VM)
    outs["fc1_out"] = (sds((rows, hidden), F32), VM)
    if last:
        outs["mod_out"] = (sds((3, 512), F32), VM)
    else:
        each = 128 // size
        names = ("mod_b", "cond", "index_b", "early", "table_part")
        ins.update(
            {name: (v, VM) for name, v in zip(names, sums[:5], strict=True) if v is not None}
        )
        ins["gbias_b"] = (sums[5], ANY)
        for b, count in zip("ab", table_lens, strict=True):
            outs[f"table_{b}_out"] = (sds((heads, count), F32), VM)
            outs[f"ada_{b}_out"] = (sds((rows, 3 * 512), F32), VM)
        scratch.update(
            everyone=pltpu.VMEM((size, 8, 512), F32),
            tables=pltpu.VMEM((size, each, 128), F32),
            whole_table=pltpu.VMEM((128, 128), F32),
            table=pltpu.VMEM((64, heads * groups[0]), F32),
            table_b=pltpu.VMEM((128, heads * groups[1]), F32),
            other_sem=dma((heads,)),
            small=pltpu.VMEM((8, 512), F32),
            tabs=pltpu.VMEM((size, each, 128), F32),
            tab_parts=pltpu.VMEM((size - 1, each, 128), F32),
            tab_sum=pltpu.VMEM((each, 128), F32),
            small_sem=dma((2, size - 1)),
            table_sem=dma((2, size - 1)),
            sum_sem=dma((2, size - 1)),
        )

    own_all = pltpu.VMEM((windows, half, model), BF16)
    own_two = pltpu.VMEM((2, half, model), BF16)
    own_one = pltpu.VMEM((half, model), F32)
    every = pltpu.VMEM((windows, width, model), BF16)
    scratch.update(
        grad=pltpu.VMEM((windows, half, model), F32),
        part1=own_one,
        part2=own_one,
        gh=pltpu.VMEM((width, hidden), BF16),
        gqkv=pltpu.VMEM((width, 3 * inner), BF16),
        fc1_w=pltpu.VMEM(cut, BF16),
        fc2_w=pltpu.VMEM(cut, BF16),
        qkv_w=pltpu.VMEM((model, 3 * inner), BF16),
        proj_w=pltpu.VMEM(proj_w.shape, BF16),
        gm=every,
        rest=pltpu.VMEM((*sliced, 4 * inner), BF16),
        wgrad=pltpu.VMEM((model, max(4 * inner, hidden)), F32),
        ps1s=own_two,
        ps1r=own_two,
        ps2s=own_two,
        ps2r=own_two,
        xs1s=own_all,
        xs2s=own_two,
        xs1r=own_all,
        xs2r=own_all,
        buf1=pltpu.VMEM((kinds, chunks, lines, rows, chunk), BF16),
        buf2=pltpu.VMEM((kinds, chunks, lines - 1, rows, chunk), BF16),
        msum=pltpu.VMEM((6, 8, model), F32),
        mtot=pltpu.VMEM((4, 3, 512), F32),
        mrecv=pltpu.VMEM((4, 3, 512), F32),
        w_sem=dma((9,)),
        qkv_sem=dma((3,)),
        in_sem=dma((11, 2)),
        gm_sem=dma((2, windows)),
        ga_sem=dma((2, windows)),
        ps1_sem=dma((2, 2)),
        ps2_sem=dma((2, 2)),
        xs1_sem=dma((2, windows)),
        xs2_sem=dma((2, windows)),
        hand_sem=dma((2, 2)),
        mod_sem=dma((4,)),
        gate=pltpu.VMEM((2, 2, 512), F32),
        across_sem=dma((2, kinds, chunks)),
        along_sem=dma((2, kinds, chunks, lines - 1)),
    )
    names = (*ins, *outs, *scratch)
    results = pl.pallas_call(
        functools.partial(backward_kernel, windows, last, size, names),
        out_shape=[shape for shape, _ in outs.values()],
        in_specs=[spec for _, spec in ins.values()],
        out_specs=[spec for _, spec in outs.values()],
        scratch_shapes=list(scratch.values()),
        compiler_params=pltpu.CompilerParams(
            collective_id=collective_id, has_side_effects=True, vmem_limit_bytes=VMEM_LIMIT
        ),
        name="backward_last" if last else "backward_first",
    )(*[value for value, _ in ins.values()])
    return dict(zip(outs, results, strict=True))


def lookup(index, table, out, r):
    heads, groups = table.shape[0], table.shape[1]
    for block in range(index.shape[1] // 128):
        c = pl.ds(block * 128, 128)
        row = index[r, c]
        low = row & 127
        high = row >> 7
        found = [jnp.zeros((16, 128), F32) for _ in range(heads)]
        for g in range(groups):
            here = high == g
            for h in range(heads):
                spread = jnp.broadcast_to(table[h, pl.ds(g, 1), :], (16, 128))
                taken = jnp.take_along_axis(spread, low, axis=1, mode="promise_in_bounds")
                found[h] = jnp.where(here, taken, found[h])
        for h in range(heads):
            out[h, r, c] = found[h].astype(BF16)


def scatter(index, grad, out, part=0, parts=1):
    heads = len(grad)
    groups = out.shape[1] // heads
    rows, width = index.shape
    if part == 0:
        out[...] = jnp.zeros_like(out)
    count = rows // 8 // parts
    lows = out.shape[0]
    shift = lows.bit_length() - 1
    low_rows = lax.broadcasted_iota(jnp.int32, (lows, width), 0)
    high_rows = lax.broadcasted_iota(jnp.int32, (groups, width), 0)

    def some(i):
        r = pl.ds(pl.multiple_of((part * count + i) * 8, 8), 8)
        index_rows = index[r, :]
        low = index_rows & (lows - 1)
        high = index_rows >> shift
        grads = [g[r, :] for g in grad]
        total = out[...]
        for i in range(8):
            onehot = jnp.where(low_rows == low[i : i + 1], 1.0, 0.0).astype(BF16)
            here = high_rows == high[i : i + 1]
            placed = jnp.concatenate(
                [jnp.where(here, g[i : i + 1], 0.0) for g in grads], axis=0
            ).astype(BF16)
            total = total + dot_nt(onehot, placed)
        out[...] = total

    loop(count, some)


def copy_kernel(count, *refs):
    given, out, held = refs[:count], refs[count : 2 * count], refs[2 * count : 3 * count]
    ins, outs = refs[3 * count :]
    reads = [pltpu.make_async_copy(given[i], held[i], ins.at[i]) for i in range(count)]
    writes = [pltpu.make_async_copy(held[i], out[i], outs.at[i]) for i in range(count)]
    for copy in reads:
        copy.start()
    for read, write in zip(reads, writes, strict=True):
        read.wait()
        write.start()
    for copy in writes:
        copy.wait()


def copy_out(arrays):
    return pl.pallas_call(
        functools.partial(copy_kernel, len(arrays)),
        out_shape=[jax.ShapeDtypeStruct(a.shape, a.dtype) for a in arrays],
        in_specs=[ANY] * len(arrays),
        out_specs=[ANY] * len(arrays),
        scratch_shapes=[pltpu.VMEM(a.shape, a.dtype) for a in arrays]
        + [dma((len(arrays),)), dma((len(arrays),))],
        compiler_params=pltpu.CompilerParams(vmem_limit_bytes=VMEM_LIMIT),
        name="copy_out",
    )(*arrays)


def local(
    tokens,
    cond,
    pad_mask,
    spatial_index,
    joint_index,
    qkv_a,
    proj_a,
    fc1_a,
    fc2_a,
    table_a,
    ada_a,
    qkv_b,
    proj_b,
    fc1_b,
    fc2_b,
    table_b,
    ada_b,
    cotangent,
    dp_size,
    mp_size,
):
    model = tokens.shape[1]
    inner = proj_a.shape[0]
    params_a = (qkv_a.transpose(1, 0, 2), proj_a, fc1_a, fc2_a)
    params_b = (qkv_b.transpose(1, 0, 2), proj_b, fc1_b, fc2_b)
    hidden_keys = jnp.where(pad_mask.reshape(-1) > 0, 0.0, -1e30).astype(F32)
    mask_a = hidden_keys.reshape(FRAMES, 2, 2, 64).transpose(0, 2, 1, 3).reshape(FRAMES, 1, -1)
    mask_b = hidden_keys.reshape(FRAMES, 2, 2, 4, 2, 8).transpose(1, 4, 2, 0, 3, 5)
    mask_b = mask_b.reshape(4, 1, -1)
    groups = (FRAMES, 4 * SIDE, model)

    first = {
        "cond": cond,
        "ada_a": ada_a,
        "ada_b": ada_b,
        "spatial": spatial_index,
        "joint": joint_index,
        "table": table_a.T,
        "next_table": table_b.T,
    }
    kept_a = block_forward(tokens.reshape(groups), first, None, params_a, mask_a, dp_size, 1)
    mods = kept_a["mods"]
    x_b = kept_a["y"].reshape(4, -1, model)
    then = (x_b, mods, kept_a["next_bias"])
    kept_b = block_forward(cotangent.reshape(groups), None, then, params_b, mask_b, dp_size, 2)
    back_b = block_backward(
        x_b,
        kept_b["top"].reshape(x_b.shape),
        mods,
        params_b,
        kept_b,
        kept_a["next_index"],
        (table_a.shape[0], table_b.shape[0]),
        kept_b["fc2_grad"],
        None,
        dp_size,
        3,
    )
    back_a = block_backward(
        kept_a["stream_s"],
        back_b["gx"].reshape(FRAMES, -1, model),
        mods,
        params_a,
        kept_a,
        kept_a["index"],
        (table_a.shape[0], table_b.shape[0]),
        back_b["carry_next"],
        (
            back_b["mod_out"],
            kept_a["cond_act"],
            kept_a["next_index"],
            back_b.get("qkv_out"),
            back_b["table_part"],
            back_b["gbias"],
        ),
        dp_size,
        4,
    )

    def block_grads(b, fc):
        to = "_b_out" if b == "b" else "_out"
        return (
            back_a["qkv" + to],
            fc["proj_out"],
            fc["fc1_out"],
            fc["fc2_out"],
            back_a[f"table_{b}_out"],
            back_a[f"ada_{b}_out"],
        )

    results = list(
        copy_out((kept_b["y"], back_a["gx"], *block_grads("a", back_a), *block_grads("b", back_b)))
    )
    for i in (2, 8):
        results[i] = results[i].transpose(1, 0, 2)
        results[i + 4] = results[i + 4].T
    return (
        results[0].reshape(tokens.shape),
        results[1].reshape(tokens.shape),
        *results[2:],
    )


def solution(mesh):
    in_specs = (
        P(("dp", "mp"), None),
        P("dp", None),
        P("dp", None),
        P(),
        P(),
        P(None, None, "mp"),
        P("mp", None),
        P(None, "mp"),
        P("mp", None),
        P(None, "mp"),
        P(None, "mp"),
        P(None, None, "mp"),
        P("mp", None),
        P(None, "mp"),
        P("mp", None),
        P(None, "mp"),
        P(None, "mp"),
        P(("dp", "mp"), None),
    )
    out_specs = (
        P(("dp", "mp"), None),
        P(("dp", "mp"), None),
        P("dp", None, "mp"),
        P("mp", "dp"),
        P("dp", "mp"),
        P("mp", "dp"),
        P(None, "mp"),
        P("dp", "mp"),
        P("dp", None, "mp"),
        P("mp", "dp"),
        P("dp", "mp"),
        P("mp", "dp"),
        P(None, "mp"),
        P("dp", "mp"),
    )
    body = functools.partial(local, dp_size=mesh.shape["dp"], mp_size=mesh.shape["mp"])
    return jax.shard_map(body, mesh=mesh, in_specs=in_specs, out_specs=out_specs, check_vma=False)
```

```python
import functools

import jax
import jax.numpy as jnp
from jax import lax
from jax.experimental import pallas as pl
from jax.experimental.pallas import tpu as pltpu
from jax.sharding import PartitionSpec as P

FRAMES = 5
SIDE = 16
EPSILON = 1e-06
HIGHEST = lax.Precision.HIGHEST
MESH = pl.DeviceIdType.MESH
F32 = jnp.float32
BF16 = jnp.bfloat16
VMEM_LIMIT = 60 << 20
GELU_K = 0.7978845608028654
GELU_C = 0.044715
ANY = pl.BlockSpec(memory_space=pl.ANY)
VM = pl.BlockSpec(memory_space=pltpu.VMEM)


def own_rows(src, dst, sems, x, core, sibling, partner, diagonal):
    sends, local, recvs = sems

    def place(j):
        return dst.at[lax.div(j, 2), lax.rem(j, 2)]

    def moves():
        found = []
        for k in range(5):
            j = 5 * x + lax.div(5 * core + k, 2)
            to = (partner,) if k % 2 == 0 else (diagonal, sibling)
            for i, other in enumerate(to):
                found.append(remote(src.at[k], place(j), sends.at[k, i], recvs.at[j], other))
            if k % 2 == 0:
                found.append(pltpu.make_async_copy(src.at[k], place(j), local.at[k // 2]))
        return found

    def start():
        for copy in moves():
            copy.start()

    def wait(j):
        row = 2 * j + core
        k = lax.rem(row, 5)
        here = (lax.div(row, 10) == x) & (lax.div(lax.rem(row, 10), 5) == core)

        @pl.when(here)
        def _():
            pltpu.make_async_copy(src.at[k], place(j), local.at[lax.div(k, 2)]).wait()

        @pl.when(jnp.logical_not(here))
        def _():
            remote(src.at[0], place(j), sends.at[0, 0], recvs.at[j], partner).wait_recv()

    def drain():
        for k in range(5):
            for i in range(1 if k % 2 == 0 else 2):
                remote(src.at[k], place(0), sends.at[k, i], recvs.at[0], partner).wait_send()

    return start, wait, drain


def qkv_copies(src, dst, sems):
    inner = src.shape[2]
    return [
        pltpu.make_async_copy(src.at[i], dst.at[:, pl.ds(i * inner, inner)], sems.at[i])
        for i in range(3)
    ]


def index_copies(r):
    copies = []
    for name, size, count in (("spatial", 64, 2), ("joint", 32, FRAMES)):
        dst = r["index_v" if name == "spatial" else "next_index_v"]
        for outer in range(count):
            for owner in range(2):
                copies.append(
                    pltpu.make_async_copy(
                        r[name].at[pl.ds((outer * 2 + owner) * size, size)],
                        dst.at[pl.ds((owner * count + outer) * size, size)],
                        r["index_sem"].at[len(copies)],
                    )
                )
    return copies


def place_index(src, dst, shift, count):
    width, wide = src.shape[1], dst.shape[1]
    lane = lax.broadcasted_iota(jnp.int32, (width, wide), 1)
    group = lane >> shift
    owner = (group >= count).astype(jnp.int32)
    origin = (((group - owner * count) * 2 + owner) << shift) + (lane & ((1 << shift) - 1))
    moved = lax.broadcasted_iota(jnp.int32, (width, wide), 0) == origin
    order = jnp.where(moved & (lane < width), 1.0, 0.0).astype(BF16)
    values = src[...]
    low = dot((values & 127).astype(F32).astype(BF16), order)
    high = dot((values >> 7).astype(F32).astype(BF16), order)
    placed = (low + 128.0 * high).astype(jnp.int32)
    dst[...] = jnp.where(lax.broadcasted_iota(jnp.int32, dst.shape, 1) < width, placed, -1)


def lane_table(src, dst):
    heads, rows = src.shape
    dst[...] = jnp.zeros_like(dst)
    values = src[...].astype(F32)
    for g in range(dst.shape[1]):
        count = min(128, rows - g * 128)
        for h in range(heads):
            dst[h, pl.ds(g, 1), pl.ds(0, count)] = values[h : h + 1, g * 128 : g * 128 + count]


def dma(shape):
    return pltpu.SemaphoreType.DMA(shape)


def places():
    me = lax.axis_index("mp")
    x = lax.div(me, 2)
    core = lax.rem(me, 2)
    return x, core, x * 2 + 1 - core, (1 - x) * 2 + core, (1 - x) * 2 + 1 - core


def greet(others):
    barrier = pltpu.get_barrier_semaphore()
    for other in others:
        pl.semaphore_signal(barrier, inc=1, device_id={"mp": other}, device_id_type=MESH)
    pl.semaphore_wait(barrier, len(others))


def remote(src, dst, send_sem, recv_sem, other):
    return pltpu.make_async_remote_copy(
        src_ref=src,
        dst_ref=dst,
        send_sem=send_sem,
        recv_sem=recv_sem,
        device_id={"mp": other},
        device_id_type=MESH,
    )


def loop(count, body):
    def step(i, _):
        body(i)
        return 0

    lax.fori_loop(0, count, step, 0)


def rows16(count, body, step=16):
    loop(count // step, lambda i: body(pl.ds(pl.multiple_of(i * step, step), step)))


def norm(values):
    centred = values - jnp.mean(values, axis=-1, keepdims=True)
    inv = lax.rsqrt(jnp.mean(centred * centred, axis=-1, keepdims=True) + EPSILON)
    return centred * inv, inv


def norm_back(normed, inv, grad):
    mean_g = jnp.mean(grad, axis=-1, keepdims=True)
    mean_gn = jnp.mean(grad * normed, axis=-1, keepdims=True)
    return (grad - mean_g - normed * mean_gn) * inv


def dot(a, b):
    return jnp.dot(a, b, preferred_element_type=F32)


def dot_nt(a, b):
    return lax.dot_general(a, b, (((1,), (1,)), ((), ())), preferred_element_type=F32)


def dot_tn(a, b):
    return lax.dot_general(a, b, (((0,), (0,)), ((), ())), preferred_element_type=F32)


def store_a_to_b(dst, frame, value):
    shaped = value.reshape(2, 4, 2, 8, value.shape[-1])
    for qr in range(2):
        for qc in range(2):
            dst[qr * 2 + qc, pl.ds(pl.multiple_of(frame * 4, 4), 4)] = shaped[qr, :, qc]


def store_b_to_a(dst, window, value):
    shaped = value.reshape(FRAMES, 4, 8, value.shape[-1])
    qr, qc = lax.div(window, 2), lax.rem(window, 2)
    for frame in range(FRAMES):
        dst[frame * 2 + qr, :, qc] = shaped[frame]


def store_a_to_a(dst, frame, value):
    shaped = value.reshape(2, 4, 2, 8, value.shape[-1])
    for qr in range(2):
        dst[frame * 2 + qr] = shaped[qr]


def hand_out(groups, out, send_sem, recv_sem, x, core, sibling):
    copies = []
    for i in range(2):
        copies.append(
            remote(
                groups.at[5 * x + 3 - 3 * core + i],
                out.at[1 + 2 * i],
                send_sem.at[i],
                recv_sem.at[i],
                sibling,
            )
        )
        copies[-1].start()
    for i in range(3):
        out[2 * i] = groups[5 * x + 2 * core + i]
    for copy in copies:
        copy.wait()


def forward_kernel(windows, last, names, *refs):
    r = dict(zip(names, refs, strict=True))
    stream, mask, bias, y_out = r["stream"], r["mask"], r["bias"], r["y"]
    mod = r["mod"].at[1] if last else r["mods"].at[0]
    qkv_w, proj_w, fc1_w, fc2_w = r["qkv_w"], r["proj_w"], r["fc1_w"], r["fc2_w"]
    h1, qkv, prob, att, ao = r["h1_v"], r["qkv_s_v"], r["prob_v"], r["att_v"], r["ao_v"]
    x1, h2, act, dg, mo = r["x1_v"], r["h2_v"], r["act_v"], r["dg_v"], r["mo_v"]
    ps1s, ps1r, ps2s, ps2r = r["ps1s"], r["ps1r"], r["ps2s"], r["ps2r"]
    xs1s, xs1r, xs2s, xs2r = r["xs1s"], r["xs1r"], r["xs2s"], r["xs2r"]
    part1, part2, out_sem = r["part1"], r["part2"], r["out_sem"]
    h1_sem, h2_sem, ps1_sem, ps2_sem = r["h1_sem"], r["h2_sem"], r["ps1_sem"], r["ps2_sem"]
    xs1_sem, xs2_sem = r["xs1_sem"], r["xs2_sem"]
    width = h1.shape[1]
    half = width // 2
    model = h1.shape[2]
    heads = bias.shape[0]
    inner = proj_w.shape[0]
    head_dim = inner // heads
    piece = half // FRAMES
    x, core, sibling, partner, diagonal = places()
    own = pl.ds(pl.multiple_of(core * half, 16), half)
    theirs = pl.ds(pl.multiple_of((1 - core) * half, 16), half)

    weights = qkv_copies(r["qkv"], qkv_w, r["qkv_sem"]) + [
        pltpu.make_async_copy(r[name], r[name + "_w"], r["w_sem"].at[i])
        for i, name in enumerate(("proj", "fc1", "fc2"))
    ]
    if not last:
        firsts = index_copies(r) + [
            pltpu.make_async_copy(r["ada_" + b], r["ada_v"].at[i], r["ada_sem"].at[i])
            for i, b in enumerate("ab")
        ]
        for copy in firsts:
            copy.start()
    for copy in weights:
        copy.start()
    saves = [
        (r[name + "_v"], r[name])
        for name in ("h1", "qkv_s", "prob", "att", "ao", "x1", "h2", "act", "dg", "mo")
        + (("gm",) if last else ())
    ]

    def save(which, f):
        src, dst = saves[which]
        return pltpu.make_async_copy(src.at[f], dst.at[f], out_sem.at[which, f])

    def share(buf, sem, f, rows):
        return remote(buf.at[f, own], buf.at[f, rows], sem.at[0, f], sem.at[1, f], sibling)

    def to_sibling(src, dst, sem, f):
        return remote(src.at[f], dst.at[f], sem.at[0, f], sem.at[1, f], sibling)

    def to_partner(src, dst, sem, f):
        return remote(src.at[f], dst.at[f], sem.at[0, f], sem.at[1, f], partner)

    greet((sibling, partner, diagonal))
    rows_start, rows_wait, rows_drain = own_rows(
        r["rows"],
        r["top_rows"] if last else stream,
        (r["rows_send"], r["rows_local"], r["rows_recv"]),
        x,
        core,
        sibling,
        partner,
        diagonal,
    )
    later = (x == 0) & (core == 1)
    if last:
        rows_start()
    else:
        pl.when(jnp.logical_not(later))(rows_start)
        me = lax.axis_index("mp")
        pieces, mods, parts = r["pieces"], r["mods"], r["parts"]
        cond = r["cond"][...].astype(F32)
        cond_act = (cond / (1.0 + jnp.exp(-cond))).astype(BF16)
        for i in range(2):
            r["cond_act"][pl.ds(i, 1)] = cond_act[:, i * 512 : i * 512 + 512].astype(F32)
        spread = jnp.broadcast_to(cond_act, (16, model))
        for i in range(2):
            firsts[-2 + i].wait()
            product = dot(spread, r["ada_v"][i])
            for j in range(3):
                parts[i, pl.ds(j, 1)] = product[0:1, j * 512 : j * 512 + 512]
        mod_copies = []
        for i in range(3):
            mod_copies.append(
                remote(
                    parts,
                    pieces.at[me],
                    r["mod_sem"].at[0, i],
                    r["mod_sem"].at[1, i],
                    lax.rem(me + 1 + i, 4),
                )
            )
            mod_copies[-1].start()
        pieces[me] = parts[...]
        for copy in firsts[:-2]:
            copy.wait()
        place_index(r["index_v"], r["index"], 6, 2)
        place_index(r["next_index_v"], r["next_index"], 5, FRAMES)
        lane_table(r["table"], r["table_v"])
        lane_table(r["next_table"], r["next_table_v"])
        rows16(width, lambda rows: lookup(r["index"], r["table_v"], bias, rows))
        pl.when(later)(rows_start)
        for copy in mod_copies:
            copy.wait()
        for i in range(12):
            half_row = pl.ds(i % 2 * 512, 512)
            for b in range(2):
                mods[b, pl.ds(i // 2, 1), half_row] = pieces[i // 3, b, pl.ds(i % 3, 1)]

    def own_stream(f):
        return stream[f].astype(F32).reshape(half, model)

    def first_norm(f):
        if not last:
            rows_wait(2 * f)
            rows_wait(2 * f + 1)
            keep_stream(f).start()
        normed, _ = norm(own_stream(f))
        h1[f, own] = (normed * (1.0 + mod[1:2]) + mod[0:1]).astype(BF16)
        share(h1, h1_sem, f, own).start()

    def keep_stream(f):
        return pltpu.make_async_copy(stream.at[f], r["stream_s"].at[f], r["top_sem"].at[f])

    loop(windows if last else 2, first_norm)
    for copy in weights[:4]:
        copy.wait()

    def top():
        def place(f):
            rows_wait(2 * f)
            rows_wait(2 * f + 1)
            store_a_to_b(r["top_v"], f, r["top_rows"][f].astype(F32).reshape(-1, model))

        loop(FRAMES, place)

        def give(f):
            grad = r["top_v"][f].reshape(half, model)
            pltpu.make_async_copy(r["top_v"].at[f], r["top"].at[f], r["top_sem"].at[f]).start()
            r["gm_v"][f, own] = (mod[5:6] * grad).astype(BF16)
            share(r["gm_v"], r["gm_sem"], f, own).start()

        loop(windows, give)

    def top_weights():
        def some(f):
            share(r["gm_v"], r["gm_sem"], f, theirs).wait_recv()
            save(10, f).start()

        loop(windows, some)
        grads, acts = r["gm_v"][...].reshape(-1, model), act[...].reshape(-1, act.shape[2])
        fc2_grad = r["fc2_grad_v"]
        for start in range(0, acts.shape[1], 256):
            c = slice(start, start + 256)
            piece = dot_tn(grads, acts[:, c]).astype(BF16)
            fc2_grad[..., c] = piece.reshape(*fc2_grad.shape[:-1], 256)
        grad_copy().start()

    def grad_copy():
        return pltpu.make_async_copy(r["fc2_grad_v"], r["fc2_grad"], r["w_sem"].at[4])

    lane_head = lax.div(lax.broadcasted_iota(jnp.int32, (width, inner), 1), head_dim)

    def attention(f):
        share(h1, h1_sem, f, theirs).wait_recv()
        save(0, f).start()
        qkv[f] = dot(h1[f], qkv_w[...]).astype(BF16)
        save(1, f).start()
        queries = qkv[f, :, :inner] * BF16(head_dim ** (-0.5))
        keys = qkv[f, :, inner : 2 * inner]
        vals = qkv[f, :, 2 * inner :]
        zero = jnp.zeros((), BF16)
        out = jnp.zeros((width, inner), F32)
        for h in range(heads):
            scores = dot_nt(jnp.where(lane_head == h, queries, zero), keys)
            scores = scores + bias[h, :, :width].astype(F32) + mask[f]
            weight = jnp.exp(scores - jnp.max(scores, axis=-1, keepdims=True))
            p = (weight * (1.0 / jnp.sum(weight, axis=-1, keepdims=True))).astype(BF16)
            prob[f, h] = p
            out = out + dot(p, jnp.where(lane_head == h, vals, zero))
        att[f] = out.astype(BF16)
        save(2, f).start()
        save(3, f).start()

        ps1s[f] = dot(att[f, theirs], proj_w[...]).astype(BF16)
        to_sibling(ps1s, ps1r, ps1_sem, f).start()
        part1[...] = dot(att[f, own], proj_w[...])

    def sum_first(f):
        to_sibling(ps1s, ps1r, ps1_sem, f).wait_recv()
        xs1s[f] = (part1[...] + ps1r[f].astype(F32)).astype(BF16)
        to_partner(xs1s, xs1r, xs1_sem, f).start()

    def sum_second(f):
        to_sibling(ps2s, ps2r, ps2_sem, f).wait_recv()
        xs2s[f] = (part2[...] + ps2r[f].astype(F32)).astype(BF16)
        second_xs(f, 1 - x).start()

    def second_xs(f, holder):
        rows = pl.ds(0, half)
        if last:
            rows = pl.ds(pl.multiple_of(2 * piece * holder, piece), 3 * piece)
        return remote(
            xs2s.at[f, rows], xs2r.at[f, rows], xs2_sem.at[0, f], xs2_sem.at[1, f], partner
        )

    def middle(f):
        to_partner(xs1s, xs1r, xs1_sem, f).wait_recv()

        total = xs1s[f].astype(F32) + xs1r[f].astype(F32)
        mid = own_stream(f) + mod[2:3] * total
        ao[f] = total.astype(BF16)
        x1[f] = mid
        normed, _ = norm(mid)
        h2[f, own] = (normed * (1.0 + mod[4:5]) + mod[3:4]).astype(BF16)
        share(h2, h2_sem, f, own).start()
        save(4, f).start()
        save(5, f).start()

    def mlp(f):
        share(h2, h2_sem, f, theirs).wait_recv()
        save(6, f).start()

        for start in range(0, act.shape[2], 256):
            c = pl.ds(start, 256)
            u = dot(h2[f], fc1_w[:, c])
            sq = u * u
            t = jnp.tanh(GELU_K * (u + GELU_C * u * sq))
            one_t = 0.5 * (1.0 + t)
            act[f, :, c] = (u * one_t).astype(BF16)
            slope = one_t + (0.5 * GELU_K) * u * (1.0 - t * t) * (1.0 + (3.0 * GELU_C) * sq)
            dg[f, :, c] = slope.astype(BF16)
        save(7, f).start()
        save(8, f).start()
        ps2s[f] = dot(act[f, theirs], fc2_w[...]).astype(BF16)
        to_sibling(ps2s, ps2r, ps2_sem, f).start()
        part2[...] = dot(act[f, own], fc2_w[...])

    def finish(f):
        second_xs(f, x).wait_recv()
        if last:
            keep = pl.ds(pl.multiple_of(2 * piece * x, piece), 3 * piece)
            total = xs2s[f, keep].astype(F32) + xs2r[f, keep].astype(F32)
            result = x1[f, keep] + mod[5:6] * total
            mo[f] = jnp.zeros((half, model), BF16)
            qr, qc = lax.div(f, 2), lax.rem(f, 2)
            for i in range(3):
                frame = 2 * x + i
                counted = (frame != 2) | (qr == x)
                cut = slice(i * piece, (i + 1) * piece)
                rows = pl.ds(pl.multiple_of((2 * x + i) * piece, piece), piece)
                mo[f, rows] = jnp.where(counted, total[cut], 0.0).astype(BF16)
                r["groups"][frame * 2 + qr, :, qc] = result[cut].reshape(4, 8, model)
        else:
            total = xs2s[f].astype(F32) + xs2r[f].astype(F32)
            mo[f] = total.astype(BF16)
            store_a_to_b(y_out, f, x1[f] + mod[5:6] * total)
        save(9, f).start()

    def first_step(t):
        attention(t)
        sum_first(t)
        if not last:

            @pl.when(t + 2 < windows)
            def _():
                first_norm(t + 2)

    def second_step(t):
        mlp(t)

        @pl.when(t + 1 < windows)
        def _():
            middle(t + 1)

        sum_second(t)

    def last_step(t):
        if not last:
            blocks = r["next_index"].shape[0] // 16
            each = -(-blocks // windows)

            def next_bias(i):
                block = t * each + i

                @pl.when(block < blocks)
                def _():
                    rows = pl.ds(pl.multiple_of(block * 16, 16), 16)
                    lookup(r["next_index"], r["next_table_v"], r["next_bias"], rows)

            loop(each, next_bias)
        finish(t)

    loop(windows, first_step)
    if last:
        top()
    for copy in weights[4:]:
        copy.wait()
    middle(0)
    loop(windows, second_step)
    if last:
        top_weights()
    loop(windows, last_step)
    if last:
        hand_out(r["groups"], y_out, r["hand_sem"].at[0], r["hand_sem"].at[1], x, core, sibling)

    def drain(f):
        for which in range(len(saves)):
            save(which, f).wait()
        share(h1, h1_sem, f, own).wait_send()
        share(h2, h2_sem, f, own).wait_send()
        to_sibling(ps1s, ps1r, ps1_sem, f).wait_send()
        to_sibling(ps2s, ps2r, ps2_sem, f).wait_send()
        to_partner(xs1s, xs1r, xs1_sem, f).wait_send()
        second_xs(f, 1 - x).wait_send()
        if last:
            share(r["gm_v"], r["gm_sem"], f, own).wait_send()
            pltpu.make_async_copy(r["top_v"].at[f], r["top"].at[f], r["top_sem"].at[f]).wait()
        else:
            keep_stream(f).wait()

    loop(windows, drain)
    rows_drain()
    if last:
        grad_copy().wait()


def block_forward(rows, first, then, params, mask, size, collective_id):
    last = then is not None
    qkv_w, proj_w, fc1_w, fc2_w = params
    windows, _, width = mask.shape
    model = rows.shape[-1]
    half = width // 2
    heads = then[2].shape[0] if last else first["table"].shape[0]
    inner = proj_w.shape[0]
    hidden = fc1_w.shape[1]
    sds = jax.ShapeDtypeStruct
    ins = {"rows": (rows, ANY), "mask": (mask, VM)}
    outs, scratch = {}, {}
    if last:
        ins.update({name: (v, VM) for name, v in zip(("stream", "mod", "bias"), then, strict=True)})
    else:
        for name, value in first.items():
            whole = name in ("ada_a", "ada_b", "spatial", "joint")
            ins[name] = (value, ANY if whole else VM)
        spatial, joint = first["spatial"], first["joint"]
        next_shape = (joint.shape[0], -(-joint.shape[1] // 128) * 128)
        outs["mods"] = (sds((2, 6, model), F32), VM)
        outs["cond_act"] = (sds((2, 512), F32), VM)
        outs["index"] = (sds(spatial.shape, jnp.int32), VM)
        outs["next_index"] = (sds(next_shape, jnp.int32), VM)
        outs["next_bias"] = (sds((heads, *next_shape), BF16), VM)
        for name in ("table", "next_table"):
            count = -(-first[name].shape[1] // 128)
            scratch[name + "_v"] = pltpu.VMEM((heads, count, 128), F32)
        scratch["index_v"] = pltpu.VMEM(spatial.shape, jnp.int32)
        scratch["next_index_v"] = pltpu.VMEM(joint.shape, jnp.int32)
        scratch["ada_v"] = pltpu.VMEM((2, *first["ada_a"].shape), BF16)
        scratch["parts"] = pltpu.VMEM((2, 3, 512), F32)
        scratch["index_sem"] = dma((4 + 2 * FRAMES,))
        scratch["ada_sem"] = dma((2,))
        outs["stream_s"] = (sds((windows, 2, half // 2, model), BF16), ANY)
        scratch["stream"] = pltpu.VMEM((windows, 2, half // 2, model), BF16)
        scratch["bias"] = pltpu.VMEM((heads, *spatial.shape), BF16)
        scratch["pieces"] = pltpu.VMEM((4, 2, 3, 512), F32)
        scratch["mod_sem"] = dma((2, 3))
    scratch["rows_send"] = dma((5, 2))
    scratch["rows_local"] = dma((3,))
    scratch["rows_recv"] = dma((2 * FRAMES,))
    for name, value in (("qkv", qkv_w), ("proj", proj_w), ("fc1", fc1_w), ("fc2", fc2_w)):
        ins[name] = (value, ANY)
        shape = (model, 3 * inner) if name == "qkv" else value.shape
        scratch[name + "_w"] = pltpu.VMEM(shape, value.dtype)
    saved = {
        "h1": ((windows, width, model), BF16),
        "qkv_s": ((windows, width, 3 * inner), BF16),
        "prob": ((windows, heads, width, width), BF16),
        "att": ((windows, width, inner), BF16),
        "ao": ((windows, half, model), BF16),
        "x1": ((windows, half, model), F32),
        "h2": ((windows, width, model), BF16),
        "act": ((windows, width, hidden), BF16),
        "dg": ((windows, width, hidden), BF16),
        "mo": ((windows, half, model), BF16),
    }
    if last:
        outs["top"] = (sds((windows, half // 8, 8, model), F32), ANY)
        scratch["top_v"] = pltpu.VMEM((windows, half // 8, 8, model), F32)
        scratch["top_rows"] = pltpu.VMEM((FRAMES, 2, 4 * SIDE, model), BF16)
        saved["gm"] = ((windows, width, model), BF16)
        saved["fc2_grad"] = ((size // 2, 2, model // size, hidden), BF16)
    for name, (shape, dtype) in saved.items():
        outs[name] = (sds(shape, dtype), ANY)
        scratch[name + "_v"] = pltpu.VMEM(shape, dtype)
    if last:
        outs["y"] = (sds((FRAMES, 4, 2, 8, model), F32), VM)
        scratch["groups"] = pltpu.VMEM((2 * FRAMES, 4, 2, 8, model), F32)
    else:
        outs["y"] = (sds((4, FRAMES * 4, 8, model), F32), VM)
    own_all = pltpu.VMEM((windows, half, model), BF16)
    for name in ("ps1s", "ps1r", "xs1s", "xs1r", "ps2s", "ps2r", "xs2s", "xs2r"):
        scratch[name] = own_all
    for name in ("h1", "h2", "gm", "ps1", "ps2", "xs1", "xs2"):
        scratch[name + "_sem"] = dma((2, windows))
    scratch.update(
        part1=pltpu.VMEM((half, model), F32),
        part2=pltpu.VMEM((half, model), F32),
        w_sem=dma((5,)),
        qkv_sem=dma((3,)),
        out_sem=dma((11, windows)),
        top_sem=dma((windows,)),
        hand_sem=dma((2, 2)),
    )
    names = (*ins, *outs, *scratch)
    results = pl.pallas_call(
        functools.partial(forward_kernel, windows, last, names),
        out_shape=[shape for shape, _ in outs.values()],
        in_specs=[spec for _, spec in ins.values()],
        out_specs=[spec for _, spec in outs.values()],
        scratch_shapes=list(scratch.values()),
        compiler_params=pltpu.CompilerParams(
            collective_id=collective_id, has_side_effects=True, vmem_limit_bytes=VMEM_LIMIT
        ),
        name="forward_last" if last else "forward_first",
    )(*[value for value, _ in ins.values()])
    return dict(zip(outs, results, strict=True))


QKV_EARLY = 0
STREAMS = ("dg", "h2", "qkv_s", "prob", "h1", "x1", "ao", "mo", "stream")


def backward_kernel(windows, last, size, names, *refs):
    r = dict(zip(names, refs, strict=True))
    mod, index = r["mod"].at[1 if last else 0], r.get("index")
    grad, part1, part2, gh, gqkv = r["grad"], r["part1"], r["part2"], r["gh"], r["gqkv"]
    fc1_w, fc2_w, qkv_w, proj_w = r["fc1_w"], r["fc2_w"], r["qkv_w"], r["proj_w"]
    gm, rest, wgrad, gbias = r["gm"], r["rest"], r["wgrad"], r["gbias"]
    ga = gm
    ps1s, ps1r, ps2s, ps2r = r["ps1s"], r["ps1r"], r["ps2s"], r["ps2r"]
    xs1s, xs1r, xs2s, xs2r = r["xs1s"], r["xs1r"], r["xs2s"], r["xs2r"]
    buf1, buf2, msum, mtot, mrecv = r["buf1"], r["buf2"], r["msum"], r["mtot"], r["mrecv"]
    _, half, model = grad.shape
    width = 2 * half
    heads = gbias.shape[0]
    inner = proj_w.shape[0]
    head_dim = inner // heads
    hidden = gh.shape[1]
    scale = head_dim ** (-0.5)
    chunk = buf1.shape[-1]
    fc_chunks = hidden // chunk
    rest_chunks = 4 * inner // chunk
    carry_chunks = r["carry"].shape[-1] // chunk
    now = range(QKV_EARLY if last else rest_chunks - 1)
    kinds = {"fc1": 0, "carry": 1, "rest": 2, "fc2": 3}
    sources = {"fc1": fc1_w, "carry": rest, "rest": rest, "fc2": r.get("fc2_grad")}
    if last:
        plan = {
            (0, 1): [("carry", 0)],
            (0, 2): [("carry", 1)],
            (0, 3): [("carry", 2)],
            (1, 0): [("carry", 3), ("fc1", 0)],
            (1, 1): [("fc1", 1)],
            (1, 2): [("fc1", 2)],
            (1, 3): [("fc1", 3), ("rest", 3)],
        }
    else:
        plan = {
            (0, 1): [("carry", 0)],
            (0, 2): [("carry", 1)],
            (0, 4): [("fc2", 0)],
            (1, 0): [("fc2", 1), ("fc2", 2)],
            (1, 1): [("fc2", 3), ("fc1", 0)],
            (1, 2): [("fc1", 1)],
            (1, 3): [("fc1", 2)],
            (1, 4): [("fc1", 3)],
        }
    if carry_chunks == 3:
        plan[0, 3] = [("carry", 2)]
    x, core, sibling, partner, diagonal = places()
    own = pl.ds(pl.multiple_of(core * half, 16), half)
    theirs = pl.ds(pl.multiple_of((1 - core) * half, 16), half)
    lines = size // 2
    here = lax.axis_index("dp")
    line, side = lax.div(here, 2), lax.rem(here, 2)

    targets = {
        "grad_y": grad,
        "gm_s": gm,
        "carry": rest.at[..., pl.ds(0, r["carry"].shape[-1])],
        "fc2": fc2_w,
        "fc1": fc1_w,
        "act": r.get("act_v"),
        "proj": proj_w,
        "att": r["att_v"],
    }
    loads = {
        name: pltpu.make_async_copy(r[name], target, r["w_sem"].at[i])
        for i, (name, target) in enumerate(targets.items())
        if name in r
    }
    qkv_loads = qkv_copies(r["qkv"], qkv_w, r["qkv_sem"])
    for_mlp = ("dg", "h2")
    for_attention = ("qkv_s", "prob", "h1")
    for_middle = ("x1", "ao", "mo")

    def fetch(name, f):
        slot = lax.rem(f, 2)
        sem = r["in_sem"].at[STREAMS.index(name), slot]
        return pltpu.make_async_copy(r[name].at[f], r[name + "_v"].at[slot], sem)

    def share(buf, sem, f, rows):
        return remote(buf.at[f, own], buf.at[f, rows], sem.at[0, f], sem.at[1, f], sibling)

    def to_sibling(src, dst, sem, f):
        slot = lax.rem(f, 2)
        return remote(src.at[slot], dst.at[slot], sem.at[0, slot], sem.at[1, slot], sibling)

    def first_ps(f):
        return to_sibling(ps1s, ps1r, r["ps1_sem"], f)

    def second_ps(f):
        return to_sibling(ps2s, ps2r, r["ps2_sem"], f)

    def first_xs(f):
        sem = r["xs1_sem"]
        return remote(xs1s.at[f], xs1r.at[f], sem.at[0, f], sem.at[1, f], partner)

    def second_xs(f):
        sem, slot = r["xs2_sem"], lax.rem(f, 2)
        return remote(xs2s.at[slot], xs2r.at[f], sem.at[0, slot], sem.at[1, f], partner)

    def along_dp(src, dst, send_sem, recv_sem, other):
        return pltpu.make_async_remote_copy(
            src_ref=src,
            dst_ref=dst,
            send_sem=send_sem,
            recv_sem=recv_sem,
            device_id={"dp": other},
            device_id_type=MESH,
        )

    def chunk_cols(i):
        return pl.ds(pl.multiple_of(i * chunk, chunk), chunk)

    def across(kind, i):
        k = kinds[kind]
        return along_dp(
            sources[kind].at[:, 1 - side, :, chunk_cols(i)],
            buf1.at[k, i],
            r["across_sem"].at[0, k, i],
            r["across_sem"].at[1, k, i],
            line * 2 + 1 - side,
        )

    def along(kind, i, j):
        k = kinds[kind]
        to = lax.rem(line + 1 + j, lines)
        return along_dp(
            buf1.at[k, i, to],
            buf2.at[k, i, j],
            r["along_sem"].at[0, k, i, j],
            r["along_sem"].at[1, k, i, j],
            to * 2 + side,
        )

    def reduce_side(kind, i):
        k = kinds[kind]
        across(kind, i).wait_recv()
        mine = sources[kind][:, side, :, chunk_cols(i)]
        buf1[k, i] = (mine.astype(F32) + buf1[k, i].astype(F32)).astype(BF16)
        loop(lines - 1, lambda j: along(kind, i, j).start())

    def reduce_line(kind, i):
        k = kinds[kind]
        loop(lines - 1, lambda j: along(kind, i, j).wait_recv())
        return buf1[k, i, line].astype(F32) + jnp.sum(buf2[k, i].astype(F32), axis=0)

    def take_up(phase, f):
        for (when, step), sums in plan.items():
            if when != phase:
                continue

            @pl.when(f == step)
            def _(sums=sums):
                for kind, i in sums:
                    reduce_side(kind, i)

    def drain_sum(kind, i):
        if kind != "carry":
            across(kind, i).wait_send()
        loop(lines - 1, lambda j: along(kind, i, j).wait_send())

    for copy in loads.values():
        copy.start()
    for which in for_mlp:
        fetch(which, 0).start()
    for copy in qkv_loads:
        copy.start()

    barrier = pltpu.get_barrier_semaphore()
    for other in (sibling, partner):
        pl.semaphore_signal(barrier, inc=1, device_id={"mp": other}, device_id_type=MESH)

    def greet_dp(j):
        pl.semaphore_signal(
            barrier, inc=1, device_id={"dp": lax.rem(here + 1 + j, size)}, device_id_type=MESH
        )

    loop(size - 1, greet_dp)
    pl.semaphore_wait(barrier, 1 + size)

    def top(f):
        gm[f, own] = (mod[5:6] * grad[f]).astype(BF16)
        share(gm, r["gm_sem"], f, own).start()

    loads["grad_y"].wait()
    if last:
        loads["gm_s"].wait()
    else:
        loop(windows, top)
    loads["carry"].wait()
    loop(carry_chunks, lambda i: across("carry", i).start())
    msum[...] = jnp.zeros_like(msum)
    gbias[...] = jnp.zeros_like(gbias)
    wgrad[...] = jnp.zeros_like(wgrad)

    lane_head = lax.div(lax.broadcasted_iota(jnp.int32, (width, inner), 1), head_dim)
    zero = jnp.zeros((), BF16)

    def flat(weight):
        value = weight[...]
        return value.reshape(-1, value.shape[-1])

    def mlp_back(f):
        slot = lax.rem(f, 2)
        for which in for_mlp:
            fetch(which, f).wait()
        if not last:

            @pl.when(f == 0)
            def _():
                share(gm, r["gm_sem"], f, theirs).wait_recv()

        gh[...] = (dot_nt(gm[f], flat(fc2_w)) * r["dg_v"][slot].astype(F32)).astype(BF16)

        @pl.when(f >= 2)
        def _():
            first_ps(f - 2).wait_send()

        ps1s[slot] = dot_nt(gh[theirs], flat(fc1_w)).astype(BF16)
        first_ps(f).start()
        part1[...] = dot_nt(gh[own], flat(fc1_w))

    def sum_first(f):
        slot = lax.rem(f, 2)
        first_ps(f).wait_recv()
        xs1s[f] = (part1[...] + ps1r[slot].astype(F32)).astype(BF16)
        first_xs(f).start()

    def fc2_weights():
        loop(windows - 1, lambda f: share(gm, r["gm_sem"], f + 1, theirs).wait_recv())
        loads["act"].wait()
        grads, acts = gm[...].reshape(-1, model), r["act_v"][...].reshape(-1, hidden)
        out = r["fc2_grad"]
        for i in range(fc_chunks):
            c = slice(i * chunk, (i + 1) * chunk)
            out[..., c] = dot_tn(grads, acts[:, c]).astype(BF16).reshape(*out.shape[:-1], chunk)
            across("fc2", i).start()

    def mlp_weights(f):
        slot = lax.rem(f, 2)
        for start in range(0, hidden, 512):
            c = pl.ds(start, 512)
            wgrad[:, c] += dot_tn(r["h2_v"][slot], gh[:, c])

    def fold(values):
        return values.reshape(half // 8, 8, model).sum(axis=0)

    def middle(f):
        slot = lax.rem(f, 2)
        for which in for_middle:
            fetch(which, f).wait()
        first_xs(f).wait_recv()
        grad_h = xs1s[f].astype(F32) + xs1r[f].astype(F32)
        normed, inv = norm(r["x1_v"][slot])
        gy = grad[f]
        grad_mid = gy + norm_back(normed, inv, grad_h * (1.0 + mod[4:5]))
        msum[2] += fold(grad_mid * r["ao_v"][slot].astype(F32))
        msum[3] += fold(grad_h)
        msum[4] += fold(grad_h * normed)
        msum[5] += fold(gy * r["mo_v"][slot].astype(F32))
        grad[f] = grad_mid
        ga[f, own] = (mod[2:3] * grad_mid).astype(BF16)
        share(ga, r["ga_sem"], f, own).start()

    def attention_back(f):
        slot = lax.rem(f, 2)
        qkv = r["qkv_s_v"]
        for which in for_attention:
            fetch(which, f).wait()

        @pl.when(f < windows - 1)
        def _():
            share(ga, r["ga_sem"], f, theirs).wait_recv()

        grad_att = dot_nt(ga[f], proj_w[...]).astype(BF16)
        grad_att_t = grad_att.T
        queries_t = qkv[slot, :, :inner].T
        keys = qkv[slot, :, inner : 2 * inner] * BF16(scale)
        vals = qkv[slot, :, 2 * inner :]
        grad_q = jnp.zeros((width, inner), F32)
        grad_k, grad_v = [], []
        for h in range(heads):
            part = slice(h * head_dim, (h + 1) * head_dim)
            p = r["prob_v"][slot, h]
            grad_p = dot_nt(jnp.where(lane_head == h, grad_att, zero), vals)
            pf = p.astype(F32)
            weighted = pf * grad_p
            grad_s = weighted - pf * jnp.sum(weighted, axis=-1, keepdims=True)
            gbias[h, :, :width] += grad_s
            rounded = grad_s.astype(BF16)
            grad_q = grad_q + dot(rounded, jnp.where(lane_head == h, keys, zero))
            grad_v.append(dot(grad_att_t[part], p))
            grad_k.append(dot(queries_t[part], rounded) * scale)
        gqkv[:, :inner] = grad_q.astype(BF16)
        gqkv[:, inner : 2 * inner] = jnp.concatenate(grad_k, axis=0).astype(BF16).T
        gqkv[:, 2 * inner :] = jnp.concatenate(grad_v, axis=0).astype(BF16).T

        @pl.when(f >= 2)
        def _():
            second_ps(f - 2).wait_send()

        ps2s[slot] = dot_nt(gqkv[theirs], qkv_w[...]).astype(BF16)
        second_ps(f).start()
        part2[...] = dot_nt(gqkv[own], qkv_w[...])

    def sum_second(f):
        slot = lax.rem(f, 2)
        second_ps(f).wait_recv()

        @pl.when(f >= 2)
        def _():
            second_xs(f - 2).wait_send()

        xs2s[slot] = (part2[...] + ps2r[slot].astype(F32)).astype(BF16)
        second_xs(f).start()

    def attention_weights(f):
        slot = lax.rem(f, 2)
        for start in range(0, 3 * inner, 384):
            c = pl.ds(start, 384)
            wgrad[:, c] += dot_tn(r["h1_v"][slot], gqkv[:, c])

    def proj_weights():
        share(ga, r["ga_sem"], windows - 1, theirs).wait_recv()
        loads["att"].wait()
        piece = dot_tn(ga[...].reshape(-1, model), r["att_v"][...].reshape(-1, inner))
        for i in range(carry_chunks):
            across("carry", i).wait_send()
        c = pl.ds(3 * inner, inner)
        rest[..., c] = piece.astype(BF16).reshape(*rest.shape[:-1], inner)
        across("rest", rest_chunks - 1).start()

    def finish(f):
        slot = lax.rem(f, 2)
        fetch("stream", f).wait()
        second_xs(f).wait_recv()
        grad_h = xs2s[slot].astype(F32) + xs2r[f].astype(F32)
        normed, inv = norm(r["stream_v"][slot].astype(F32).reshape(half, model))
        msum[0] += fold(grad_h)
        msum[1] += fold(grad_h * normed)
        grad_x = grad[f] + norm_back(normed, inv, grad_h * (1.0 + mod[1:2]))
        if last:
            store_b_to_a(r["gx"], f, grad_x)
        else:
            grad[f] = grad_x

    def first_step(f):
        @pl.when(f + 1 < windows)
        def _():
            for which in for_mlp:
                fetch(which, f + 1).start()

        @pl.when(f == 0)
        def _():
            loads["fc2"].wait()
            loads["fc1"].wait()

        mlp_back(f)
        mlp_weights(f)
        sum_first(f)
        if not last:
            pl.when(f == 0)(fc2_weights)
        take_up(0, f)

    loop(windows, first_step)
    if not last:
        loop(windows, lambda f: share(gm, r["gm_sem"], f, own).wait_send())

    for which in (*for_attention, *for_middle, "stream"):
        fetch(which, 0).start()
    shape = fc1_w.shape
    fc1_w[...] = wgrad[:, :hidden].astype(BF16).reshape(shape)
    loop(fc_chunks, lambda i: across("fc1", i).start())
    wgrad[:, : 3 * inner] = jnp.zeros((model, 3 * inner), F32)
    for which in for_middle:
        fetch(which, 1).start()
    middle(0)
    for copy in (loads["proj"], *qkv_loads):
        copy.wait()

    gate = r["gate"]
    if last:
        sems = r["mod_sem"]
        gate_copy = remote(gate.at[0], gate.at[1], sems.at[2], sems.at[3], partner)

    def give_gate():
        for i in range(2):
            c = slice(i * 512, i * 512 + 512)
            gate[0, pl.ds(i, 1)] = jnp.sum(msum[5, :, c], axis=0, keepdims=True)
        gate_copy.start()

    def second_step(f):
        @pl.when(f + 1 < windows)
        def _():
            for which in for_attention:
                fetch(which, f + 1).start()
            middle(f + 1)

        @pl.when(f + 2 < windows)
        def _():
            for which in for_middle:
                fetch(which, f + 2).start()

        attention_back(f)
        attention_weights(f)
        sum_second(f)
        pl.when(f == windows - 2)(proj_weights)
        if last:
            pl.when(f == windows - 2)(give_gate)

        take_up(1, f)

        @pl.when(f >= 1)
        def _():
            finish(f - 1)

        @pl.when((f >= 1) & (f + 1 < windows))
        def _():
            fetch("stream", f + 1).start()

        @pl.when(f == 0)
        def _():
            fetch("stream", 1).start()

    loop(windows, second_step)

    shape = (*rest.shape[:-1], 3 * inner)
    rest[..., pl.ds(0, 3 * inner)] = wgrad[:, : 3 * inner].astype(BF16).reshape(shape)
    for i in now:
        across("rest", i).start()
    if last:
        later = pl.ds(len(now) * chunk, (rest_chunks - 1 - len(now)) * chunk)
        carry = pltpu.make_async_copy(rest.at[..., later], r["carry_next"], r["w_sem"].at[8])
        carry.start()
    if not last:
        wide = r["gbias_b"].shape[2]
        tall = r["gbias_b"].shape[1]

        def other_place(h):
            return pl.ds(h // 2 * tall, tall), pl.ds(h % 2 * wide, wide)

        other_loads = []
        for h in range(heads):
            other_loads.append(
                pltpu.make_async_copy(
                    r["gbias_b"].at[h], wgrad.at[other_place(h)], r["other_sem"].at[h]
                )
            )
            other_loads[-1].start()
        mine = [gbias.at[h] for h in range(heads)]
        other = [wgrad.at[other_place(h)] for h in range(heads)]
        scatter(index, mine, r["table"])
    else:
        for i in range(2):
            scatter(index, [gbias.at[h] for h in range(heads)], r["table_part"], i, 4)
    take_up(2, 0)
    finish(windows - 1)
    for i in range(12):
        c = slice(i % 2 * 512, i % 2 * 512 + 512)
        mtot[i // 3, pl.ds(i % 3, 1)] = jnp.sum(msum[i // 2, :, c], axis=0, keepdims=True)
    if last:
        gate_copy.wait()
        mtot[3, 1:3] = gate[0] + gate[1]
    mod_copy = remote(mtot, mrecv, r["mod_sem"].at[0], r["mod_sem"].at[1], sibling)
    mod_copy.start()
    small, everyone, tabs = r.get("small"), r.get("everyone"), r.get("tabs")

    def give_small(j):
        return along_dp(
            small,
            everyone.at[here],
            r["small_sem"].at[0, j],
            r["small_sem"].at[1, j],
            lax.rem(here + 1 + j, size),
        )

    def give_table(j):
        to = lax.rem(here + 1 + j, size)
        sem = r["table_sem"]
        return along_dp(tabs.at[to], r["tab_parts"].at[j], sem.at[0, j], sem.at[1, j], to)

    def give_sum(j):
        to = lax.rem(here + 1 + j, size)
        sem = r["sum_sem"]
        return along_dp(r["tab_sum"], r["tables"].at[here], sem.at[0, j], sem.at[1, j], to)

    def start_mods():
        mod_copy.wait()
        me = lax.axis_index("mp")
        small[0:3] = mtot[me] + mrecv[me]
        small[3:6] = r["mod_b"][...]
        small[6:8] = r["cond"][...]
        everyone[here] = small[...]
        loop(size - 1, lambda j: give_small(j).start())

    def start_tables():
        each = tabs.shape[1]
        whole = r["whole_table"]
        whole[...] = jnp.zeros_like(whole)
        base = 0
        for table in (r["table"], r["table_b"]):
            rows, columns = table.shape
            whole[:rows, base : base + columns] = table[...]
            base += columns
        for i in range(size):
            tabs[i] = whole[i * each : (i + 1) * each]
        loop(size - 1, lambda j: give_table(j).start())

    def finish_tables():
        loop(size - 1, lambda j: give_table(j).wait_recv())
        total = tabs[here] + jnp.sum(r["tab_parts"][...], axis=0)
        r["tab_sum"][...] = total
        r["tables"][here] = total
        give_ada()
        loop(size - 1, lambda j: give_sum(j).start())

    def give_ada():
        loop(size - 1, lambda j: give_small(j).wait_recv())
        rows = r["ada_a_out"].shape[0]
        lane = lax.broadcasted_iota(jnp.int32, (rows, model), 1)
        row = lax.broadcasted_iota(jnp.int32, (rows, model), 0) + here * rows
        chosen = jnp.where(lane == row, 1.0, 0.0).astype(BF16)
        conds = [everyone[:, 6 + i, :].astype(BF16) for i in range(2)]
        mine = dot_nt(chosen[:, :512], conds[0]) + dot_nt(chosen[:, 512:], conds[1])
        for i in range(6):
            out = r["ada_a_out" if i < 3 else "ada_b_out"]
            out[:, pl.ds(i % 3 * 512, 512)] = jnp.dot(
                mine, everyone[:, i, :], precision=HIGHEST, preferred_element_type=F32
            )

    def finish_sums():
        loop(size - 1, lambda j: give_sum(j).wait_recv())
        whole, tables = r["whole_table"], r["tables"]
        each = tables.shape[1]
        for i in range(size):
            whole[i * each : (i + 1) * each] = tables[i]
        turned = whole[...].T
        base = 0
        for name, table in (("table_a_out", r["table"]), ("table_b_out", r["table_b"])):
            out, lows = r[name], table.shape[0]
            groups = table.shape[1] // heads
            for h in range(heads):
                for g in range(-(-out.shape[1] // lows)):
                    count = min(lows, out.shape[1] - g * lows)
                    row = base + h * groups + g
                    out[pl.ds(h, 1), pl.ds(g * lows, count)] = turned[row : row + 1, :count]
            base += heads * groups
        for give in (give_small, give_table, give_sum):
            loop(size - 1, lambda j, give=give: give(j).wait_send())

    hands = []
    if not last:
        gx = r["gx"]

        def group(j):
            which = 5 * x + j
            rows = pl.ds(pl.multiple_of(lax.rem(which, 2) * 64, 64), 64)
            return lax.div(which, 2), rows

        for i in range(2):
            f, rows = group(3 - 3 * core + i)
            hands.append(
                remote(
                    grad.at[f, rows],
                    gx.at[1 + 2 * i],
                    r["hand_sem"].at[0, i],
                    r["hand_sem"].at[1, i],
                    sibling,
                )
            )
            hands[-1].start()
        for i in range(3):
            f, rows = group(2 * core + i)
            gx[2 * i] = grad[f, rows]

    if last:
        for i in now:
            reduce_side("rest", i)
    else:
        for copy in other_loads:
            copy.wait()
        reduce_side("rest", rest_chunks - 1)
        r["table_b"][...] = r["table_part"][...]
        for i in range(2, 4):
            scatter(r["index_b"], other, r["table_b"], i, 4)
            if i == 2:
                start_mods()
            else:
                start_tables()
            reduce_side("rest", i - 2)
        reduce_side("rest", 2)
    outputs = [
        ("carry", range(carry_chunks)),
        ("fc1", range(fc_chunks)),
        ("rest", (rest_chunks - 1, *now)),
    ]
    if not last:
        outputs.insert(1, ("fc2", range(fc_chunks)))

    def finish_chunk(kind, i):
        value = reduce_line(kind, i)
        if kind == "fc1":
            r["fc1_out"][:, pl.ds(i * chunk, chunk)] = value
        elif kind == "fc2" or (last and kind == "carry"):
            r["fc2_out"][pl.ds(i * chunk, chunk)] = value.T
        else:
            piece = i if kind == "rest" else 3 - carry_chunks + i
            to = "_b_out" if kind == "carry" else "_out"
            if piece < 3:
                r["qkv" + to][piece] = value
            else:
                r["proj_out"][...] = value.T

    if not last:
        if QKV_EARLY:
            r["qkv_b_out"][pl.ds(0, QKV_EARLY)] = r["early"][...]
    for kind, chunks in outputs:
        if kind == "rest" and not last:
            finish_tables()
        for i in chunks:
            finish_chunk(kind, i)
    if last:
        carry.wait()
        mod_copy.wait()
        me = lax.axis_index("mp")
        r["mod_out"][...] = mtot[me] + mrecv[me]
    else:
        finish_sums()
    for copy in hands:
        copy.wait()

    def drain(f):
        share(ga, r["ga_sem"], f, own).wait_send()
        first_xs(f).wait_send()

    loop(windows, drain)
    for f in range(windows - 2, windows):
        for copy in (first_ps(f), second_ps(f), second_xs(f)):
            copy.wait_send()

    for kind, chunks in outputs:
        for i in chunks:
            drain_sum(kind, i)


def block_backward(
    stream, grad_y, mod, params, kept, index, table_lens, carry, sums, size, collective_id
):
    last = "gm" in kept
    qkv_w, proj_w, fc1_w, fc2_w = params
    windows, half, model = kept["x1"].shape
    width = 2 * half
    heads = kept["prob"].shape[1]
    inner = proj_w.shape[0]
    hidden = fc1_w.shape[1]
    rows = model // size
    lines = size // 2
    chunk = inner
    chunks = max(hidden, 4 * inner) // chunk
    kinds = 3 if last else 4
    groups = [-(-count // lows) for count, lows in zip(table_lens, (64, 128))]
    sds = jax.ShapeDtypeStruct
    sliced = (lines, 2, rows)
    cut = (*sliced, hidden)

    ins, outs, scratch = {}, {}, {}
    ins["grad_y"] = (grad_y, ANY)
    ins["mod"] = (mod, VM)
    ins["index"] = (index, VM)
    for name in STREAMS:
        value = stream if name == "stream" else kept[name]
        ins[name] = (value, ANY)
        scratch[name + "_v"] = pltpu.VMEM((2,) + value.shape[1:], value.dtype)
    ins["att"] = (kept["att"], ANY)
    scratch["att_v"] = pltpu.VMEM(kept["att"].shape, BF16)
    ins["qkv"] = (qkv_w, ANY)
    ins["proj"] = (proj_w, ANY)
    ins["fc1"] = (fc1_w.reshape(cut), ANY)
    ins["fc2"] = (fc2_w.reshape(cut), ANY)
    ins["carry"] = (carry, ANY)
    if last:
        ins["gm_s"] = (kept["gm"], ANY)
        outs["gx"] = (sds((2 * FRAMES, 4, 2, 8, model), F32), VM)
        outs["carry_next"] = (sds((*sliced, (3 - QKV_EARLY) * inner), BF16), ANY)
        if QKV_EARLY:
            outs["qkv_out"] = (sds((QKV_EARLY, rows, inner), F32), VM)
        outs["proj_out"] = (sds((inner, rows), F32), VM)
        outs["gbias"] = (sds((heads, *index.shape), F32), VM)
        outs["table_part"] = (sds((128, heads * groups[1]), F32), VM)
    else:
        ins["act"] = (kept["act"], ANY)
        scratch["act_v"] = pltpu.VMEM(kept["act"].shape, BF16)
        scratch["fc2_grad"] = pltpu.VMEM(cut, BF16)
        scratch["gbias"] = pltpu.VMEM((heads, *index.shape), F32)
        outs["gx"] = (sds((FRAMES, 4 * SIDE, model), F32), VM)
        for to in ("_out", "_b_out"):
            outs["qkv" + to] = (sds((3, rows, inner), F32), VM)
        outs["proj_out"] = (sds((inner, rows), F32), VM)
    outs["fc2_out"] = (sds((hidden, rows), F32), VM)
    outs["fc1_out"] = (sds((rows, hidden), F32), VM)
    if last:
        outs["mod_out"] = (sds((3, 512), F32), VM)
    else:
        each = 128 // size
        names = ("mod_b", "cond", "index_b", "early", "table_part")
        ins.update(
            {name: (v, VM) for name, v in zip(names, sums[:5], strict=True) if v is not None}
        )
        ins["gbias_b"] = (sums[5], ANY)
        for b, count in zip("ab", table_lens, strict=True):
            outs[f"table_{b}_out"] = (sds((heads, count), F32), VM)
            outs[f"ada_{b}_out"] = (sds((rows, 3 * 512), F32), VM)
        scratch.update(
            everyone=pltpu.VMEM((size, 8, 512), F32),
            tables=pltpu.VMEM((size, each, 128), F32),
            whole_table=pltpu.VMEM((128, 128), F32),
            table=pltpu.VMEM((64, heads * groups[0]), F32),
            table_b=pltpu.VMEM((128, heads * groups[1]), F32),
            other_sem=dma((heads,)),
            small=pltpu.VMEM((8, 512), F32),
            tabs=pltpu.VMEM((size, each, 128), F32),
            tab_parts=pltpu.VMEM((size - 1, each, 128), F32),
            tab_sum=pltpu.VMEM((each, 128), F32),
            small_sem=dma((2, size - 1)),
            table_sem=dma((2, size - 1)),
            sum_sem=dma((2, size - 1)),
        )

    own_all = pltpu.VMEM((windows, half, model), BF16)
    own_two = pltpu.VMEM((2, half, model), BF16)
    own_one = pltpu.VMEM((half, model), F32)
    every = pltpu.VMEM((windows, width, model), BF16)
    scratch.update(
        grad=pltpu.VMEM((windows, half, model), F32),
        part1=own_one,
        part2=own_one,
        gh=pltpu.VMEM((width, hidden), BF16),
        gqkv=pltpu.VMEM((width, 3 * inner), BF16),
        fc1_w=pltpu.VMEM(cut, BF16),
        fc2_w=pltpu.VMEM(cut, BF16),
        qkv_w=pltpu.VMEM((model, 3 * inner), BF16),
        proj_w=pltpu.VMEM(proj_w.shape, BF16),
        gm=every,
        rest=pltpu.VMEM((*sliced, 4 * inner), BF16),
        wgrad=pltpu.VMEM((model, max(4 * inner, hidden)), F32),
        ps1s=own_two,
        ps1r=own_two,
        ps2s=own_two,
        ps2r=own_two,
        xs1s=own_all,
        xs2s=own_two,
        xs1r=own_all,
        xs2r=own_all,
        buf1=pltpu.VMEM((kinds, chunks, lines, rows, chunk), BF16),
        buf2=pltpu.VMEM((kinds, chunks, lines - 1, rows, chunk), BF16),
        msum=pltpu.VMEM((6, 8, model), F32),
        mtot=pltpu.VMEM((4, 3, 512), F32),
        mrecv=pltpu.VMEM((4, 3, 512), F32),
        w_sem=dma((9,)),
        qkv_sem=dma((3,)),
        in_sem=dma((11, 2)),
        gm_sem=dma((2, windows)),
        ga_sem=dma((2, windows)),
        ps1_sem=dma((2, 2)),
        ps2_sem=dma((2, 2)),
        xs1_sem=dma((2, windows)),
        xs2_sem=dma((2, windows)),
        hand_sem=dma((2, 2)),
        mod_sem=dma((4,)),
        gate=pltpu.VMEM((2, 2, 512), F32),
        across_sem=dma((2, kinds, chunks)),
        along_sem=dma((2, kinds, chunks, lines - 1)),
    )
    names = (*ins, *outs, *scratch)
    results = pl.pallas_call(
        functools.partial(backward_kernel, windows, last, size, names),
        out_shape=[shape for shape, _ in outs.values()],
        in_specs=[spec for _, spec in ins.values()],
        out_specs=[spec for _, spec in outs.values()],
        scratch_shapes=list(scratch.values()),
        compiler_params=pltpu.CompilerParams(
            collective_id=collective_id, has_side_effects=True, vmem_limit_bytes=VMEM_LIMIT
        ),
        name="backward_last" if last else "backward_first",
    )(*[value for value, _ in ins.values()])
    return dict(zip(outs, results, strict=True))


def lookup(index, table, out, r):
    heads, groups = table.shape[0], table.shape[1]
    for block in range(index.shape[1] // 128):
        c = pl.ds(block * 128, 128)
        row = index[r, c]
        low = row & 127
        high = row >> 7
        found = [jnp.zeros((16, 128), F32) for _ in range(heads)]
        for g in range(groups):
            here = high == g
            for h in range(heads):
                spread = jnp.broadcast_to(table[h, pl.ds(g, 1), :], (16, 128))
                taken = jnp.take_along_axis(spread, low, axis=1, mode="promise_in_bounds")
                found[h] = jnp.where(here, taken, found[h])
        for h in range(heads):
            out[h, r, c] = found[h].astype(BF16)


def scatter(index, grad, out, part=0, parts=1):
    heads = len(grad)
    groups = out.shape[1] // heads
    rows, width = index.shape
    if part == 0:
        out[...] = jnp.zeros_like(out)
    count = rows // 8 // parts
    lows = out.shape[0]
    shift = lows.bit_length() - 1
    low_rows = lax.broadcasted_iota(jnp.int32, (lows, width), 0)
    high_rows = lax.broadcasted_iota(jnp.int32, (groups, width), 0)

    def some(i):
        r = pl.ds(pl.multiple_of((part * count + i) * 8, 8), 8)
        index_rows = index[r, :]
        low = index_rows & (lows - 1)
        high = index_rows >> shift
        grads = [g[r, :] for g in grad]
        total = out[...]
        for i in range(8):
            onehot = jnp.where(low_rows == low[i : i + 1], 1.0, 0.0).astype(BF16)
            here = high_rows == high[i : i + 1]
            placed = jnp.concatenate(
                [jnp.where(here, g[i : i + 1], 0.0) for g in grads], axis=0
            ).astype(BF16)
            total = total + dot_nt(onehot, placed)
        out[...] = total

    loop(count, some)


def copy_kernel(count, *refs):
    given, out, held = refs[:count], refs[count : 2 * count], refs[2 * count : 3 * count]
    ins, outs = refs[3 * count :]
    reads = [pltpu.make_async_copy(given[i], held[i], ins.at[i]) for i in range(count)]
    writes = [pltpu.make_async_copy(held[i], out[i], outs.at[i]) for i in range(count)]
    for copy in reads:
        copy.start()
    for read, write in zip(reads, writes, strict=True):
        read.wait()
        write.start()
    for copy in writes:
        copy.wait()


def copy_out(arrays):
    return pl.pallas_call(
        functools.partial(copy_kernel, len(arrays)),
        out_shape=[jax.ShapeDtypeStruct(a.shape, a.dtype) for a in arrays],
        in_specs=[ANY] * len(arrays),
        out_specs=[ANY] * len(arrays),
        scratch_shapes=[pltpu.VMEM(a.shape, a.dtype) for a in arrays]
        + [dma((len(arrays),)), dma((len(arrays),))],
        compiler_params=pltpu.CompilerParams(vmem_limit_bytes=VMEM_LIMIT),
        name="copy_out",
    )(*arrays)


def local(
    tokens,
    cond,
    pad_mask,
    spatial_index,
    joint_index,
    qkv_a,
    proj_a,
    fc1_a,
    fc2_a,
    table_a,
    ada_a,
    qkv_b,
    proj_b,
    fc1_b,
    fc2_b,
    table_b,
    ada_b,
    cotangent,
    dp_size,
    mp_size,
):
    model = tokens.shape[1]
    inner = proj_a.shape[0]
    params_a = (qkv_a.transpose(1, 0, 2), proj_a, fc1_a, fc2_a)
    params_b = (qkv_b.transpose(1, 0, 2), proj_b, fc1_b, fc2_b)
    hidden_keys = jnp.where(pad_mask.reshape(-1) > 0, 0.0, -1e30).astype(F32)
    mask_a = hidden_keys.reshape(FRAMES, 2, 2, 64).transpose(0, 2, 1, 3).reshape(FRAMES, 1, -1)
    mask_b = hidden_keys.reshape(FRAMES, 2, 2, 4, 2, 8).transpose(1, 4, 2, 0, 3, 5)
    mask_b = mask_b.reshape(4, 1, -1)
    groups = (FRAMES, 4 * SIDE, model)

    first = {
        "cond": cond,
        "ada_a": ada_a,
        "ada_b": ada_b,
        "spatial": spatial_index,
        "joint": joint_index,
        "table": table_a.T,
        "next_table": table_b.T,
    }
    kept_a = block_forward(tokens.reshape(groups), first, None, params_a, mask_a, dp_size, 1)
    mods = kept_a["mods"]
    x_b = kept_a["y"].reshape(4, -1, model)
    then = (x_b, mods, kept_a["next_bias"])
    kept_b = block_forward(cotangent.reshape(groups), None, then, params_b, mask_b, dp_size, 2)
    back_b = block_backward(
        x_b,
        kept_b["top"].reshape(x_b.shape),
        mods,
        params_b,
        kept_b,
        kept_a["next_index"],
        (table_a.shape[0], table_b.shape[0]),
        kept_b["fc2_grad"],
        None,
        dp_size,
        3,
    )
    back_a = block_backward(
        kept_a["stream_s"],
        back_b["gx"].reshape(FRAMES, -1, model),
        mods,
        params_a,
        kept_a,
        kept_a["index"],
        (table_a.shape[0], table_b.shape[0]),
        back_b["carry_next"],
        (
            back_b["mod_out"],
            kept_a["cond_act"],
            kept_a["next_index"],
            back_b.get("qkv_out"),
            back_b["table_part"],
            back_b["gbias"],
        ),
        dp_size,
        4,
    )

    def block_grads(b, fc):
        to = "_b_out" if b == "b" else "_out"
        return (
            back_a["qkv" + to],
            fc["proj_out"],
            fc["fc1_out"],
            fc["fc2_out"],
            back_a[f"table_{b}_out"],
            back_a[f"ada_{b}_out"],
        )

    results = list(
        copy_out((kept_b["y"], back_a["gx"], *block_grads("a", back_a), *block_grads("b", back_b)))
    )
    for i in (2, 8):
        results[i] = results[i].transpose(1, 0, 2)
        results[i + 4] = results[i + 4].T
    return (
        results[0].reshape(tokens.shape),
        results[1].reshape(tokens.shape),
        *results[2:],
    )


def solution(mesh):
    in_specs = (
        P(("dp", "mp"), None),
        P("dp", None),
        P("dp", None),
        P(),
        P(),
        P(None, None, "mp"),
        P("mp", None),
        P(None, "mp"),
        P("mp", None),
        P(None, "mp"),
        P(None, "mp"),
        P(None, None, "mp"),
        P("mp", None),
        P(None, "mp"),
        P("mp", None),
        P(None, "mp"),
        P(None, "mp"),
        P(("dp", "mp"), None),
    )
    out_specs = (
        P(("dp", "mp"), None),
        P(("dp", "mp"), None),
        P("dp", None, "mp"),
        P("mp", "dp"),
        P("dp", "mp"),
        P("mp", "dp"),
        P(None, "mp"),
        P("dp", "mp"),
        P("dp", None, "mp"),
        P("mp", "dp"),
        P("dp", "mp"),
        P("mp", "dp"),
        P(None, "mp"),
        P("dp", "mp"),
    )
    body = functools.partial(local, dp_size=mesh.shape["dp"], mp_size=mesh.shape["mp"])
    return jax.shard_map(body, mesh=mesh, in_specs=in_specs, out_specs=out_specs, check_vma=False)
```
